32 devices in a mesh: batch: 8 (over z, x), rep: 4 (over y, core).
Axes of the slice: x: 2, y: 2, z: 4, core: 2. Of those that a mesh axis runs over, the one named last changes fastest.
Arguments:
- tokens: bfloat16 [32, 1024, 1024], P(('batch', 'rep')), may hold values from -6 to 6
- ln1_gain: bfloat16 [1024], replicated, may hold values from 0.099609375 to 1.8984375
- ln1_shift: bfloat16 [1024], replicated, may hold values from -3 to 3
- qkv_weight: bfloat16 [1024, 3072], replicated, may hold values from -0.1875 to 0.1875
- qkv_bias: bfloat16 [3072], replicated, may hold values from -1.75 to 1.75
- out_weight: bfloat16 [1024, 1024], replicated, may hold values from -1.5 to 1.5
- out_bias: bfloat16 [1024], replicated, may hold values from -1.75 to 1.75
- ln2_gain: bfloat16 [1024], replicated, may hold values from 0.099609375 to 1.8984375
- ln2_shift: bfloat16 [1024], replicated, may hold values from -3 to 3
- fc_weight: bfloat16 [1024, 4096], replicated, may hold values from -0.1875 to 0.1875
- fc_bias: bfloat16 [4096], replicated, may hold values from -1.75 to 1.75
- proj_weight: bfloat16 [4096, 1024], replicated, may hold values from -0.09375 to 0.09375
- proj_bias: bfloat16 [1024], replicated, may hold values from -1.75 to 1.75
- prefix_embed: bfloat16 [10, 1024], replicated, may hold values from -6 to 6
- reparam_in: bfloat16 [1024, 512], replicated, may hold values from -0.1875 to 0.1875
- reparam_in_bias: bfloat16 [512], replicated, may hold values from -3 to 3
- reparam_out: bfloat16 [512, 2048], P(None, 'rep'), may hold values from -0.375 to 0.375
- reparam_out_bias: bfloat16 [2048], P('rep'), may hold values from -1.75 to 1.75
- bucket: int32 [32], P(('batch', 'rep')), may hold values from 256 to 1024, as said below
- seg_lens: int32 [32, 4], P(('batch', 'rep')), may hold values from 128 to 256, as said below
- cotangent: bfloat16 [32, 1024, 1024], P(('batch', 'rep')), may hold values from -6 to 6
Outputs:
- block_out: bfloat16 [32, 1024, 1024], P(('batch', 'rep'))
- tokens_grad: bfloat16 [32, 1024, 1024], P(('batch', 'rep'))
- embed_grad: float32 [10, 1024], replicated
- reparam_in_grad: float32 [1024, 512], replicated
- reparam_in_bias_grad: float32 [512], replicated
- reparam_out_grad: float32 [512, 2048], P(None, 'rep')
- reparam_out_bias_grad: float32 [2048], P('rep')
The draws below stay inside these ranges and needn't reach their ends.
Inputs may be any that keep to these rules, and one draw needn't show every extreme that they name: `bucket`: each entry is 256 or 1024; both occur in every draw. `seg_lens`: in a row of bucket 256 entry j is the live length of the j-th 256-slot bucket; in a row of bucket 1024 the sum of the row's entries is the live length of its one sequence. Some entry equals 256.
All inputs are finite; a program needn't handle non-finite values.
Results may differ from the reference program's by a relative error of at most 0.015.
Values may be sent and summed in bfloat16 or wider, within the bound.
No kernel may reach another device: no remote copies, remote signals or barrier semaphores. Data moves between devices by JAX's collectives and lax.ppermute only.
A program may use at most 384 MiB of HBM per device.

```python
import jax
import jax.numpy as jnp
from jax import lax

D = 1024
HEADS = 16
HEAD_DIM = 64
FF = 4096
PREFIX = 10
REPARAM = 512
KVCOLS = 2048
SLOTS = 1024
SHORT = 256
SEGS = 4
ROWS = 32


def draw_bucket(key, part):
    flags = jax.random.randint(jax.random.fold_in(key, 11), (ROWS,), 0, 2)
    pick_long = jax.random.randint(jax.random.fold_in(key, 12), (), 0, ROWS)
    offset = jax.random.randint(jax.random.fold_in(key, 13), (), 1, ROWS)
    pick_short = (pick_long + offset) % ROWS
    position = jnp.arange(ROWS)
    flags = jnp.where(position == pick_long, 1, jnp.where(position == pick_short, 0, flags))
    return (SHORT + (SLOTS - SHORT) * flags).astype(jnp.int32)


def draw_seg_lens(key, part):
    values = jax.random.randint(jax.random.fold_in(key, 21), (ROWS * SEGS,), SHORT // 2, SHORT + 1)
    chosen = jax.random.randint(jax.random.fold_in(key, 22), (), 0, ROWS * SEGS)
    values = jnp.where(jnp.arange(ROWS * SEGS) == chosen, SHORT, values)
    return values.reshape(ROWS, SEGS).astype(jnp.int32)


def levels(own_key, extent, cuts, least, high):
    factor_of, own = 1.0, jax.random.fold_in(own_key, 6)
    for dim, shards_of in cuts:
        steps = jnp.exp(jax.random.uniform(jax.random.fold_in(own, dim), (shards_of,), jnp.float32, least / len(cuts), high / len(cuts)))
        factor_of = factor_of * jnp.repeat(steps, extent[dim] // shards_of).reshape([-1 if axis == dim else 1 for axis in range(len(extent))])
    return factor_of


def scatter_about(rng, extent, spread, reach, cuts=(), held_as=jnp.bfloat16):
    values = jax.random.normal(rng, extent, jnp.float32) * spread
    if len(cuts) > 0:
        values = levels(rng, extent, cuts, -0.22, 0.18) * values
    return jnp.clip(values, min=-reach, max=reach).astype(held_as)


def setup_inputs(seed: int = 0) -> dict:
    keys = jax.random.split(jax.random.key(seed), 22)
    tokens = scatter_about(keys[0], (ROWS, SLOTS, D), 1.0, 6.0, ((0, 32),))
    ln1_gain = jnp.clip(1.0 + 0.18 * jax.random.normal(keys[1], (D,), jnp.float32), 0.099609375, 1.8984375).astype(jnp.bfloat16)
    ln1_shift = scatter_about(keys[2], (D,), 0.5, 3.0)
    qkv_weight = scatter_about(keys[3], (D, 3 * D), D ** -0.5, 0.1875)
    qkv_bias = scatter_about(keys[4], (3 * D,), 0.3, 1.75)
    out_weight = scatter_about(keys[5], (D, D), (D // 64) ** -0.5, 1.5)
    out_bias = scatter_about(keys[6], (D,), 0.3, 1.75)
    ln2_gain = jnp.clip(1.0 + 0.18 * jax.random.normal(keys[7], (D,), jnp.float32), 0.099609375, 1.8984375).astype(jnp.bfloat16)
    ln2_shift = scatter_about(keys[8], (D,), 0.5, 3.0)
    fc_weight = scatter_about(keys[9], (D, FF), D ** -0.5, 0.1875)
    fc_bias = scatter_about(keys[10], (FF,), 0.3, 1.75)
    proj_weight = scatter_about(keys[11], (FF, D), FF ** -0.5, 0.09375)
    proj_bias = scatter_about(keys[12], (D,), 0.3, 1.75)
    prefix_embed = scatter_about(keys[13], (PREFIX, D), 1.0, 6.0)
    reparam_in = scatter_about(keys[14], (D, REPARAM), D ** -0.5, 0.1875)
    reparam_in_bias = scatter_about(keys[15], (REPARAM,), 0.5, 3.0)
    reparam_out = scatter_about(keys[16], (REPARAM, KVCOLS), (REPARAM // 2) ** -0.5, 0.375, ((1, 4),))
    reparam_out_bias = scatter_about(keys[17], (KVCOLS,), 0.3, 1.75, ((0, 4),))
    bucket = draw_bucket(jax.random.fold_in(keys[21], 71), 0)
    seg_lens = draw_seg_lens(jax.random.fold_in(keys[21], 71), 0)
    cotangent = scatter_about(keys[20], (ROWS, SLOTS, D), 1.0, 6.0, ((0, 32),))
    return dict(tokens=tokens, ln1_gain=ln1_gain, ln1_shift=ln1_shift, qkv_weight=qkv_weight, qkv_bias=qkv_bias, out_weight=out_weight, out_bias=out_bias, ln2_gain=ln2_gain, ln2_shift=ln2_shift, fc_weight=fc_weight, fc_bias=fc_bias, proj_weight=proj_weight, proj_bias=proj_bias, prefix_embed=prefix_embed, reparam_in=reparam_in, reparam_in_bias=reparam_in_bias, reparam_out=reparam_out, reparam_out_bias=reparam_out_bias, bucket=bucket, seg_lens=seg_lens, cotangent=cotangent)


norm_eps = 1e-05
gelu_coef = 0.7978845608028654
gelu_cube = 0.044715
masked_score = -1e+30

@jax.custom_vjp
def low(v):
    return lax.optimization_barrier(v.astype(jnp.bfloat16)).astype(jnp.float32)

@jax.custom_vjp
def low_back(v):
    return v

def low_keep(v):
    return (low(v), None)

def low_pass(kept, grad):
    return (grad,)

def back_keep(v):
    return (v, None)

def back_low(kept, grad):
    return (low(grad),)
low.defvjp(low_keep, low_pass)
low_back.defvjp(back_keep, back_low)

def round_both(values):
    return low_back(low(values))

def matmul_hi(left, right):
    return jnp.dot(left, right, precision=lax.Precision.HIGHEST)

def layer_norm(values, gain_v, shift_v):
    row_mean = lax.optimization_barrier(jnp.mean(values, axis=-1, keepdims=True))
    centred = values - row_mean
    variance = lax.optimization_barrier(jnp.mean(centred * centred, axis=-1, keepdims=True))
    return centred * lax.rsqrt(variance + norm_eps) * gain_v + shift_v

def gelu_tanh(values):
    inner = gelu_coef * (values + gelu_cube * values * values * values)
    return 0.5 * values * (1.0 + jnp.tanh(inner))

def row_layout(bucket_row, lens_row, slot_count, short_len):
    position = jnp.arange(slot_count, dtype=jnp.int32)
    long_row = bucket_row == slot_count
    seg_index = position // short_len
    seg_table = seg_index[:, None] == jnp.arange(lens_row.shape[0], dtype=jnp.int32)[None, :]
    short_live = lax.optimization_barrier(jnp.sum(jnp.where(seg_table, lens_row[None, :], 0), axis=1))
    seg_id = jnp.where(long_row, 0, seg_index)
    in_seg = jnp.where(long_row, position, position - seg_index * short_len)
    seg_length = jnp.where(long_row, jnp.sum(lens_row), short_live)
    return (seg_id, in_seg < seg_length)

def allowed_block(seg_id, live_mask, first_row, block_rows):
    position = jnp.arange(seg_id.shape[0], dtype=jnp.int32)
    query_pos = position[first_row:first_row + block_rows]
    query_seg = seg_id[first_row:first_row + block_rows]
    tokens_ok = (query_seg[:, None] == seg_id[None, :]) & (position[None, :] <= query_pos[:, None]) & live_mask[None, :]
    prefix_ok = jnp.ones((block_rows, PREFIX), dtype=jnp.bool_)
    return jnp.concatenate([prefix_ok, tokens_ok], axis=1)

def block_row(x_row, bucket_row, lens_row, prefix_keys, prefix_vals, frozen):
    ln1_gain, ln1_shift, qkv_weight, qkv_bias, out_weight, out_bias, ln2_gain, ln2_shift, fc_weight, fc_bias, proj_weight, proj_bias = frozen
    slot_count = x_row.shape[0]
    seg_id, live_mask = row_layout(bucket_row, lens_row, slot_count, SHORT)
    normed = low(layer_norm(x_row, ln1_gain, ln1_shift))
    mixed_qkv = matmul_hi(normed, qkv_weight) + qkv_bias
    queries = round_both(mixed_qkv[:, :D]).reshape(slot_count, HEADS, HEAD_DIM)
    row_keys = round_both(mixed_qkv[:, D:2 * D]).reshape(slot_count, HEADS, HEAD_DIM)
    row_vals = round_both(mixed_qkv[:, 2 * D:]).reshape(slot_count, HEADS, HEAD_DIM)
    keys_all = jnp.concatenate([prefix_keys, row_keys], axis=0)
    vals_all = jnp.concatenate([prefix_vals, row_vals], axis=0)
    allowed = allowed_block(seg_id, live_mask, 0, slot_count)
    raw = jnp.einsum('qhd,khd->hqk', queries, keys_all, precision=lax.Precision.HIGHEST) * HEAD_DIM ** (-0.5)
    raw = low_back(raw)
    scores = jnp.where(allowed[None], raw, masked_score)
    peak_val = lax.optimization_barrier(jnp.max(scores, axis=-1, keepdims=True))
    raised = jnp.exp(scores - peak_val)
    softened = raised / lax.optimization_barrier(jnp.sum(raised, axis=-1, keepdims=True))
    attended = jnp.einsum('hqk,khd->qhd', low(softened), vals_all, precision=lax.Precision.HIGHEST)
    attended = round_both(attended.reshape(slot_count, D))
    branch = low_back(matmul_hi(attended, out_weight) + out_bias)
    middle = x_row + branch
    normed_two = low(layer_norm(middle, ln2_gain, ln2_shift))
    pre_fc = low_back(matmul_hi(normed_two, fc_weight) + fc_bias)
    active = low(gelu_tanh(pre_fc))
    result = middle + matmul_hi(active, proj_weight) + proj_bias
    return jnp.where(live_mask[:, None], result, 0.0)

def reference(tokens, ln1_gain, ln1_shift, qkv_weight, qkv_bias, out_weight, out_bias, ln2_gain, ln2_shift, fc_weight, fc_bias, proj_weight, proj_bias, prefix_embed, reparam_in, reparam_in_bias, reparam_out, reparam_out_bias, bucket, seg_lens, cotangent):
    frozen = tuple((item.astype(jnp.float32) for item in (ln1_gain, ln1_shift, qkv_weight, qkv_bias, out_weight, out_bias, ln2_gain, ln2_shift, fc_weight, fc_bias, proj_weight, proj_bias)))
    row_fn = jax.checkpoint(block_row)

    def forward(token_f, embed_f, in_weight, in_bias, out_w, out_b):
        tanh_pre = jnp.tanh(low_back(matmul_hi(embed_f, in_weight) + in_bias))
        hidden = low(tanh_pre)
        prefix_kv = round_both(matmul_hi(hidden, out_w) + out_b)
        prefix_keys = prefix_kv[:, :D].reshape(PREFIX, HEADS, HEAD_DIM)
        prefix_vals = prefix_kv[:, D:].reshape(PREFIX, HEADS, HEAD_DIM)

        def each_row(item):
            return row_fn(item[0], item[1], item[2], prefix_keys, prefix_vals, frozen)
        return lax.map(each_row, (token_f, bucket, seg_lens))
    block_f, pullback = jax.vjp(forward, tokens.astype(jnp.float32), prefix_embed.astype(jnp.float32), reparam_in.astype(jnp.float32), reparam_in_bias.astype(jnp.float32), reparam_out.astype(jnp.float32), reparam_out_bias.astype(jnp.float32))
    grads = pullback(cotangent.astype(jnp.float32))
    return (block_f.astype(jnp.bfloat16), grads[0].astype(jnp.bfloat16), grads[1], grads[2], grads[3], grads[4], grads[5])
```

```python
import jax
import jax.numpy as jnp
from jax import lax
from jax.experimental import pallas as pl
from jax.experimental.pallas import tpu as pltpu
from jax.sharding import PartitionSpec as P

D = 1024
HEADS = 16
HEAD_DIM = 64
FF = 4096
PREFIX = 10
PAD = 16
SHORT = 256
BLK = 256
QUAD = 4 * HEAD_DIM
QUADS = HEADS // 4
HALF = 512
CHUNK = 512

BF = jnp.bfloat16
F32 = jnp.float32
norm_eps = 1e-05
gelu_coef = 0.7978845608028654
gelu_cube = 0.044715
masked_score = -1e30

LN1_G, LN1_B, QKV_B, OUT_B, LN2_G, LN2_B, FC_B, PROJ_B = 0, 1024, 2048, 5120, 6144, 7168, 8192, 12288


def dot_nn(left, right):
    return jnp.dot(left, right, preferred_element_type=F32)


def dot_nt(left, right):
    return lax.dot_general(left, right, (((1,), (1,)), ((), ())), preferred_element_type=F32)


def dot_tn(left, right):
    return lax.dot_general(left, right, (((0,), (0,)), ((), ())), preferred_element_type=F32)


def normalise(values):
    row_mean = jnp.mean(values, axis=-1, keepdims=True)
    centred = values - row_mean
    variance = jnp.mean(centred * centred, axis=-1, keepdims=True)
    inv = lax.rsqrt(variance + norm_eps)
    return centred * inv, inv


def norm_back(grad, norm, inv):
    along = jnp.mean(grad * norm, axis=-1, keepdims=True)
    return (grad - jnp.mean(grad, axis=-1, keepdims=True) - norm * along) * inv


def gelu_pair(u):
    sq = u * u
    w = jnp.tanh(u * (gelu_coef + (gelu_coef * gelu_cube) * sq))
    a = 0.5 * w + 0.5
    slope = a * (1.0 + u * (1.0 - a) * (2.0 * gelu_coef + (6.0 * gelu_coef * gelu_cube) * sq))
    return u * a, slope


def head_mask(shape, head):
    lane = lax.broadcasted_iota(jnp.int32, shape, 1)
    return (lane < HEAD_DIM) if head % 2 == 0 else (lane >= HEAD_DIM)


def quad_prefix(prefix, quad):
    row = lax.broadcasted_iota(jnp.int32, (128, QUAD), 0) // PAD
    col = lax.broadcasted_iota(jnp.int32, (128, QUAD), 1) // HEAD_DIM
    tiled = jnp.concatenate([prefix] * 8, axis=0)
    return jnp.where(row == col + 4 * (quad % 2), tiled, jnp.zeros_like(tiled))


def full_prefix(prefix):
    shape = (HEADS * PAD, D)
    row = lax.broadcasted_iota(jnp.int32, shape, 0) // PAD
    col = lax.broadcasted_iota(jnp.int32, shape, 1) // HEAD_DIM
    tiled = jnp.concatenate([prefix] * HEADS, axis=0)
    return jnp.where(row == col, tiled, jnp.zeros_like(tiled))


def reparam_kernel(embed_ref, in_w_ref, in_b_ref, out_w_ref, out_b_ref, tanh_ref, kv_ref, pad_ref):
    pad_ref[...] = jnp.zeros_like(pad_ref)
    pad_ref[0:PREFIX, :] = embed_ref[...].astype(F32)
    tanh_pre = jnp.tanh(dot_nn(pad_ref[...].astype(BF), in_w_ref[...]) + in_b_ref[...].astype(F32))
    tanh_ref[...] = tanh_pre
    kv_ref[...] = (dot_nn(tanh_pre.astype(BF), out_w_ref[...]) + out_b_ref[...].astype(F32)).astype(BF)


def project_kernel(x_ref, w_ref, vec_ref, bias_ref, out_ref, normed_ref):
    step = pl.program_id(0)
    slots = x_ref.shape[0]
    factor = jnp.where(step == 0, HEAD_DIM**-0.5, 1.0)

    def norm_part(first, rows):
        norm, _ = normalise(x_ref[first : first + rows, :].astype(F32))
        gain, shift = vec_ref[:, LN1_G : LN1_G + D], vec_ref[:, LN1_B : LN1_B + D]
        normed_ref[first : first + rows, :] = (norm * gain + shift).astype(BF)

    def dot_part(first, rows):
        mixed = dot_nn(normed_ref[first : first + rows, :], w_ref[...]) + bias_ref[...]
        out_ref[first : first + rows, :] = (mixed.astype(BF).astype(F32) * factor).astype(BF)

    @pl.when(step == 0)
    def _():
        norm_part(0, BLK)
        for first in range(0, slots, BLK):
            if first + BLK < slots:
                norm_part(first + BLK, BLK)
            dot_part(first, BLK)

    @pl.when(step > 0)
    def _():
        for first in range(0, slots, HALF):
            dot_part(first, HALF)


def live_column(bucket_ref, lens_ref, first, rows, slots):
    position = lax.broadcasted_iota(jnp.int32, (rows, 1), 0) + first
    segment = position // SHORT
    total = jnp.int32(0)
    short_len = jnp.zeros((rows, 1), jnp.int32)
    for index in range(slots // SHORT):
        total = total + lens_ref[0, index]
        short_len = jnp.where(segment == index, lens_ref[0, index], short_len)
    return position < jnp.where(bucket_ref[0] == slots, total, segment * SHORT + short_len)


def attend(q_ref, k_ref, v_ref, pk_ref, pv_ref, att_ref, pp_ref, lse_ref, quad, long_row):
    slots = q_ref.shape[0]
    blocks = slots // BLK
    cols = pl.ds(pl.multiple_of(quad * QUAD, QUAD), QUAD)
    pair_cols = pl.ds(pl.multiple_of((quad // 2) * 128, 128), 128)
    prefix_keys = quad_prefix(pk_ref[...], quad)
    prefix_vals = quad_prefix(pv_ref[...], quad)
    causal = lax.broadcasted_iota(jnp.int32, (BLK, BLK), 1) <= lax.broadcasted_iota(jnp.int32, (BLK, BLK), 0)
    lane = lax.broadcasted_iota(jnp.int32, (BLK, 128), 1)
    lane_head = lane // PAD - 4 * (quad % 2)
    lane_real = lane % PAD < PREFIX

    def keys_of(block):
        return (0 if long_row else block * BLK), (block + 1) * BLK

    def scores(block, head):
        first, last = keys_of(block)
        pair = slice(128 * (head // 2), 128 * (head // 2) + 128)
        queries = q_ref[block * BLK : (block + 1) * BLK, pair]
        queries = jnp.where(head_mask((BLK, 128), head), queries, jnp.zeros_like(queries))
        raw = dot_nt(queries, k_ref[first:last, pair])
        own = jnp.where(causal, raw[:, -BLK:], masked_score)
        return own if last - first == BLK else jnp.concatenate([raw[:, :-BLK], own], axis=1)

    units = [(block, head) for block in range(blocks) for head in range(4)]
    ahead = 2
    queue = [scores(*unit) for unit in units[:ahead]]
    for index, (block, head) in enumerate(units):
        if index + ahead < len(units):
            queue.append(scores(*units[index + ahead]))
        rows = slice(block * BLK, (block + 1) * BLK)
        if head == 0:
            prefix_raw = dot_nt(q_ref[rows, :], prefix_keys)
            probs_quad = jnp.zeros((BLK, 128), F32)
            lse_quad = jnp.zeros((BLK, 128), F32)
            outs = []
        first, last = keys_of(block)
        pair = slice(128 * (head // 2), 128 * (head // 2) + 128)
        prefix_scores = jnp.where((lane_head == head) & lane_real, prefix_raw, masked_score)
        score = jnp.concatenate([queue[index], prefix_scores], axis=1)
        queue[index] = None
        peak = jnp.max(score, axis=1, keepdims=True)
        raised = jnp.exp(score - peak)
        summed = jnp.sum(raised, axis=1, keepdims=True)
        inv = 1.0 / summed
        outs.append(dot_nn(raised[:, : last - first].astype(BF), v_ref[first:last, pair]) * inv)
        probs_quad = probs_quad + raised[:, last - first :] * inv
        lse_quad = jnp.where(lane_head == head, peak + jnp.log(summed), lse_quad)
        if head == 3:
            probs_low = probs_quad.astype(BF)
            left = head_mask((BLK, 128), 0)
            merged = jnp.concatenate(
                [jnp.where(left, outs[0], outs[1]), jnp.where(left, outs[2], outs[3])], axis=1
            ) + dot_nn(probs_low, prefix_vals)
            att_ref[rows, cols] = merged.astype(BF)

            @pl.when(quad % 2 == 0)
            def _():
                pp_ref[rows, pair_cols] = probs_low
                lse_ref[rows, pair_cols] = lse_quad

            @pl.when(quad % 2 == 1)
            def _():
                pp_ref[rows, pair_cols] = pp_ref[rows, pair_cols] + probs_low
                lse_ref[rows, pair_cols] = lse_ref[rows, pair_cols] + lse_quad


def forward_kernel(
    bucket_ref, lens_ref,
    q_ref, k_ref, v_ref, pk_ref, pv_ref,
    x_ref, cot_ref, q_rows_ref, prefix_ref, vec_ref, out_w_hbm, fc_w_hbm, proj_w_hbm,
    block_ref, d_mid_ref, d_att_ref, d_sp_ref, lse_t_ref, delta_t_ref, prefix_row_ref,
    att_ref, pp_ref, lse_ref, out_w_ref, fc_w_ref, proj_w_ref, mid_ref, norm_ref, acc_ref, d_acc_ref,
    vp_ref, spread_ref, d_kp_ref, d_vp_ref, sems,
):
    step = pl.program_id(0)
    slots = q_ref.shape[0]
    copies = [
        pltpu.make_async_copy(out_w_hbm, out_w_ref, sems.at[0]),
        pltpu.make_async_copy(fc_w_hbm, fc_w_ref, sems.at[1]),
        pltpu.make_async_copy(proj_w_hbm, proj_w_ref, sems.at[2]),
    ]
    long_row = bucket_ref[0] == slots

    @pl.when(step == 0)
    def _():
        for copy in copies:
            copy.start()
        vp_ref[...] = full_prefix(prefix_ref[:, D:])
        row = lax.broadcasted_iota(jnp.int32, (D, HEADS * PAD), 0) // HEAD_DIM
        col = lax.broadcasted_iota(jnp.int32, (D, HEADS * PAD), 1) // PAD
        spread_ref[...] = jnp.where(row == col, 1.0, 0.0).astype(BF)
        d_kp_ref[...] = jnp.zeros_like(d_kp_ref)
        d_vp_ref[...] = jnp.zeros_like(d_vp_ref)

    @pl.when((step < QUADS) & long_row)
    def _():
        attend(q_ref, k_ref, v_ref, pk_ref, pv_ref, att_ref, pp_ref, lse_ref, step, True)

    @pl.when((step < QUADS) & jnp.logical_not(long_row))
    def _():
        attend(q_ref, k_ref, v_ref, pk_ref, pv_ref, att_ref, pp_ref, lse_ref, step, False)

    @pl.when(step == QUADS)
    def _():
        for copy in copies:
            copy.wait()

    @pl.when(step >= QUADS)
    def _():
        first = pl.multiple_of((step - QUADS) * HALF, HALF)
        rows = pl.ds(first, HALF)
        live = live_column(bucket_ref, lens_ref, first, HALF, slots)
        attended = att_ref[rows, :]
        mid = x_ref[...].astype(F32) + dot_nn(attended, out_w_ref[...]) + vec_ref[:, OUT_B : OUT_B + D]
        mid_ref[...] = mid
        norm, inv = normalise(mid)
        norm_ref[...] = norm
        normed_two = (norm * vec_ref[:, LN2_G : LN2_G + D] + vec_ref[:, LN2_B : LN2_B + D]).astype(BF)
        grad_out = jnp.where(live, cot_ref[...].astype(F32), 0.0).astype(BF)

        def opened(chunk):
            part = slice(chunk * CHUNK, (chunk + 1) * CHUNK)
            pre = dot_nn(normed_two, fc_w_ref[:, part]) + vec_ref[:, FC_B + part.start : FC_B + part.stop]
            return pre, dot_nt(grad_out, proj_w_ref[part, :])

        chunks = FF // CHUNK
        ready = opened(0)
        for chunk in range(chunks):
            pre, d_act = ready
            if chunk + 1 < chunks:
                ready = opened(chunk + 1)
            part = slice(chunk * CHUNK, (chunk + 1) * CHUNK)
            act, slope = gelu_pair(pre)
            d_pre = (d_act * slope).astype(BF)
            forth = dot_nn(act.astype(BF), proj_w_ref[part, :])
            back = dot_nt(d_pre, fc_w_ref[:, part])
            if chunk == 0:
                acc_ref[...] = forth
                d_acc_ref[...] = back
            else:
                acc_ref[...] += forth
                d_acc_ref[...] += back
        result = mid_ref[...] + acc_ref[...] + vec_ref[:, PROJ_B : PROJ_B + D]
        block_ref[...] = jnp.where(live, result, 0.0).astype(BF)
        d_mid = grad_out.astype(F32) + norm_back(
            d_acc_ref[...] * vec_ref[:, LN2_G : LN2_G + D], norm_ref[...], inv
        )
        d_mid_ref[...] = d_mid
        d_att = dot_nt(d_mid.astype(BF), out_w_ref[...]).astype(BF)
        d_att_ref[...] = d_att
        product = (d_att.astype(F32) * attended.astype(F32)).astype(BF)
        delta = dot_nn(product, spread_ref[...])
        probs = pp_ref[rows, :]
        d_sp = (probs.astype(F32) * (dot_nt(d_att, vp_ref[...]) - delta)).astype(BF)
        d_sp_ref[...] = d_sp
        d_kp_ref[...] += dot_tn(d_sp, q_rows_ref[...])
        d_vp_ref[...] += dot_tn(probs, d_att)
        lse_t_ref[...] = lse_ref[rows, :].T
        delta_t_ref[...] = delta.T

    @pl.when(step == pl.num_programs(0) - 1)
    def _():
        shape = (HEADS * PAD, D)
        own = (
            lax.broadcasted_iota(jnp.int32, shape, 0) // PAD
            == lax.broadcasted_iota(jnp.int32, shape, 1) // HEAD_DIM
        )
        for index, ref in enumerate((d_kp_ref, d_vp_ref)):
            kept = jnp.where(own, ref[...], 0.0)
            total = kept[0:PAD, :]
            for head in range(1, HEADS):
                total = total + kept[head * PAD : (head + 1) * PAD, :]
            prefix_row_ref[:, index * D : (index + 1) * D] = total.astype(BF)


def attend_back(
    q_ref, k_ref, v_ref, do_ref, pk_ref, dsp_ref, lse_ref, delta_ref, mix_ref, quad, long_row
):
    slots = q_ref.shape[0]
    blocks = slots // BLK
    causal = lax.broadcasted_iota(jnp.int32, (BLK, BLK), 0) <= lax.broadcasted_iota(jnp.int32, (BLK, BLK), 1)
    left = head_mask((BLK, 128), 0)
    prefix_keys = quad_prefix(pk_ref[...], quad)

    def keys_of(block):
        return (0 if long_row else block * BLK), (block + 1) * BLK

    def opened(block, head):
        first, last = keys_of(block)
        rows = slice(block * BLK, (block + 1) * BLK)
        pair = slice(128 * (head // 2), 128 * (head // 2) + 128)
        mask = head_mask((BLK, 128), head)
        queries, d_out = q_ref[rows, pair], do_ref[rows, pair]
        raw = dot_nt(k_ref[first:last, pair], jnp.where(mask, queries, jnp.zeros_like(queries)))
        d_prob = dot_nt(v_ref[first:last, pair], jnp.where(mask, d_out, jnp.zeros_like(d_out)))
        own = jnp.where(causal, raw[-BLK:], masked_score)
        return (own if last - first == BLK else jnp.concatenate([raw[:-BLK], own], axis=0)), d_prob

    for pair_index in range(2):
        pair = slice(128 * pair_index, 128 * pair_index + 128)
        units = [(block, 2 * pair_index + side) for block in range(blocks) for side in range(2)]
        ahead = 2
        queue = [opened(*unit) for unit in units[:ahead]]
        d_keys = [[None] * blocks for _ in range(2)]
        d_vals = [[None] * blocks for _ in range(2)]
        d_queries = [None, None]
        for index, (block, head) in enumerate(units):
            if index + ahead < len(units):
                queue.append(opened(*units[index + ahead]))
            score, d_prob = queue[index]
            queue[index] = None
            first, last = keys_of(block)
            rows = slice(block * BLK, (block + 1) * BLK)
            stat = slice(head * PAD, head * PAD + 1)
            prob = jnp.exp(score - lse_ref[stat, rows])
            d_score = (prob * (d_prob - delta_ref[stat, rows])).astype(BF)
            side = head % 2
            d_queries[side] = dot_tn(d_score, k_ref[first:last, pair])
            d_key = dot_nn(d_score, q_ref[rows, pair])
            d_val = dot_nn(prob.astype(BF), do_ref[rows, pair])
            for place, key_block in enumerate(range(first // BLK, last // BLK)):
                part = slice(place * BLK, (place + 1) * BLK)
                for sums, value in ((d_keys, d_key), (d_vals, d_val)):
                    so_far = sums[side][key_block]
                    sums[side][key_block] = value[part] if so_far is None else so_far + value[part]
            if side == 1:
                d_query = jnp.where(left, d_queries[0], d_queries[1]) + dot_nn(
                    dsp_ref[rows, :], prefix_keys[:, pair]
                )
                mix_ref[0, quad, rows, pair] = (d_query * HEAD_DIM**-0.5).astype(BF)
        for block in range(blocks):
            rows = slice(block * BLK, (block + 1) * BLK)
            mix_ref[1, quad, rows, pair] = jnp.where(left, d_keys[0][block], d_keys[1][block]).astype(BF)
            mix_ref[2, quad, rows, pair] = jnp.where(left, d_vals[0][block], d_vals[1][block]).astype(BF)


def backward_kernel(
    bucket_ref,
    q_ref, k_ref, v_ref, do_ref, pk_ref, dsp_ref, lse_ref, delta_ref, x_ref, d_mid_ref, vec_ref, qkv_w_hbm,
    grad_ref,
    mix_ref, qkv_w_ref, sem,
):
    step = pl.program_id(0)
    slots = q_ref.shape[0]
    copy = pltpu.make_async_copy(qkv_w_hbm, qkv_w_ref, sem)
    long_row = bucket_ref[0] == slots
    args = (q_ref, k_ref, v_ref, do_ref, pk_ref, dsp_ref, lse_ref, delta_ref, mix_ref, step)

    @pl.when(step == 0)
    def _():
        copy.start()

    @pl.when((step < QUADS) & long_row)
    def _():
        attend_back(*args, True)

    @pl.when((step < QUADS) & jnp.logical_not(long_row))
    def _():
        attend_back(*args, False)

    @pl.when(step == QUADS)
    def _():
        copy.wait()

    @pl.when(step >= QUADS)
    def _():
        rows = pl.ds(pl.multiple_of((step - QUADS) * HALF, HALF), HALF)
        d_mixed = jnp.concatenate(
            [mix_ref[third, quad, rows, :] for third in range(3) for quad in range(QUADS)], axis=1
        )
        d_normed = dot_nt(d_mixed, qkv_w_ref[...])
        norm, inv = normalise(x_ref[...].astype(F32))
        back = norm_back(d_normed * vec_ref[:, LN1_G : LN1_G + D], norm, inv)
        grad_ref[...] = (d_mid_ref[...] + back).astype(BF)


def tail_kernel(
    place_ref, rows_ref, tanh_ref, embed_ref, in_w_ref, out_w_ref,
    embed_grad_ref, in_grad_ref, in_bias_ref, out_grad_ref, out_bias_ref, pad_ref, sum_ref,
):
    pad_ref[...] = jnp.zeros_like(pad_ref)
    pad_ref[0:PREFIX, :] = embed_ref[...].astype(F32)
    tanh_pre = tanh_ref[...]
    total = rows_ref[0].astype(F32)
    for row in range(1, rows_ref.shape[0]):
        total = total + rows_ref[row].astype(F32)
    prefix_grad = total.astype(BF)
    sum_ref[...] = prefix_grad
    width = out_grad_ref.shape[1]
    own_cols = sum_ref[:, pl.ds(pl.multiple_of(place_ref[0] * width, 128), width)]
    out_grad_ref[...] = dot_tn(tanh_pre.astype(BF), own_cols)
    out_bias_ref[...] = jnp.sum(own_cols.astype(F32), axis=0, keepdims=True)
    d_pre = (dot_nt(prefix_grad, out_w_ref[...]) * (1.0 - tanh_pre * tanh_pre)).astype(BF)
    in_grad_ref[...] = dot_tn(pad_ref[...].astype(BF), d_pre)
    in_bias_ref[...] = jnp.sum(d_pre.astype(F32), axis=0, keepdims=True)
    embed_grad_ref[...] = dot_nt(d_pre, in_w_ref[...])[0:PREFIX]


VMEM = pl.BlockSpec(memory_space=pltpu.VMEM)
SMEM = pl.BlockSpec(memory_space=pltpu.SMEM)
ANY = pl.BlockSpec(memory_space=pl.ANY)


def params(mib, steps=0):
    semantics = ("arbitrary",) * steps if steps else None
    return pltpu.CompilerParams(vmem_limit_bytes=mib * 2**20, dimension_semantics=semantics)


def cost(flops, moved):
    return pl.CostEstimate(flops=int(flops), bytes_accessed=int(moved), transcendentals=0)


def shape(dims, dtype):
    return jax.ShapeDtypeStruct(dims, dtype)


def local(
    tokens, ln1_gain, ln1_shift, qkv_weight, qkv_bias, out_weight, out_bias, ln2_gain, ln2_shift, fc_weight,
    fc_bias, proj_weight, proj_bias, prefix_embed, reparam_in, reparam_in_bias, reparam_out, reparam_out_bias,
    bucket, seg_lens, cotangent,
):
    x, cot = tokens[0], cotangent[0]
    slots = x.shape[0]
    halves = slots // HALF
    own_width = reparam_out.shape[1]
    hidden_width = reparam_in.shape[1]
    vectors = jnp.concatenate(
        [ln1_gain, ln1_shift, qkv_bias, out_bias, ln2_gain, ln2_shift, fc_bias, proj_bias]
    ).astype(F32)[None, :]

    tanh_pre, own_kv = pl.pallas_call(
        reparam_kernel,
        out_shape=(shape((PAD, hidden_width), F32), shape((PAD, own_width), BF)),
        in_specs=[VMEM] * 5,
        out_specs=(VMEM, VMEM),
        scratch_shapes=[pltpu.VMEM((PAD, D), F32)],
        compiler_params=params(16),
        name="reparam",
    )(prefix_embed, reparam_in, reparam_in_bias[None, :], reparam_out, reparam_out_bias[None, :])
    prefix_kv = lax.all_gather(own_kv, "rep", axis=1, tiled=True)

    mixed = pl.pallas_call(
        project_kernel,
        grid=(3,),
        out_shape=shape((slots, 3 * D), BF),
        in_specs=[
            pl.BlockSpec((slots, D), lambda n: (0, 0)),
            pl.BlockSpec((D, D), lambda n: (0, n)),
            pl.BlockSpec((1, LN1_B + D), lambda n: (0, 0)),
            pl.BlockSpec((1, D), lambda n: (0, QKV_B // D + n)),
        ],
        out_specs=pl.BlockSpec((slots, D), lambda n: (0, n)),
        scratch_shapes=[pltpu.VMEM((slots, D), BF)],
        compiler_params=params(40, 1),
        cost_estimate=cost(6 * slots * D * D, 16 * 2**20),
        name="project",
    )(x, qkv_weight, vectors, vectors)

    def quad_at(offset):
        return pl.BlockSpec((slots, QUAD), lambda g: (0, offset + jnp.minimum(g, QUADS - 1)))

    def prefix_at(offset):
        return pl.BlockSpec((PAD, QUAD), lambda g: (0, offset + jnp.minimum(g, QUADS - 1)))

    def half_of(width):
        return pl.BlockSpec((HALF, width), lambda g: (jnp.maximum(g - QUADS, 0), 0))

    half_t = pl.BlockSpec((HEADS * PAD, HALF), lambda g: (0, jnp.maximum(g - QUADS, 0)))
    vector_spec = pl.BlockSpec(vectors.shape, lambda g: (0, 0))
    lanes = HEADS * PAD
    block_out, d_mid, d_att, d_sp, lse_t, delta_t, prefix_row = pl.pallas_call(
        forward_kernel,
        grid=(QUADS + halves,),
        out_shape=(
            shape((slots, D), BF),
            shape((slots, D), F32),
            shape((slots, D), BF),
            shape((slots, lanes), BF),
            shape((lanes, slots), F32),
            shape((lanes, slots), F32),
            shape((PAD, 2 * D), BF),
        ),
        in_specs=[
            SMEM, SMEM,
            quad_at(0), quad_at(QUADS), quad_at(2 * QUADS), prefix_at(0), prefix_at(QUADS),
            half_of(D), half_of(D), half_of(D),
            pl.BlockSpec((PAD, 2 * D), lambda g: (0, 0)), vector_spec, ANY, ANY, ANY,
        ],
        out_specs=(
            half_of(D), half_of(D), half_of(D), half_of(lanes), half_t, half_t,
            pl.BlockSpec((PAD, 2 * D), lambda g: (0, 0)),
        ),
        scratch_shapes=[
            pltpu.VMEM((slots, D), BF),
            pltpu.VMEM((slots, lanes), BF),
            pltpu.VMEM((slots, lanes), F32),
            pltpu.VMEM((D, D), BF),
            pltpu.VMEM((D, FF), BF),
            pltpu.VMEM((FF, D), BF),
            pltpu.VMEM((HALF, D), F32),
            pltpu.VMEM((HALF, D), F32),
            pltpu.VMEM((HALF, D), F32),
            pltpu.VMEM((HALF, D), F32),
            pltpu.VMEM((lanes, D), BF),
            pltpu.VMEM((D, lanes), BF),
            pltpu.VMEM((lanes, D), F32),
            pltpu.VMEM((lanes, D), F32),
            pltpu.SemaphoreType.DMA((3,)),
        ],
        compiler_params=params(60, 1),
        cost_estimate=cost(50e9, 40 * 2**20),
        name="forward",
    )(
        bucket, seg_lens, mixed, mixed, mixed, prefix_kv, prefix_kv, x, cot, mixed, prefix_kv, vectors,
        out_weight, fc_weight, proj_weight,
    )

    early, _ = lax.optimization_barrier((reparam_out, prefix_kv))
    out_full = lax.all_gather(early, "rep", axis=1, tiled=True)
    all_rows = lax.all_gather(prefix_row, ("batch", "rep"), axis=0, tiled=False)

    stat_spec = pl.BlockSpec((4 * PAD, slots), lambda g: (jnp.minimum(g, QUADS - 1), 0))
    tokens_grad = pl.pallas_call(
        backward_kernel,
        grid=(QUADS + halves,),
        out_shape=shape((slots, D), BF),
        in_specs=[
            SMEM,
            quad_at(0), quad_at(QUADS), quad_at(2 * QUADS), quad_at(0), prefix_at(0),
            pl.BlockSpec((slots, 128), lambda g: (0, jnp.minimum(g, QUADS - 1) // 2)),
            stat_spec, stat_spec, half_of(D), half_of(D), vector_spec, ANY,
        ],
        out_specs=half_of(D),
        scratch_shapes=[
            pltpu.VMEM((3, QUADS, slots, QUAD), BF),
            pltpu.VMEM((D, 3 * D), BF),
            pltpu.SemaphoreType.DMA,
        ],
        compiler_params=params(60, 1),
        cost_estimate=cost(40e9, 30 * 2**20),
        name="backward",
    )(bucket, mixed, mixed, mixed, d_att, prefix_kv, d_sp, lse_t, delta_t, x, d_mid, vectors, qkv_weight)

    place = lax.axis_index("rep").astype(jnp.int32)[None]
    embed_grad, in_grad, in_bias_grad, out_grad, out_bias_grad = pl.pallas_call(
        tail_kernel,
        out_shape=(
            shape((PREFIX, D), F32),
            shape((D, hidden_width), F32),
            shape((1, hidden_width), F32),
            shape((hidden_width, own_width), F32),
            shape((1, own_width), F32),
        ),
        in_specs=[SMEM] + [VMEM] * 5,
        out_specs=(VMEM,) * 5,
        scratch_shapes=[pltpu.VMEM((PAD, D), F32), pltpu.VMEM((PAD, 2 * D), BF)],
        compiler_params=params(24),
        name="tail",
    )(place, all_rows, tanh_pre, prefix_embed, reparam_in, out_full)
    return (
        block_out[None],
        tokens_grad[None],
        embed_grad,
        in_grad,
        in_bias_grad[0],
        out_grad,
        out_bias_grad[0],
    )


def solution(mesh):
    row = P(("batch", "rep"), None, None)
    placed = (row, *[P()] * 15, P(None, "rep"), P("rep"), P(("batch", "rep")), P(("batch", "rep"), None), row)
    return jax.shard_map(
        local,
        mesh=mesh,
        in_specs=placed,
        out_specs=(row, row, P(), P(), P(), P(None, "rep"), P("rep")),
        check_vma=False,
    )
```

```python
import jax
import jax.numpy as jnp
from jax import lax
from jax.experimental import pallas as pl
from jax.experimental.pallas import tpu as pltpu
from jax.sharding import PartitionSpec as P

D = 1024
HEADS = 16
HEAD_DIM = 64
FF = 4096
PREFIX = 10
PAD = 16
SHORT = 256
BLK = 256
QUAD = 4 * HEAD_DIM
QUADS = HEADS // 4
CHUNK = 1024

BF = jnp.bfloat16
F32 = jnp.float32
norm_eps = 1e-05
gelu_coef = 0.7978845608028654
gelu_cube = 0.044715
masked_score = -1e30


def dot_nn(left, right):
    return jnp.dot(left, right, preferred_element_type=F32)


def dot_nt(left, right):
    return lax.dot_general(left, right, (((1,), (1,)), ((), ())), preferred_element_type=F32)


def dot_tn(left, right):
    return lax.dot_general(left, right, (((0,), (0,)), ((), ())), preferred_element_type=F32)


def normalise(values):
    row_mean = jnp.mean(values, axis=-1, keepdims=True)
    centred = values - row_mean
    variance = jnp.mean(centred * centred, axis=-1, keepdims=True)
    inv = lax.rsqrt(variance + norm_eps)
    return centred * inv, inv


def norm_back(grad, norm, inv):
    along = jnp.mean(grad * norm, axis=-1, keepdims=True)
    return (grad - jnp.mean(grad, axis=-1, keepdims=True) - norm * along) * inv


def gelu_pair(u):
    sq = u * u
    w = jnp.tanh(u * (gelu_coef + (gelu_coef * gelu_cube) * sq))
    a = 0.5 * w + 0.5
    slope = a * (1.0 + u * (1.0 - a) * (2.0 * gelu_coef + (6.0 * gelu_coef * gelu_cube) * sq))
    return u * a, slope


def head_mask(shape, head):
    lane = lax.broadcasted_iota(jnp.int32, shape, 1)
    return (lane < HEAD_DIM) if head % 2 == 0 else (lane >= HEAD_DIM)


def quad_prefix(prefix, quad):
    row = lax.broadcasted_iota(jnp.int32, (128, QUAD), 0) // PAD
    col = lax.broadcasted_iota(jnp.int32, (128, QUAD), 1) // HEAD_DIM
    tiled = jnp.concatenate([prefix] * 8, axis=0)
    return jnp.where(row == col + 4 * (quad % 2), tiled, jnp.zeros_like(tiled))


def full_prefix(prefix):
    shape = (HEADS * PAD, D)
    row = lax.broadcasted_iota(jnp.int32, shape, 0) // PAD
    col = lax.broadcasted_iota(jnp.int32, shape, 1) // HEAD_DIM
    tiled = jnp.concatenate([prefix] * HEADS, axis=0)
    return jnp.where(row == col, tiled, jnp.zeros_like(tiled))


def row_of(ref, first=0, size=None):
    size = ref.shape[0] if size is None else size
    return ref[first : first + size].astype(F32)[None, :]


def padded_embed(embed_ref, pad_ref):
    pad_ref[...] = jnp.zeros_like(pad_ref)
    pad_ref[0:PREFIX, :] = embed_ref[...].astype(F32)
    return pad_ref[...].astype(BF)


def reparam_kernel(embed_ref, in_w_ref, in_b_ref, out_w_ref, out_b_ref, tanh_ref, kv_ref, pad_ref):
    tanh_pre = jnp.tanh(dot_nn(padded_embed(embed_ref, pad_ref), in_w_ref[...]) + row_of(in_b_ref))
    tanh_ref[...] = tanh_pre
    kv_ref[...] = (dot_nn(tanh_pre.astype(BF), out_w_ref[...]) + row_of(out_b_ref)).astype(BF)


def project_kernel(x_ref, gain_ref, shift_ref, bias_ref, w_ref, out_ref, normed_ref):
    step = pl.program_id(0)
    slots = x_ref.shape[0]
    factor = jnp.where(step == 0, HEAD_DIM**-0.5, 1.0)

    def norm_part(first):
        norm, _ = normalise(x_ref[first : first + BLK, :].astype(F32))
        normed_ref[first : first + BLK, :] = (norm * row_of(gain_ref) + row_of(shift_ref)).astype(BF)

    def dot_part(first, rows):
        mixed = dot_nn(normed_ref[first : first + rows, :], w_ref[...]) + row_of(bias_ref)
        out_ref[first : first + rows, :] = (mixed.astype(BF).astype(F32) * factor).astype(BF)

    @pl.when(step == 0)
    def _():
        norm_part(0)
        for first in range(0, slots, BLK):
            if first + BLK < slots:
                norm_part(first + BLK)
            dot_part(first, BLK)

    @pl.when(step > 0)
    def _():
        for first in range(0, slots, 2 * BLK):
            dot_part(first, 2 * BLK)


def live_column(bucket_ref, lens_ref, first, rows, slots):
    position = lax.broadcasted_iota(jnp.int32, (rows, 1), 0) + first
    segment = position // SHORT
    total = jnp.int32(0)
    short_len = jnp.zeros((rows, 1), jnp.int32)
    for index in range(slots // SHORT):
        total = total + lens_ref[0, index]
        short_len = jnp.where(segment == index, lens_ref[0, index], short_len)
    return position < jnp.where(bucket_ref[0] == slots, total, segment * SHORT + short_len)


def attend(q_ref, k_ref, v_ref, prefix_ref, att_ref, pp_ref, lse_ref, quad, long_row):
    slots = q_ref.shape[0]
    blocks = slots // BLK
    cols = pl.ds(pl.multiple_of(quad * QUAD, QUAD), QUAD)
    pair_cols = pl.ds(pl.multiple_of((quad // 2) * 128, 128), 128)
    prefix_keys = quad_prefix(prefix_ref[:, cols], quad)
    prefix_vals = quad_prefix(prefix_ref[:, pl.ds(pl.multiple_of(D + quad * QUAD, QUAD), QUAD)], quad)
    causal = lax.broadcasted_iota(jnp.int32, (BLK, BLK), 1) <= lax.broadcasted_iota(jnp.int32, (BLK, BLK), 0)
    lane = lax.broadcasted_iota(jnp.int32, (BLK, 128), 1)
    lane_head = lane // PAD - 4 * (quad % 2)
    lane_real = lane % PAD < PREFIX

    def keys_of(block):
        return (0 if long_row else block * BLK), (block + 1) * BLK

    def scores(block, head):
        first, last = keys_of(block)
        pair = slice(128 * (head // 2), 128 * (head // 2) + 128)
        queries = q_ref[block * BLK : (block + 1) * BLK, pair]
        queries = jnp.where(head_mask((BLK, 128), head), queries, jnp.zeros_like(queries))
        raw = dot_nt(queries, k_ref[first:last, pair])
        own = jnp.where(causal, raw[:, -BLK:], masked_score)
        return own if last - first == BLK else jnp.concatenate([raw[:, :-BLK], own], axis=1)

    units = [(block, head) for block in range(blocks) for head in range(4)]
    ahead = 2
    queue = [scores(*unit) for unit in units[:ahead]]
    for index, (block, head) in enumerate(units):
        if index + ahead < len(units):
            queue.append(scores(*units[index + ahead]))
        rows = slice(block * BLK, (block + 1) * BLK)
        if head == 0:
            prefix_raw = dot_nt(q_ref[rows, :], prefix_keys)
            probs_quad = jnp.zeros((BLK, 128), F32)
            lse_quad = jnp.zeros((BLK, 128), F32)
            outs = []
        first, last = keys_of(block)
        pair = slice(128 * (head // 2), 128 * (head // 2) + 128)
        prefix_scores = jnp.where((lane_head == head) & lane_real, prefix_raw, masked_score)
        score = jnp.concatenate([queue[index], prefix_scores], axis=1)
        queue[index] = None
        peak = jnp.max(score, axis=1, keepdims=True)
        raised = jnp.exp(score - peak)
        summed = jnp.sum(raised, axis=1, keepdims=True)
        inv = 1.0 / summed
        outs.append(dot_nn(raised[:, : last - first].astype(BF), v_ref[first:last, pair]) * inv)
        probs_quad = probs_quad + raised[:, last - first :] * inv
        lse_quad = jnp.where(lane_head == head, peak + jnp.log(summed), lse_quad)
        if head == 3:
            probs_low = probs_quad.astype(BF)
            left = head_mask((BLK, 128), 0)
            merged = jnp.concatenate(
                [jnp.where(left, outs[0], outs[1]), jnp.where(left, outs[2], outs[3])], axis=1
            ) + dot_nn(probs_low, prefix_vals)
            att_ref[rows, cols] = merged.astype(BF)

            @pl.when(quad % 2 == 0)
            def _():
                pp_ref[rows, pair_cols] = probs_low
                lse_ref[rows, pair_cols] = lse_quad

            @pl.when(quad % 2 == 1)
            def _():
                pp_ref[rows, pair_cols] = pp_ref[rows, pair_cols] + probs_low
                lse_ref[rows, pair_cols] = lse_ref[rows, pair_cols] + lse_quad


def forward_kernel(
    place_ref, bucket_ref, lens_ref, q_ref, k_ref, v_ref, x_ref, cot_ref, q_rows_ref,
    out_b_ref, gain_ref, shift_ref, fc_b_ref, proj_b_ref, out_w_hbm, fc_w_hbm, proj_w_hbm, *refs,
):
    pieces, refs = refs[: len(refs) - 28], refs[len(refs) - 28 :]
    (
        block_ref, d_mid_ref, d_att_ref, d_sp_ref, lse_t_ref, delta_t_ref, prefix_row_ref, prefix_ref,
        att_ref, pp_ref, lse_ref, out_w_ref, fc_w_ref, proj_w_ref, norm_ref, inv_ref, normed_ref, grad_out_ref,
        acc_ref, d_acc_ref, pre_ref, d_act_ref, bias_ref, vp_ref, spread_ref, d_kp_ref, d_vp_ref, sems,
    ) = refs
    step = pl.program_id(0)
    slots = q_ref.shape[0]
    copies = [
        pltpu.make_async_copy(out_w_hbm, out_w_ref, sems.at[0]),
        pltpu.make_async_copy(fc_w_hbm, fc_w_ref, sems.at[1]),
        pltpu.make_async_copy(proj_w_hbm, proj_w_ref, sems.at[2]),
    ]
    long_row = bucket_ref[0] == slots

    @pl.when(step == 0)
    def _():
        for copy in copies:
            copy.start()
        width = pieces[0].shape[1]
        for shift, piece in enumerate(pieces):
            owner = (place_ref[0] + (len(pieces) - shift)) % len(pieces)
            prefix_ref[:, pl.ds(pl.multiple_of(owner * width, 128), width)] = piece[...]
        vp_ref[...] = full_prefix(prefix_ref[:, D:])
        row = lax.broadcasted_iota(jnp.int32, (D, HEADS * PAD), 0) // HEAD_DIM
        col = lax.broadcasted_iota(jnp.int32, (D, HEADS * PAD), 1) // PAD
        spread_ref[...] = jnp.where(row == col, 1.0, 0.0).astype(BF)
        bias_ref[...] = row_of(fc_b_ref)
        d_kp_ref[...] = jnp.zeros_like(d_kp_ref)
        d_vp_ref[...] = jnp.zeros_like(d_vp_ref)

    @pl.when((step < QUADS) & long_row)
    def _():
        attend(q_ref, k_ref, v_ref, prefix_ref, att_ref, pp_ref, lse_ref, step, True)

    @pl.when((step < QUADS) & jnp.logical_not(long_row))
    def _():
        attend(q_ref, k_ref, v_ref, prefix_ref, att_ref, pp_ref, lse_ref, step, False)

    blocks = slots // BLK
    chunks = FF // CHUNK

    @pl.when(step == QUADS)
    def _():
        copies[0].wait()

    @pl.when((step >= QUADS) & (step < QUADS + blocks))
    def _():
        first = pl.multiple_of((step - QUADS) * BLK, BLK)
        rows = pl.ds(first, BLK)
        mid = x_ref[...].astype(F32) + dot_nn(att_ref[rows, :], out_w_ref[...]) + row_of(out_b_ref)
        norm, inv = normalise(mid)
        norm_ref[rows, :] = norm.astype(BF)
        inv_ref[rows, :] = inv
        normed_ref[rows, :] = (norm * row_of(gain_ref) + row_of(shift_ref)).astype(BF)
        live = live_column(bucket_ref, lens_ref, first, BLK, slots)
        grad_out_ref[rows, :] = jnp.where(live, cot_ref[...].astype(F32), 0.0).astype(BF)
        acc_ref[rows, :] = mid + row_of(proj_b_ref)

    def opened(block, chunk):
        rows = pl.ds(pl.multiple_of(block * BLK, BLK), BLK)
        part = pl.ds(pl.multiple_of(chunk * CHUNK, CHUNK), CHUNK)
        pre = dot_nn(normed_ref[rows, :], fc_w_ref[:, part]) + bias_ref[:, part]
        return pre, dot_nt(grad_out_ref[rows, :], proj_w_ref[part, :])

    @pl.when(step == QUADS + blocks)
    def _():
        copies[1].wait()
        copies[2].wait()
        pre_ref[...], d_act_ref[...] = opened(jnp.int32(0), jnp.int32(0))

    @pl.when(step >= QUADS + blocks)
    def _():
        block = step - QUADS - blocks
        rows = pl.ds(pl.multiple_of(block * BLK, BLK), BLK)
        d_acc_ref[...] = jnp.zeros_like(d_acc_ref)

        def chunk_step(chunk, carry):
            pre, d_act = pre_ref[...], d_act_ref[...]
            wraps = chunk == chunks - 1
            following = opened(
                jnp.where(wraps, jnp.minimum(block + 1, blocks - 1), block), jnp.where(wraps, 0, chunk + 1)
            )
            part = pl.ds(pl.multiple_of(chunk * CHUNK, CHUNK), CHUNK)
            act, slope = gelu_pair(pre)
            acc_ref[rows, :] += dot_nn(act.astype(BF), proj_w_ref[part, :])
            d_acc_ref[...] += dot_nt((d_act * slope).astype(BF), fc_w_ref[:, part])
            pre_ref[...], d_act_ref[...] = following
            return carry

        lax.fori_loop(0, chunks, chunk_step, 0)
        live = live_column(bucket_ref, lens_ref, block * BLK, BLK, slots)
        block_ref[...] = jnp.where(live, acc_ref[rows, :], 0.0).astype(BF)
        d_mid = grad_out_ref[rows, :].astype(F32) + norm_back(
            d_acc_ref[...] * row_of(gain_ref), norm_ref[rows, :].astype(F32), inv_ref[rows, :]
        )
        d_mid_ref[...] = d_mid
        d_att = dot_nt(d_mid.astype(BF), out_w_ref[...]).astype(BF)
        d_att_ref[...] = d_att
        product = (d_att.astype(F32) * att_ref[rows, :].astype(F32)).astype(BF)
        delta = dot_nn(product, spread_ref[...])
        probs = pp_ref[rows, :]
        d_sp = (probs.astype(F32) * (dot_nt(d_att, vp_ref[...]) - delta)).astype(BF)
        d_sp_ref[...] = d_sp
        d_kp_ref[...] += dot_tn(d_sp, q_rows_ref[...])
        d_vp_ref[...] += dot_tn(probs, d_att)
        lse_t_ref[...] = lse_ref[rows, :].T
        delta_t_ref[...] = delta.T

    @pl.when(step == pl.num_programs(0) - 1)
    def _():
        shape = (HEADS * PAD, D)
        own = (
            lax.broadcasted_iota(jnp.int32, shape, 0) // PAD
            == lax.broadcasted_iota(jnp.int32, shape, 1) // HEAD_DIM
        )
        for index, ref in enumerate((d_kp_ref, d_vp_ref)):
            kept = jnp.where(own, ref[...], 0.0)
            total = kept[0:PAD, :]
            for head in range(1, HEADS):
                total = total + kept[head * PAD : (head + 1) * PAD, :]
            prefix_row_ref[:, index * D : (index + 1) * D] = total.astype(BF)


def attend_back(
    q_ref, k_ref, v_ref, do_ref, pk_ref, dsp_ref, lse_ref, delta_ref, mix_ref, pair, long_row
):
    slots = q_ref.shape[0]
    blocks = slots // BLK
    causal = lax.broadcasted_iota(jnp.int32, (BLK, BLK), 0) <= lax.broadcasted_iota(jnp.int32, (BLK, BLK), 1)
    left = head_mask((BLK, 128), 0)
    row = lax.broadcasted_iota(jnp.int32, (128, 128), 0) // PAD
    col = lax.broadcasted_iota(jnp.int32, (128, 128), 1) // HEAD_DIM
    tiled = jnp.concatenate([pk_ref[...]] * 8, axis=0)
    prefix_keys = jnp.where(row == col + 2 * (pair % 4), tiled, jnp.zeros_like(tiled))

    def keys_of(block):
        return (0 if long_row else block * BLK), (block + 1) * BLK

    def opened(block, side):
        first, last = keys_of(block)
        rows = slice(block * BLK, (block + 1) * BLK)
        mask = head_mask((BLK, 128), side)
        queries, d_out = q_ref[rows, :], do_ref[rows, :]
        raw = dot_nt(k_ref[first:last, :], jnp.where(mask, queries, jnp.zeros_like(queries)))
        d_prob = dot_nt(v_ref[first:last, :], jnp.where(mask, d_out, jnp.zeros_like(d_out)))
        own = jnp.where(causal, raw[-BLK:], masked_score)
        return (own if last - first == BLK else jnp.concatenate([raw[:-BLK], own], axis=0)), d_prob

    units = [(block, side) for block in range(blocks) for side in range(2)]
    ahead = 2
    queue = [opened(*unit) for unit in units[:ahead]]
    d_keys = [[None] * blocks for _ in range(2)]
    d_vals = [[None] * blocks for _ in range(2)]
    d_queries = [None, None]
    for index, (block, side) in enumerate(units):
        if index + ahead < len(units):
            queue.append(opened(*units[index + ahead]))
        score, d_prob = queue[index]
        queue[index] = None
        first, last = keys_of(block)
        rows = slice(block * BLK, (block + 1) * BLK)
        stat = slice(side * PAD, side * PAD + 1)
        prob = jnp.exp(score - lse_ref[stat, rows])
        d_score = (prob * (d_prob - delta_ref[stat, rows])).astype(BF)
        d_queries[side] = dot_tn(d_score, k_ref[first:last, :])
        d_key = dot_nn(d_score, q_ref[rows, :])
        d_val = dot_nn(prob.astype(BF), do_ref[rows, :])
        for place, key_block in enumerate(range(first // BLK, last // BLK)):
            part = slice(place * BLK, (place + 1) * BLK)
            for sums, value in ((d_keys, d_key), (d_vals, d_val)):
                so_far = sums[side][key_block]
                sums[side][key_block] = value[part] if so_far is None else so_far + value[part]
        if side == 1:
            d_query = jnp.where(left, d_queries[0], d_queries[1]) + dot_nn(dsp_ref[rows, :], prefix_keys)
            mix_ref[0, rows, :] = (d_query * HEAD_DIM**-0.5).astype(BF)
    for block in range(blocks):
        rows = slice(block * BLK, (block + 1) * BLK)
        mix_ref[1, rows, :] = jnp.where(left, d_keys[0][block], d_keys[1][block]).astype(BF)
        mix_ref[2, rows, :] = jnp.where(left, d_vals[0][block], d_vals[1][block]).astype(BF)


def attend_back_kernel(bucket_ref, q_ref, *refs):
    args = (q_ref, *refs, pl.program_id(0))
    long_row = bucket_ref[0] == q_ref.shape[0]

    @pl.when(long_row)
    def _():
        attend_back(*args, True)

    @pl.when(jnp.logical_not(long_row))
    def _():
        attend_back(*args, False)


def project_back_kernel(d_mix_ref, w_ref, gain_ref, x_hbm, d_mid_hbm, grad_ref, acc_ref, x_ref, d_mid_ref, sems):
    step = pl.program_id(0)
    last = pl.num_programs(0) - 1
    slots = x_ref.shape[0]
    copies = [
        pltpu.make_async_copy(x_hbm, x_ref, sems.at[0]),
        pltpu.make_async_copy(d_mid_hbm, d_mid_ref, sems.at[1]),
    ]

    @pl.when(step == 0)
    def _():
        for copy in copies:
            copy.start()
        acc_ref[...] = dot_nt(d_mix_ref[0], w_ref[...])

    @pl.when((step > 0) & (step < last))
    def _():
        acc_ref[...] += dot_nt(d_mix_ref[0], w_ref[...])

    @pl.when(step == last)
    def _():
        for copy in copies:
            copy.wait()
        for first in range(0, slots, BLK):
            rows = slice(first, first + BLK)
            d_normed = acc_ref[rows, :] + dot_nt(d_mix_ref[0, rows, :], w_ref[...])
            norm, inv = normalise(x_ref[rows, :].astype(F32))
            back = norm_back(d_normed * row_of(gain_ref), norm, inv)
            grad_ref[rows, :] = (d_mid_ref[rows, :] + back).astype(BF)


def summed_in_order(place, pieces, ordered_ref):
    for shift, piece in enumerate(pieces):
        ordered_ref[(place + (len(pieces) - shift)) % len(pieces)] = piece[...]
    total = ordered_ref[0].astype(F32)
    for owner in range(1, len(pieces)):
        total = total + ordered_ref[owner].astype(F32)
    return total


def tail_kernel(place_ref, tanh_ref, embed_ref, in_w_ref, *refs):
    count = (len(refs) - 9) // 2
    weights, pieces = refs[:count], refs[count : 2 * count]
    (
        embed_grad_ref, in_grad_ref, in_bias_ref, out_grad_ref, out_bias_ref,
        pad_ref, ordered_ref, sum_ref, parts_ref,
    ) = refs[2 * count :]
    tanh_pre = tanh_ref[...]
    sum_ref[...] = summed_in_order(place_ref[0], pieces, ordered_ref).astype(BF)
    width = out_grad_ref.shape[1]
    for shift, weight in enumerate(weights):
        owner = (place_ref[0] + (count - shift)) % count
        own_cols = sum_ref[:, pl.ds(pl.multiple_of(owner * width, 128), width)]
        parts_ref[owner] = dot_nt(own_cols, weight[...])
        if shift == 0:
            out_grad_ref[...] = dot_tn(tanh_pre.astype(BF), own_cols)
            out_bias_ref[...] = jnp.sum(own_cols.astype(F32), axis=0, keepdims=True)
    d_hidden = parts_ref[0]
    for owner in range(1, count):
        d_hidden = d_hidden + parts_ref[owner]
    d_pre = (d_hidden * (1.0 - tanh_pre * tanh_pre)).astype(BF)
    in_grad_ref[...] = dot_tn(padded_embed(embed_ref, pad_ref), d_pre)
    in_bias_ref[...] = jnp.sum(d_pre.astype(F32), axis=0, keepdims=True)
    embed_grad_ref[...] = dot_nt(d_pre, in_w_ref[...])[0:PREFIX]


SMEM = pl.BlockSpec(memory_space=pltpu.SMEM)
ANY = pl.BlockSpec(memory_space=pl.ANY)


def params(mib):
    return pltpu.CompilerParams(vmem_limit_bytes=mib * 2**20, dimension_semantics=("arbitrary",))


def cost(flops, moved):
    return pl.CostEstimate(flops=int(flops), bytes_accessed=int(moved), transcendentals=0)


def shape(dims, dtype):
    return jax.ShapeDtypeStruct(dims, dtype)


def whole(array):
    return pl.BlockSpec(array.shape, lambda g: (0,) * len(array.shape))


def to_all(value, axis):
    size = lax.axis_size(axis)
    return [value] + [
        lax.ppermute(value, axis, [(place, (place + shift) % size) for place in range(size)])
        for shift in range(1, size)
    ]


def local(
    tokens, ln1_gain, ln1_shift, qkv_weight, qkv_bias, out_weight, out_bias, ln2_gain, ln2_shift, fc_weight,
    fc_bias, proj_weight, proj_bias, prefix_embed, reparam_in, reparam_in_bias, reparam_out, reparam_out_bias,
    bucket, seg_lens, cotangent,
):
    x, cot = tokens[0], cotangent[0]
    slots = x.shape[0]
    blocks = slots // BLK
    own_width = reparam_out.shape[1]
    hidden_width = reparam_in.shape[1]
    rep_place = lax.axis_index("rep").astype(jnp.int32)[None]

    reparam_args = (prefix_embed, reparam_in, reparam_in_bias, reparam_out, reparam_out_bias)
    reparam_outs = (shape((PAD, hidden_width), F32), shape((PAD, own_width), BF))
    tanh_pre, own_kv = pl.pallas_call(
        reparam_kernel,
        grid=(1,),
        out_shape=reparam_outs,
        in_specs=[whole(arg) for arg in reparam_args],
        out_specs=tuple(whole(out) for out in reparam_outs),
        scratch_shapes=[pltpu.VMEM((PAD, D), F32)],
        compiler_params=params(60),
        name="reparam",
    )(*reparam_args)
    prefix_pieces = to_all(own_kv, "rep")

    mixed = pl.pallas_call(
        project_kernel,
        grid=(3,),
        out_shape=shape((slots, 3 * D), BF),
        in_specs=[
            whole(x), whole(ln1_gain), whole(ln1_shift),
            pl.BlockSpec((D,), lambda n: (n,)),
            pl.BlockSpec((D, D), lambda n: (0, n)),
        ],
        out_specs=pl.BlockSpec((slots, D), lambda n: (0, n)),
        scratch_shapes=[pltpu.VMEM((slots, D), BF)],
        compiler_params=params(60),
        cost_estimate=cost(6 * slots * D * D, 16 * 2**20),
        name="project",
    )(x, ln1_gain, ln1_shift, qkv_bias, qkv_weight)
    late_weight, _ = lax.optimization_barrier((reparam_out, mixed))
    weight_pieces = to_all(late_weight, "rep")

    def quad_at(offset):
        return pl.BlockSpec((slots, QUAD), lambda g: (0, offset + jnp.minimum(g, QUADS - 1)))

    def block_of(width, start):
        return pl.BlockSpec((BLK, width), lambda g: (jnp.clip(g - start, 0, blocks - 1), 0))

    lanes = HEADS * PAD
    late = QUADS + blocks
    block_t = pl.BlockSpec((lanes, BLK), lambda g: (0, jnp.clip(g - late, 0, blocks - 1)))
    vectors = (out_bias, ln2_gain, ln2_shift, fc_bias, proj_bias)
    prefix_shape = shape((PAD, 2 * D), BF)
    block_out, d_mid, d_att, d_sp, lse_t, delta_t, prefix_row, prefix_kv = pl.pallas_call(
        forward_kernel,
        grid=(QUADS + 2 * blocks,),
        out_shape=(
            shape((slots, D), BF),
            shape((slots, D), F32),
            shape((slots, D), BF),
            shape((slots, lanes), BF),
            shape((lanes, slots), F32),
            shape((lanes, slots), F32),
            prefix_shape,
            prefix_shape,
        ),
        in_specs=[
            SMEM, SMEM, SMEM, quad_at(0), quad_at(QUADS), quad_at(2 * QUADS),
            block_of(D, QUADS), block_of(D, QUADS), block_of(D, late),
            *[whole(vector) for vector in vectors], ANY, ANY, ANY, *[whole(piece) for piece in prefix_pieces],
        ],
        out_specs=(
            block_of(D, late), block_of(D, late), block_of(D, late), block_of(lanes, late), block_t, block_t,
            whole(prefix_shape), whole(prefix_shape),
        ),
        scratch_shapes=[
            pltpu.VMEM((slots, D), BF),
            pltpu.VMEM((slots, lanes), BF),
            pltpu.VMEM((slots, lanes), F32),
            pltpu.VMEM((D, D), BF),
            pltpu.VMEM((D, FF), BF),
            pltpu.VMEM((FF, D), BF),
            pltpu.VMEM((slots, D), BF),
            pltpu.VMEM((slots, 1), F32),
            pltpu.VMEM((slots, D), BF),
            pltpu.VMEM((slots, D), BF),
            pltpu.VMEM((slots, D), F32),
            pltpu.VMEM((BLK, D), F32),
            pltpu.VMEM((BLK, CHUNK), F32),
            pltpu.VMEM((BLK, CHUNK), F32),
            pltpu.VMEM((1, FF), F32),
            pltpu.VMEM((lanes, D), BF),
            pltpu.VMEM((D, lanes), BF),
            pltpu.VMEM((lanes, D), F32),
            pltpu.VMEM((lanes, D), F32),
            pltpu.SemaphoreType.DMA((3,)),
        ],
        compiler_params=params(60),
        cost_estimate=cost(50e9, 40 * 2**20),
        name="forward",
    )(
        rep_place, bucket, seg_lens, mixed, mixed, mixed, x, cot, mixed, *vectors,
        out_weight, fc_weight, proj_weight, *prefix_pieces,
    )

    copies = jnp.broadcast_to(prefix_row, (lax.axis_size("batch"), *prefix_row.shape))
    batch_rows = lax.all_to_all(copies, "batch", split_axis=0, concat_axis=0, tiled=True)

    pairs = HEADS // 2

    def pair_at(offset):
        return pl.BlockSpec((slots, 128), lambda g: (0, offset + g))

    stat_spec = pl.BlockSpec((2 * PAD, slots), lambda g: (g, 0))
    d_mixed = pl.pallas_call(
        attend_back_kernel,
        grid=(pairs,),
        out_shape=shape((3, slots, D), BF),
        in_specs=[
            SMEM,
            pair_at(0), pair_at(pairs), pair_at(2 * pairs), pair_at(0),
            pl.BlockSpec((PAD, 128), lambda g: (0, g)),
            pl.BlockSpec((slots, 128), lambda g: (0, g // 4)),
            stat_spec, stat_spec,
        ],
        out_specs=pl.BlockSpec((3, slots, 128), lambda g: (0, 0, g)),
        compiler_params=params(60),
        cost_estimate=cost(28e9, 20 * 2**20),
        name="attend_back",
    )(bucket, mixed, mixed, mixed, d_att, prefix_kv, d_sp, lse_t, delta_t)

    group_sum = jnp.sum(batch_rows.astype(F32), axis=0).astype(BF)
    rep_pieces = to_all(group_sum, "rep")

    tokens_grad = pl.pallas_call(
        project_back_kernel,
        grid=(3,),
        out_shape=shape((slots, D), BF),
        in_specs=[
            pl.BlockSpec((1, slots, D), lambda t: (t, 0, 0)),
            pl.BlockSpec((D, D), lambda t: (0, t)),
            whole(ln1_gain), ANY, ANY,
        ],
        out_specs=pl.BlockSpec((slots, D), lambda t: (0, 0)),
        scratch_shapes=[
            pltpu.VMEM((slots, D), F32),
            pltpu.VMEM((slots, D), BF),
            pltpu.VMEM((slots, D), F32),
            pltpu.SemaphoreType.DMA((2,)),
        ],
        compiler_params=params(60),
        cost_estimate=cost(6 * slots * D * D, 20 * 2**20),
        name="project_back",
    )(d_mixed, qkv_weight, ln1_gain, x, d_mid)

    tail_args = (tanh_pre, prefix_embed, reparam_in, *weight_pieces, *rep_pieces)
    tail_outs = (
        shape((PREFIX, D), F32),
        shape((D, hidden_width), F32),
        shape((1, hidden_width), F32),
        shape((hidden_width, own_width), F32),
        shape((1, own_width), F32),
    )
    embed_grad, in_grad, in_bias_grad, out_grad, out_bias_grad = pl.pallas_call(
        tail_kernel,
        grid=(1,),
        out_shape=tail_outs,
        in_specs=[SMEM] + [whole(arg) for arg in tail_args],
        out_specs=tuple(whole(out) for out in tail_outs),
        scratch_shapes=[
            pltpu.VMEM((PAD, D), F32),
            pltpu.VMEM((len(rep_pieces), *prefix_shape.shape), BF),
            pltpu.VMEM(prefix_shape.shape, BF),
            pltpu.VMEM((len(rep_pieces), PAD, hidden_width), F32),
        ],
        compiler_params=params(16),
        name="tail",
    )(rep_place, *tail_args)
    return (
        block_out[None],
        tokens_grad[None],
        embed_grad,
        in_grad,
        in_bias_grad[0],
        out_grad,
        out_bias_grad[0],
    )


def solution(mesh):
    row = P(("batch", "rep"), None, None)
    placed = (row, *[P()] * 15, P(None, "rep"), P("rep"), P(("batch", "rep")), P(("batch", "rep"), None), row)
    return jax.shard_map(
        local,
        mesh=mesh,
        in_specs=placed,
        out_specs=(row, row, P(), P(), P(), P(None, "rep"), P("rep")),
        check_vma=False,
    )
```

```python
import jax
import jax.numpy as jnp
from jax import lax
from jax.experimental import pallas as pl
from jax.experimental.pallas import tpu as pltpu
from jax.sharding import PartitionSpec as P

D = 1024
HEADS = 16
HEAD_DIM = 64
FF = 4096
PREFIX = 10
PAD = 16
SHORT = 256
BLK = 256
QUAD = 4 * HEAD_DIM
QUADS = HEADS // 4
EARLY_PAIRS = 4
CHUNK = 1024

BF = jnp.bfloat16
F32 = jnp.float32
norm_eps = 1e-05
gelu_coef = 0.7978845608028654
gelu_cube = 0.044715
masked_score = -1e30


def dot_nn(left, right):
    return jnp.dot(left, right, preferred_element_type=F32)


def dot_nt(left, right):
    return lax.dot_general(left, right, (((1,), (1,)), ((), ())), preferred_element_type=F32)


def dot_tn(left, right):
    return lax.dot_general(left, right, (((0,), (0,)), ((), ())), preferred_element_type=F32)


def normalise(values):
    row_mean = jnp.mean(values, axis=-1, keepdims=True)
    centred = values - row_mean
    variance = jnp.mean(centred * centred, axis=-1, keepdims=True)
    inv = lax.rsqrt(variance + norm_eps)
    return centred * inv, inv


def norm_back(grad, norm, inv):
    along = jnp.mean(grad * norm, axis=-1, keepdims=True)
    return (grad - jnp.mean(grad, axis=-1, keepdims=True) - norm * along) * inv


def gelu_pair(u):
    sq = u * u
    w = jnp.tanh(u * (gelu_coef + (gelu_coef * gelu_cube) * sq))
    a = 0.5 * w + 0.5
    slope = a * (1.0 + u * (1.0 - a) * (2.0 * gelu_coef + (6.0 * gelu_coef * gelu_cube) * sq))
    return u * a, slope


def head_mask(shape, head):
    lane = lax.broadcasted_iota(jnp.int32, shape, 1)
    return (lane < HEAD_DIM) if head % 2 == 0 else (lane >= HEAD_DIM)


def quad_prefix(prefix, quad):
    row = lax.broadcasted_iota(jnp.int32, (128, QUAD), 0) // PAD
    col = lax.broadcasted_iota(jnp.int32, (128, QUAD), 1) // HEAD_DIM
    tiled = jnp.concatenate([prefix] * 8, axis=0)
    return jnp.where(row == col + 4 * (quad % 2), tiled, jnp.zeros_like(tiled))


def full_prefix(prefix):
    shape = (HEADS * PAD, D)
    row = lax.broadcasted_iota(jnp.int32, shape, 0) // PAD
    col = lax.broadcasted_iota(jnp.int32, shape, 1) // HEAD_DIM
    tiled = jnp.concatenate([prefix] * HEADS, axis=0)
    return jnp.where(row == col, tiled, jnp.zeros_like(tiled))


def row_of(ref, first=0, size=None):
    size = ref.shape[0] if size is None else size
    return ref[first : first + size].astype(F32)[None, :]


def padded_embed(embed_ref, pad_ref):
    pad_ref[...] = jnp.zeros_like(pad_ref)
    pad_ref[0:PREFIX, :] = embed_ref[...].astype(F32)
    return pad_ref[...].astype(BF)


def reparam_kernel(embed_ref, in_w_ref, in_b_ref, out_w_ref, out_b_ref, tanh_ref, kv_ref, pad_ref):
    tanh_pre = jnp.tanh(dot_nn(padded_embed(embed_ref, pad_ref), in_w_ref[...]) + row_of(in_b_ref))
    tanh_ref[...] = tanh_pre
    kv_ref[...] = (dot_nn(tanh_pre.astype(BF), out_w_ref[...]) + row_of(out_b_ref)).astype(BF)


def project_kernel(x_ref, gain_ref, shift_ref, bias_ref, w_ref, out_ref, normed_ref):
    step = pl.program_id(0)
    slots = x_ref.shape[0]
    factor = jnp.where(step == 0, HEAD_DIM**-0.5, 1.0)

    def norm_part(first):
        norm, _ = normalise(x_ref[first : first + BLK, :].astype(F32))
        normed_ref[first : first + BLK, :] = (norm * row_of(gain_ref) + row_of(shift_ref)).astype(BF)

    def dot_part(first, count):
        rows = pl.ds(first, count)
        mixed = dot_nn(normed_ref[rows, :], w_ref[...]) + row_of(bias_ref)
        out_ref[rows, :] = (mixed.astype(BF).astype(F32) * factor).astype(BF)

    @pl.when(step == 0)
    def _():
        norm_part(0)
        for first in range(0, slots, BLK):
            if first + BLK < slots:
                norm_part(first + BLK)
            dot_part(first, BLK)

    @pl.when(step > 0)
    def _():
        def body(index, carry):
            dot_part(pl.multiple_of(index * 2 * BLK, 2 * BLK), 2 * BLK)
            return carry

        lax.fori_loop(0, slots // (2 * BLK), body, 0)


def live_column(bucket_ref, lens_ref, first, rows, slots):
    position = lax.broadcasted_iota(jnp.int32, (rows, 1), 0) + first
    segment = position // SHORT
    total = jnp.int32(0)
    short_len = jnp.zeros((rows, 1), jnp.int32)
    for index in range(slots // SHORT):
        total = total + lens_ref[0, index]
        short_len = jnp.where(segment == index, lens_ref[0, index], short_len)
    return position < jnp.where(bucket_ref[0] == slots, total, segment * SHORT + short_len)


def block_rows(block):
    return pl.ds(block * BLK if isinstance(block, int) else pl.multiple_of(block * BLK, BLK), BLK)


def key_rows(block, long_row):
    return pl.ds(0, (block + 1) * BLK) if long_row else block_rows(block)


def attend(q_ref, k_ref, v_ref, prefix_ref, att_ref, pp_ref, lse_ref, quad, query_blocks, long_row):
    cols = pl.ds(pl.multiple_of(quad * QUAD, QUAD), QUAD)
    pair_cols = pl.ds(pl.multiple_of((quad // 2) * 128, 128), 128)
    prefix_keys = quad_prefix(prefix_ref[:, cols], quad)
    prefix_vals = quad_prefix(prefix_ref[:, pl.ds(pl.multiple_of(D + quad * QUAD, QUAD), QUAD)], quad)
    causal = lax.broadcasted_iota(jnp.int32, (BLK, BLK), 1) <= lax.broadcasted_iota(jnp.int32, (BLK, BLK), 0)
    lane = lax.broadcasted_iota(jnp.int32, (BLK, 128), 1)
    lane_head = lane // PAD - 4 * (quad % 2)
    lane_real = lane % PAD < PREFIX

    def scores(block, head):
        pair = slice(128 * (head // 2), 128 * (head // 2) + 128)
        queries = q_ref[block_rows(block), pair]
        queries = jnp.where(head_mask((BLK, 128), head), queries, jnp.zeros_like(queries))
        raw = dot_nt(queries, k_ref[key_rows(block, long_row), pair])
        own = jnp.where(causal, raw[:, -BLK:], masked_score)
        return own if raw.shape[1] == BLK else jnp.concatenate([raw[:, :-BLK], own], axis=1)

    units = [(block, head) for block in query_blocks for head in range(4)]
    ahead = 2
    queue = [scores(*unit) for unit in units[:ahead]]
    for index, (block, head) in enumerate(units):
        if index + ahead < len(units):
            queue.append(scores(*units[index + ahead]))
        rows = block_rows(block)
        if head == 0:
            prefix_raw = dot_nt(q_ref[rows, :], prefix_keys)
            probs_quad = jnp.zeros((BLK, 128), F32)
            lse_quad = jnp.zeros((BLK, 128), F32)
            outs = []
        pair = slice(128 * (head // 2), 128 * (head // 2) + 128)
        count = queue[index].shape[1]
        prefix_scores = jnp.where((lane_head == head) & lane_real, prefix_raw, masked_score)
        score = jnp.concatenate([queue[index], prefix_scores], axis=1)
        queue[index] = None
        peak = jnp.max(score, axis=1, keepdims=True)
        raised = jnp.exp(score - peak)
        summed = jnp.sum(raised, axis=1, keepdims=True)
        inv = 1.0 / summed
        outs.append(dot_nn(raised[:, :count].astype(BF), v_ref[key_rows(block, long_row), pair]) * inv)
        probs_quad = probs_quad + raised[:, count:] * inv
        lse_quad = jnp.where(lane_head == head, peak + jnp.log(summed), lse_quad)
        if head == 3:
            probs_low = probs_quad.astype(BF)
            left = head_mask((BLK, 128), 0)
            merged = jnp.concatenate(
                [jnp.where(left, outs[0], outs[1]), jnp.where(left, outs[2], outs[3])], axis=1
            ) + dot_nn(probs_low, prefix_vals)
            att_ref[rows, cols] = merged.astype(BF)

            @pl.when(quad % 2 == 0)
            def _():
                pp_ref[rows, pair_cols] = probs_low
                lse_ref[rows, pair_cols] = lse_quad

            @pl.when(quad % 2 == 1)
            def _():
                pp_ref[rows, pair_cols] = pp_ref[rows, pair_cols] + probs_low
                lse_ref[rows, pair_cols] = lse_ref[rows, pair_cols] + lse_quad


def forward_kernel(
    place_ref, bucket_ref, lens_ref, q_ref, k_ref, v_ref, x_ref, cot_ref, q_rows_ref,
    out_b_ref, gain_ref, shift_ref, fc_b_ref, proj_b_ref, out_w_hbm, fc_w_hbm, proj_w_hbm, *refs,
):
    pieces, refs = refs[: len(refs) - 29], refs[len(refs) - 29 :]
    (
        block_ref, d_mid_ref, d_att_ref, d_sp_ref, lse_t_ref, delta_t_ref, prefix_rows_hbm, prefix_ref,
        att_ref, pp_ref, lse_ref, out_w_ref, fc_w_ref, proj_w_ref, norm_ref, normed_ref, grad_out_ref,
        acc_ref, d_acc_ref, pre_ref, d_act_ref, bias_ref, vp_ref, spread_ref, d_kp_ref, d_vp_ref, row_ref, sems, row_sem,
    ) = refs
    step = pl.program_id(0)
    slots = q_ref.shape[0]
    copies = [
        pltpu.make_async_copy(out_w_hbm, out_w_ref, sems.at[0]),
        pltpu.make_async_copy(fc_w_hbm, fc_w_ref, sems.at[1]),
        pltpu.make_async_copy(proj_w_hbm, proj_w_ref, sems.at[2]),
    ]
    long_row = bucket_ref[0] == slots

    @pl.when(step == 0)
    def _():
        for copy in copies:
            copy.start()
        width = pieces[0].shape[1]
        for shift, piece in enumerate(pieces):
            owner = (place_ref[0] + (len(pieces) - shift)) % len(pieces)
            prefix_ref[:, pl.ds(pl.multiple_of(owner * width, 128), width)] = piece[...]
        vp_ref[...] = full_prefix(prefix_ref[:, D:])
        row = lax.broadcasted_iota(jnp.int32, (D, HEADS * PAD), 0) // HEAD_DIM
        col = lax.broadcasted_iota(jnp.int32, (D, HEADS * PAD), 1) // PAD
        spread_ref[...] = jnp.where(row == col, 1.0, 0.0).astype(BF)
        bias_ref[...] = row_of(fc_b_ref)
        d_kp_ref[...] = jnp.zeros_like(d_kp_ref)
        d_vp_ref[...] = jnp.zeros_like(d_vp_ref)

    attend_args = (q_ref, k_ref, v_ref, prefix_ref, att_ref, pp_ref, lse_ref, step)

    @pl.when((step < QUADS) & long_row)
    def _():
        attend(*attend_args, list(range(slots // BLK)), True)

    @pl.when((step < QUADS) & jnp.logical_not(long_row))
    def _():
        def body(block, carry):
            attend(*attend_args, [block], False)
            return carry

        lax.fori_loop(0, slots // BLK, body, 0)

    @pl.when(step == QUADS)
    def _():
        for copy in copies:
            copy.wait()

    @pl.when(step >= QUADS)
    def _():
        first = pl.multiple_of((step - QUADS) * BLK, BLK)
        rows = pl.ds(first, BLK)
        live = live_column(bucket_ref, lens_ref, first, BLK, slots)
        attended = att_ref[rows, :]
        mid = x_ref[...].astype(F32) + dot_nn(attended, out_w_ref[...]) + row_of(out_b_ref)
        norm, inv = normalise(mid)
        norm_ref[...] = norm
        normed_ref[...] = (norm * row_of(gain_ref) + row_of(shift_ref)).astype(BF)
        grad_out_ref[...] = jnp.where(live, cot_ref[...].astype(F32), 0.0).astype(BF)
        acc_ref[...] = mid + row_of(proj_b_ref)
        d_acc_ref[...] = jnp.zeros_like(d_acc_ref)

        def opened(chunk):
            part = pl.ds(pl.multiple_of(chunk * CHUNK, CHUNK), CHUNK)
            pre = dot_nn(normed_ref[...], fc_w_ref[:, part]) + bias_ref[:, part]
            return pre, dot_nt(grad_out_ref[...], proj_w_ref[part, :])

        def closed(chunk, pre, d_act):
            part = pl.ds(pl.multiple_of(chunk * CHUNK, CHUNK), CHUNK)
            act, slope = gelu_pair(pre)
            forth = dot_nn(act.astype(BF), proj_w_ref[part, :])
            back = dot_nt((d_act * slope).astype(BF), fc_w_ref[:, part])
            return acc_ref[...] + forth, d_acc_ref[...] + back

        def chunk_step(chunk, carry):
            pre, d_act = pre_ref[...], d_act_ref[...]
            next_pre, next_d_act = opened(chunk + 1)
            acc_ref[...], d_acc_ref[...] = closed(chunk, pre, d_act)
            pre_ref[...], d_act_ref[...] = next_pre, next_d_act
            return carry

        chunks = FF // CHUNK
        pre_ref[...], d_act_ref[...] = opened(0)
        lax.fori_loop(0, chunks - 1, chunk_step, 0)
        result, d_normed = closed(chunks - 1, pre_ref[...], d_act_ref[...])
        block_ref[...] = jnp.where(live, result, 0.0).astype(BF)
        d_mid = grad_out_ref[...].astype(F32) + norm_back(d_normed * row_of(gain_ref), norm_ref[...], inv)
        d_mid_ref[...] = d_mid
        d_att = dot_nt(d_mid.astype(BF), out_w_ref[...]).astype(BF)
        d_att_ref[...] = d_att
        product = (d_att.astype(F32) * attended.astype(F32)).astype(BF)
        delta = dot_nn(product, spread_ref[...])
        probs = pp_ref[rows, :]
        d_sp = (probs.astype(F32) * (dot_nt(d_att, vp_ref[...]) - delta)).astype(BF)
        d_sp_ref[...] = d_sp
        d_kp_ref[...] += dot_tn(d_sp, q_rows_ref[...])
        d_vp_ref[...] += dot_tn(probs, d_att)
        lse_t_ref[...] = lse_ref[rows, :].T
        delta_t_ref[...] = delta.T

    @pl.when(step == pl.num_programs(0) - 1)
    def _():
        shape = (HEADS * PAD, D)
        own = (
            lax.broadcasted_iota(jnp.int32, shape, 0) // PAD
            == lax.broadcasted_iota(jnp.int32, shape, 1) // HEAD_DIM
        )
        for index, ref in enumerate((d_kp_ref, d_vp_ref)):
            kept = jnp.where(own, ref[...], 0.0)
            total = kept[0:PAD, :]
            for head in range(1, HEADS):
                total = total + kept[head * PAD : (head + 1) * PAD, :]
            row_ref[:, index * D : (index + 1) * D] = total.astype(BF)
        sends = [
            pltpu.make_async_copy(row_ref, prefix_rows_hbm.at[place], row_sem)
            for place in range(prefix_rows_hbm.shape[0])
        ]
        for send in sends:
            send.start()
        for send in sends:
            send.wait()


def attend_back(
    q_ref, k_ref, v_ref, do_ref, pk_ref, dsp_ref, lse_ref, delta_ref, mix_ref, cols, pair, query_blocks, long_row
):
    causal = lax.broadcasted_iota(jnp.int32, (BLK, BLK), 0) <= lax.broadcasted_iota(jnp.int32, (BLK, BLK), 1)
    left = head_mask((BLK, 128), 0)
    row = lax.broadcasted_iota(jnp.int32, (128, 128), 0) // PAD
    col = lax.broadcasted_iota(jnp.int32, (128, 128), 1) // HEAD_DIM
    tiled = jnp.concatenate([pk_ref[...]] * 8, axis=0)
    prefix_keys = jnp.where(row == col + 2 * (pair % 4), tiled, jnp.zeros_like(tiled))

    def opened(block, side):
        rows, keys = block_rows(block), key_rows(block, long_row)
        mask = head_mask((BLK, 128), side)
        queries, d_out = q_ref[rows, :], do_ref[rows, :]
        raw = dot_nt(k_ref[keys, :], jnp.where(mask, queries, jnp.zeros_like(queries)))
        d_prob = dot_nt(v_ref[keys, :], jnp.where(mask, d_out, jnp.zeros_like(d_out)))
        own = jnp.where(causal, raw[-BLK:], masked_score)
        return (own if raw.shape[0] == BLK else jnp.concatenate([raw[:-BLK], own], axis=0)), d_prob

    units = [(block, side) for block in query_blocks for side in range(2)]
    ahead = 2
    queue = [opened(*unit) for unit in units[:ahead]]
    d_keys = [[None] * len(query_blocks) for _ in range(2)]
    d_vals = [[None] * len(query_blocks) for _ in range(2)]
    d_queries = [None, None]
    for index, (block, side) in enumerate(units):
        if index + ahead < len(units):
            queue.append(opened(*units[index + ahead]))
        score, d_prob = queue[index]
        queue[index] = None
        rows, keys = block_rows(block), key_rows(block, long_row)
        stat = slice(side * PAD, side * PAD + 1)
        prob = jnp.exp(score - lse_ref[stat, rows])
        d_score = (prob * (d_prob - delta_ref[stat, rows])).astype(BF)
        d_queries[side] = dot_tn(d_score, k_ref[keys, :])
        d_key = dot_nn(d_score, q_ref[rows, :])
        d_val = dot_nn(prob.astype(BF), do_ref[rows, :])
        for place in range(d_key.shape[0] // BLK):
            part = slice(place * BLK, (place + 1) * BLK)
            for sums, value in ((d_keys, d_key), (d_vals, d_val)):
                so_far = sums[side][place]
                sums[side][place] = value[part] if so_far is None else so_far + value[part]
        if side == 1:
            d_query = jnp.where(left, d_queries[0], d_queries[1]) + dot_nn(dsp_ref[rows, :], prefix_keys)
            mix_ref[0, rows, cols] = (d_query * HEAD_DIM**-0.5).astype(BF)
    for place, block in enumerate(query_blocks):
        rows = block_rows(block)
        mix_ref[1, rows, cols] = jnp.where(left, d_keys[0][place], d_keys[1][place]).astype(BF)
        mix_ref[2, rows, cols] = jnp.where(left, d_vals[0][place], d_vals[1][place]).astype(BF)


def attend_back_pair(bucket_ref, refs, mix_ref, cols, pair, here):
    blocks = refs[0].shape[0] // BLK
    long_row = bucket_ref[0] == refs[0].shape[0]
    args = (*refs, mix_ref, cols, pair)

    @pl.when(here & long_row)
    def _():
        attend_back(*args, list(range(blocks)), True)

    @pl.when(here & jnp.logical_not(long_row))
    def _():
        def body(block, carry):
            attend_back(*args, [block], False)
            return carry

        lax.fori_loop(0, blocks, body, 0)


def early_back_kernel(bucket_ref, *refs):
    *refs, mix_ref = refs
    step = pl.program_id(0)
    attend_back_pair(bucket_ref, refs, mix_ref, slice(0, 128), step, step >= 0)


def backward_kernel(bucket_ref, *refs):
    refs, (early_ref, x_ref, d_mid_ref, gain_ref, w_hbm, grad_ref, mix_ref, w_ref, sem) = refs[:8], refs[8:]
    step = pl.program_id(0)
    pairs = mix_ref.shape[2] // 128
    copy = pltpu.make_async_copy(w_hbm, w_ref, sem)

    @pl.when(step == 0)
    def _():
        copy.start()

    cols = pl.ds(pl.multiple_of(jnp.minimum(step, pairs - 1) * 128, 128), 128)
    attend_back_pair(bucket_ref, refs, mix_ref, cols, step + (HEADS // 2 - pairs), step < pairs)

    @pl.when(step == pairs)
    def _():
        copy.wait()

    @pl.when(step >= pairs)
    def _():
        rows = block_rows(step - pairs)
        d_mixed = jnp.concatenate(
            [part for third in range(3) for part in (early_ref[third], mix_ref[third, rows, :])], axis=1
        )
        d_normed = dot_nt(d_mixed, w_ref[...])
        norm, inv = normalise(x_ref[...].astype(F32))
        back = norm_back(d_normed * row_of(gain_ref), norm, inv)
        grad_ref[...] = (d_mid_ref[...] + back).astype(BF)


def summed_in_order(place, pieces, ordered_ref):
    for shift, piece in enumerate(pieces):
        ordered_ref[(place + (len(pieces) - shift)) % len(pieces)] = piece[...]
    total = ordered_ref[0].astype(F32)
    for owner in range(1, len(pieces)):
        total = total + ordered_ref[owner].astype(F32)
    return total


def tail_kernel(place_ref, tanh_ref, embed_ref, in_w_ref, *refs):
    count = (len(refs) - 9) // 2
    weights, pieces = refs[:count], refs[count : 2 * count]
    (
        embed_grad_ref, in_grad_ref, in_bias_ref, out_grad_ref, out_bias_ref,
        pad_ref, ordered_ref, sum_ref, parts_ref,
    ) = refs[2 * count :]
    tanh_pre = tanh_ref[...]
    sum_ref[...] = summed_in_order(place_ref[0], pieces, ordered_ref).astype(BF)
    width = out_grad_ref.shape[1]
    for shift, weight in enumerate(weights):
        owner = (place_ref[0] + (count - shift)) % count
        own_cols = sum_ref[:, pl.ds(pl.multiple_of(owner * width, 128), width)]
        parts_ref[owner] = dot_nt(own_cols, weight[...])
        if shift == 0:
            out_grad_ref[...] = dot_tn(tanh_pre.astype(BF), own_cols)
            out_bias_ref[...] = jnp.sum(own_cols.astype(F32), axis=0, keepdims=True)
    d_hidden = parts_ref[0]
    for owner in range(1, count):
        d_hidden = d_hidden + parts_ref[owner]
    d_pre = (d_hidden * (1.0 - tanh_pre * tanh_pre)).astype(BF)
    in_grad_ref[...] = dot_tn(padded_embed(embed_ref, pad_ref), d_pre)
    in_bias_ref[...] = jnp.sum(d_pre.astype(F32), axis=0, keepdims=True)
    embed_grad_ref[...] = dot_nt(d_pre, in_w_ref[...])[0:PREFIX]


SMEM = pl.BlockSpec(memory_space=pltpu.SMEM)
ANY = pl.BlockSpec(memory_space=pl.ANY)


def params(mib):
    return pltpu.CompilerParams(vmem_limit_bytes=mib * 2**20, dimension_semantics=("arbitrary",))


def cost(flops, moved):
    return pl.CostEstimate(flops=int(flops), bytes_accessed=int(moved), transcendentals=0)


def shape(dims, dtype):
    return jax.ShapeDtypeStruct(dims, dtype)


def whole(array):
    return pl.BlockSpec(array.shape, lambda g: (0,) * len(array.shape))


def to_all(value, axis):
    size = lax.axis_size(axis)
    return [value] + [
        lax.ppermute(value, axis, [(place, (place + shift) % size) for place in range(size)])
        for shift in range(1, size)
    ]


def local(
    tokens, ln1_gain, ln1_shift, qkv_weight, qkv_bias, out_weight, out_bias, ln2_gain, ln2_shift, fc_weight,
    fc_bias, proj_weight, proj_bias, prefix_embed, reparam_in, reparam_in_bias, reparam_out, reparam_out_bias,
    bucket, seg_lens, cotangent,
):
    x, cot = tokens[0], cotangent[0]
    slots = x.shape[0]
    blocks = slots // BLK
    own_width = reparam_out.shape[1]
    hidden_width = reparam_in.shape[1]
    rep_place = lax.axis_index("rep").astype(jnp.int32)[None]

    reparam_args = (prefix_embed, reparam_in, reparam_in_bias, reparam_out, reparam_out_bias)
    reparam_outs = (shape((PAD, hidden_width), F32), shape((PAD, own_width), BF))
    tanh_pre, own_kv = pl.pallas_call(
        reparam_kernel,
        grid=(1,),
        out_shape=reparam_outs,
        in_specs=[whole(arg) for arg in reparam_args],
        out_specs=tuple(whole(out) for out in reparam_outs),
        scratch_shapes=[pltpu.VMEM((PAD, D), F32)],
        compiler_params=params(60),
        name="reparam",
    )(*reparam_args)
    prefix_pieces = to_all(own_kv, "rep")

    mixed = pl.pallas_call(
        project_kernel,
        grid=(3,),
        out_shape=shape((slots, 3 * D), BF),
        in_specs=[
            whole(x), whole(ln1_gain), whole(ln1_shift),
            pl.BlockSpec((D,), lambda n: (n,)),
            pl.BlockSpec((D, D), lambda n: (0, n)),
        ],
        out_specs=pl.BlockSpec((slots, D), lambda n: (0, n)),
        scratch_shapes=[pltpu.VMEM((slots, D), BF)],
        compiler_params=params(60),
        cost_estimate=cost(6 * slots * D * D, 16 * 2**20),
        name="project",
    )(x, ln1_gain, ln1_shift, qkv_bias, qkv_weight)
    late_weight, _ = lax.optimization_barrier((reparam_out, mixed))
    weight_pieces = to_all(late_weight, "rep")

    def quad_at(offset):
        return pl.BlockSpec((slots, QUAD), lambda g: (0, offset + jnp.minimum(g, QUADS - 1)))

    def block_of(width):
        return pl.BlockSpec((BLK, width), lambda g: (jnp.maximum(g - QUADS, 0), 0))

    lanes = HEADS * PAD
    block_t = pl.BlockSpec((lanes, BLK), lambda g: (0, jnp.maximum(g - QUADS, 0)))
    vectors = (out_bias, ln2_gain, ln2_shift, fc_bias, proj_bias)
    prefix_shape = shape((PAD, 2 * D), BF)
    block_out, d_mid, d_att, d_sp, lse_t, delta_t, prefix_rows, prefix_kv = pl.pallas_call(
        forward_kernel,
        grid=(QUADS + blocks,),
        out_shape=(
            shape((slots, D), BF),
            shape((slots, D), F32),
            shape((slots, D), BF),
            shape((slots, lanes), BF),
            shape((lanes, slots), F32),
            shape((lanes, slots), F32),
            shape((lax.axis_size("batch"), *prefix_shape.shape), BF),
            prefix_shape,
        ),
        in_specs=[
            SMEM, SMEM, SMEM, quad_at(0), quad_at(QUADS), quad_at(2 * QUADS),
            block_of(D), block_of(D), block_of(D),
            *[whole(vector) for vector in vectors], ANY, ANY, ANY, *[whole(piece) for piece in prefix_pieces],
        ],
        out_specs=(
            block_of(D), block_of(D), block_of(D), block_of(lanes), block_t, block_t,
            ANY, whole(prefix_shape),
        ),
        scratch_shapes=[
            pltpu.VMEM((slots, D), BF),
            pltpu.VMEM((slots, lanes), BF),
            pltpu.VMEM((slots, lanes), F32),
            pltpu.VMEM((D, D), BF),
            pltpu.VMEM((D, FF), BF),
            pltpu.VMEM((FF, D), BF),
            pltpu.VMEM((BLK, D), F32),
            pltpu.VMEM((BLK, D), BF),
            pltpu.VMEM((BLK, D), BF),
            pltpu.VMEM((BLK, D), F32),
            pltpu.VMEM((BLK, D), F32),
            pltpu.VMEM((BLK, CHUNK), F32),
            pltpu.VMEM((BLK, CHUNK), F32),
            pltpu.VMEM((1, FF), F32),
            pltpu.VMEM((lanes, D), BF),
            pltpu.VMEM((D, lanes), BF),
            pltpu.VMEM((lanes, D), F32),
            pltpu.VMEM((lanes, D), F32),
            pltpu.VMEM(prefix_shape.shape, BF),
            pltpu.SemaphoreType.DMA((3,)),
            pltpu.SemaphoreType.DMA,
        ],
        compiler_params=params(60),
        cost_estimate=cost(50e9, 40 * 2**20),
        name="forward",
    )(
        rep_place, bucket, seg_lens, mixed, mixed, mixed, x, cot, mixed, *vectors,
        out_weight, fc_weight, proj_weight, *prefix_pieces,
    )

    batch_rows = lax.all_to_all(prefix_rows, "batch", split_axis=0, concat_axis=0, tiled=True)

    pairs = HEADS // 2
    early = EARLY_PAIRS

    def back_specs(start, count):
        def pair_of(g):
            return start + jnp.minimum(g, count - 1)

        def pair_at(offset):
            return pl.BlockSpec((slots, 128), lambda g: (0, offset + pair_of(g)))

        stat_spec = pl.BlockSpec((2 * PAD, slots), lambda g: (pair_of(g), 0))
        return [
            SMEM,
            pair_at(0), pair_at(pairs), pair_at(2 * pairs), pair_at(0),
            pl.BlockSpec((PAD, 128), lambda g: (0, pair_of(g))),
            pl.BlockSpec((slots, 128), lambda g: (0, pair_of(g) // 4)),
            stat_spec, stat_spec,
        ]

    back_args = (bucket, mixed, mixed, mixed, d_att, prefix_kv, d_sp, lse_t, delta_t)
    d_mixed = pl.pallas_call(
        early_back_kernel,
        grid=(early,),
        out_shape=shape((3, slots, early * 128), BF),
        in_specs=back_specs(0, early),
        out_specs=pl.BlockSpec((3, slots, 128), lambda g: (0, 0, g)),
        compiler_params=params(60),
        cost_estimate=cost(14e9, 10 * 2**20),
        name="early_back",
    )(*back_args)

    group_sum = jnp.sum(batch_rows.astype(F32), axis=0).astype(BF)
    rep_pieces = to_all(group_sum, "rep")

    late = pairs - early
    late_rows = pl.BlockSpec((BLK, D), lambda g: (jnp.maximum(g - late, 0), 0))
    tokens_grad = pl.pallas_call(
        backward_kernel,
        grid=(late + blocks,),
        out_shape=shape((slots, D), BF),
        in_specs=[
            *back_specs(early, late),
            pl.BlockSpec((3, BLK, early * 128), lambda g: (0, jnp.maximum(g - late, 0), 0)),
            late_rows, late_rows, whole(ln1_gain), ANY,
        ],
        out_specs=late_rows,
        scratch_shapes=[
            pltpu.VMEM((3, slots, late * 128), BF),
            pltpu.VMEM((D, 3 * D), BF),
            pltpu.SemaphoreType.DMA,
        ],
        compiler_params=params(60),
        cost_estimate=cost(24e9, 30 * 2**20),
        name="backward",
    )(*back_args, d_mixed, x, d_mid, ln1_gain, qkv_weight)

    tail_args = (tanh_pre, prefix_embed, reparam_in, *weight_pieces, *rep_pieces)
    tail_outs = (
        shape((PREFIX, D), F32),
        shape((D, hidden_width), F32),
        shape((1, hidden_width), F32),
        shape((hidden_width, own_width), F32),
        shape((1, own_width), F32),
    )
    embed_grad, in_grad, in_bias_grad, out_grad, out_bias_grad = pl.pallas_call(
        tail_kernel,
        grid=(1,),
        out_shape=tail_outs,
        in_specs=[SMEM] + [whole(arg) for arg in tail_args],
        out_specs=tuple(whole(out) for out in tail_outs),
        scratch_shapes=[
            pltpu.VMEM((PAD, D), F32),
            pltpu.VMEM((len(rep_pieces), *prefix_shape.shape), BF),
            pltpu.VMEM(prefix_shape.shape, BF),
            pltpu.VMEM((len(rep_pieces), PAD, hidden_width), F32),
        ],
        compiler_params=params(16),
        name="tail",
    )(rep_place, *tail_args)
    return (
        block_out[None],
        tokens_grad[None],
        embed_grad,
        in_grad,
        in_bias_grad[0],
        out_grad,
        out_bias_grad[0],
    )


def solution(mesh):
    row = P(("batch", "rep"), None, None)
    placed = (row, *[P()] * 15, P(None, "rep"), P("rep"), P(("batch", "rep")), P(("batch", "rep"), None), row)
    return jax.shard_map(
        local,
        mesh=mesh,
        in_specs=placed,
        out_specs=(row, row, P(), P(), P(), P(None, "rep"), P("rep")),
        check_vma=False,
    )
```

```python
import jax
import jax.numpy as jnp
from jax import lax
from jax.experimental import pallas as pl
from jax.experimental.pallas import tpu as pltpu
from jax.sharding import PartitionSpec as P

D = 1024
HEADS = 16
HEAD_DIM = 64
FF = 4096
PREFIX = 10
PAD = 16
SHORT = 256
PAD_BITS, HEAD_DIM_BITS, SHORT_BITS = 4, 6, 8
BLK = 256
QUAD = 4 * HEAD_DIM
QUADS = HEADS // 4
EARLY_PAIRS = 4
CHUNK = 1024

BF = jnp.bfloat16
F32 = jnp.float32
norm_eps = 1e-05
gelu_coef = 0.7978845608028654
gelu_cube = 0.044715
masked_score = -1e30


def dot_nn(left, right):
    return jnp.dot(left, right, preferred_element_type=F32)


def dot_nt(left, right):
    return lax.dot_general(left, right, (((1,), (1,)), ((), ())), preferred_element_type=F32)


def dot_tn(left, right):
    return lax.dot_general(left, right, (((0,), (0,)), ((), ())), preferred_element_type=F32)


def normalise(values):
    row_mean = jnp.mean(values, axis=-1, keepdims=True)
    centred = values - row_mean
    variance = jnp.mean(centred * centred, axis=-1, keepdims=True)
    inv = lax.rsqrt(variance + norm_eps)
    return centred * inv, inv


def norm_back(grad, norm, inv):
    along = jnp.mean(grad * norm, axis=-1, keepdims=True)
    return (grad - jnp.mean(grad, axis=-1, keepdims=True) - norm * along) * inv


def gelu_pair(u):
    sq = u * u
    w = jnp.tanh(u * (gelu_coef + (gelu_coef * gelu_cube) * sq))
    a = 0.5 * w + 0.5
    slope = a * (1.0 + u * (1.0 - a) * (2.0 * gelu_coef + (6.0 * gelu_coef * gelu_cube) * sq))
    return u * a, slope


def head_mask(shape, head):
    lane = lax.broadcasted_iota(jnp.int32, shape, 1)
    return (lane < HEAD_DIM) if head % 2 == 0 else (lane >= HEAD_DIM)


def quad_prefix(prefix, quad):
    row = lax.broadcasted_iota(jnp.int32, (128, QUAD), 0) >> PAD_BITS
    col = lax.broadcasted_iota(jnp.int32, (128, QUAD), 1) >> HEAD_DIM_BITS
    tiled = jnp.concatenate([prefix] * 8, axis=0)
    return jnp.where(row == col + 4 * (quad % 2), tiled, jnp.zeros_like(tiled))


def full_prefix(prefix):
    shape = (HEADS * PAD, D)
    row = lax.broadcasted_iota(jnp.int32, shape, 0) >> PAD_BITS
    col = lax.broadcasted_iota(jnp.int32, shape, 1) >> HEAD_DIM_BITS
    tiled = jnp.concatenate([prefix] * HEADS, axis=0)
    return jnp.where(row == col, tiled, jnp.zeros_like(tiled))


def row_of(ref, first=0, size=None):
    size = ref.shape[0] if size is None else size
    return ref[first : first + size].astype(F32)[None, :]


def padded_embed(embed_ref, pad_ref):
    pad_ref[...] = jnp.zeros_like(pad_ref)
    pad_ref[0:PREFIX, :] = embed_ref[...].astype(F32)
    return pad_ref[...].astype(BF)


def reparam_kernel(embed_ref, in_w_ref, in_b_ref, out_w_ref, out_b_ref, tanh_ref, kv_ref, pad_ref):
    tanh_pre = jnp.tanh(dot_nn(padded_embed(embed_ref, pad_ref), in_w_ref[...]) + row_of(in_b_ref))
    tanh_ref[...] = tanh_pre
    kv_ref[...] = (dot_nn(tanh_pre.astype(BF), out_w_ref[...]) + row_of(out_b_ref)).astype(BF)


def project_kernel(x_ref, gain_ref, shift_ref, bias_ref, w_ref, out_ref, normed_ref):
    step = pl.program_id(0)
    slots = x_ref.shape[0]
    factor = jnp.where(step == 0, HEAD_DIM**-0.5, 1.0)

    def norm_part(first):
        norm, _ = normalise(x_ref[first : first + BLK, :].astype(F32))
        normed_ref[first : first + BLK, :] = (norm * row_of(gain_ref) + row_of(shift_ref)).astype(BF)

    def dot_part(first, count):
        rows = pl.ds(first, count)
        mixed = dot_nn(normed_ref[rows, :], w_ref[...]) + row_of(bias_ref)
        out_ref[rows, :] = (mixed.astype(BF).astype(F32) * factor).astype(BF)

    @pl.when(step == 0)
    def _():
        norm_part(0)
        for first in range(0, slots, BLK):
            if first + BLK < slots:
                norm_part(first + BLK)
            dot_part(first, BLK)

    @pl.when(step > 0)
    def _():
        def body(index, carry):
            dot_part(pl.multiple_of(index * 2 * BLK, 2 * BLK), 2 * BLK)
            return carry

        lax.fori_loop(0, slots // (2 * BLK), body, 0)


def live_column(bucket_ref, lens_ref, first, rows, slots):
    position = lax.broadcasted_iota(jnp.int32, (rows, 1), 0) + first
    segment = position >> SHORT_BITS
    total = jnp.int32(0)
    short_len = jnp.zeros((rows, 1), jnp.int32)
    for index in range(slots // SHORT):
        total = total + lens_ref[0, index]
        short_len = jnp.where(segment == index, lens_ref[0, index], short_len)
    return position < jnp.where(bucket_ref[0] == slots, total, segment * SHORT + short_len)


def block_rows(block):
    return pl.ds(block * BLK if isinstance(block, int) else pl.multiple_of(block * BLK, BLK), BLK)


def key_rows(block, long_row):
    return pl.ds(0, (block + 1) * BLK) if long_row else block_rows(block)


def attend(q_ref, k_ref, v_ref, prefix_ref, att_ref, pp_ref, lse_ref, quad, query_blocks, long_row):
    cols = pl.ds(pl.multiple_of(quad * QUAD, QUAD), QUAD)
    pair_cols = pl.ds(pl.multiple_of((quad // 2) * 128, 128), 128)
    prefix_keys = quad_prefix(prefix_ref[:, cols], quad)
    prefix_vals = quad_prefix(prefix_ref[:, pl.ds(pl.multiple_of(D + quad * QUAD, QUAD), QUAD)], quad)
    causal = lax.broadcasted_iota(jnp.int32, (BLK, BLK), 1) <= lax.broadcasted_iota(jnp.int32, (BLK, BLK), 0)
    lane = lax.broadcasted_iota(jnp.int32, (BLK, 128), 1)
    lane_head = (lane >> PAD_BITS) - 4 * (quad % 2)
    lane_real = (lane & (PAD - 1)) < PREFIX

    def scores(block, head):
        pair = slice(128 * (head // 2), 128 * (head // 2) + 128)
        queries = q_ref[block_rows(block), pair]
        queries = jnp.where(head_mask((BLK, 128), head), queries, jnp.zeros_like(queries))
        raw = dot_nt(queries, k_ref[key_rows(block, long_row), pair])
        own = jnp.where(causal, raw[:, -BLK:], masked_score)
        return own if raw.shape[1] == BLK else jnp.concatenate([raw[:, :-BLK], own], axis=1)

    units = [(block, head) for block in query_blocks for head in range(4)]
    ahead = 2
    queue = [scores(*unit) for unit in units[:ahead]]
    for index, (block, head) in enumerate(units):
        if index + ahead < len(units):
            queue.append(scores(*units[index + ahead]))
        rows = block_rows(block)
        if head == 0:
            prefix_raw = dot_nt(q_ref[rows, :], prefix_keys)
            probs_quad = jnp.zeros((BLK, 128), F32)
            lse_quad = jnp.zeros((BLK, 128), F32)
            outs = []
        pair = slice(128 * (head // 2), 128 * (head // 2) + 128)
        count = queue[index].shape[1]
        prefix_scores = jnp.where((lane_head == head) & lane_real, prefix_raw, masked_score)
        score = jnp.concatenate([queue[index], prefix_scores], axis=1)
        queue[index] = None
        peak = jnp.max(score, axis=1, keepdims=True)
        raised = jnp.exp(score - peak)
        summed = jnp.sum(raised, axis=1, keepdims=True)
        inv = 1.0 / summed
        outs.append(dot_nn(raised[:, :count].astype(BF), v_ref[key_rows(block, long_row), pair]) * inv)
        probs_quad = probs_quad + raised[:, count:] * inv
        lse_quad = jnp.where(lane_head == head, peak + jnp.log(summed), lse_quad)
        if head == 3:
            probs_low = probs_quad.astype(BF)
            left = head_mask((BLK, 128), 0)
            merged = jnp.concatenate(
                [jnp.where(left, outs[0], outs[1]), jnp.where(left, outs[2], outs[3])], axis=1
            ) + dot_nn(probs_low, prefix_vals)
            att_ref[rows, cols] = merged.astype(BF)

            @pl.when(quad % 2 == 0)
            def _():
                pp_ref[rows, pair_cols] = probs_low
                lse_ref[rows, pair_cols] = lse_quad

            @pl.when(quad % 2 == 1)
            def _():
                pp_ref[rows, pair_cols] = pp_ref[rows, pair_cols] + probs_low
                lse_ref[rows, pair_cols] = lse_ref[rows, pair_cols] + lse_quad


def forward_kernel(
    place_ref, bucket_ref, lens_ref, q_ref, k_ref, v_ref, x_ref, cot_ref, q_rows_ref,
    out_b_ref, gain_ref, shift_ref, fc_b_ref, proj_b_ref, out_w_hbm, fc_w_hbm, proj_w_hbm, *refs,
):
    pieces, refs = refs[: len(refs) - 29], refs[len(refs) - 29 :]
    (
        block_ref, d_mid_ref, d_att_ref, d_sp_ref, lse_t_ref, delta_t_ref, prefix_rows_hbm, prefix_ref,
        att_ref, pp_ref, lse_ref, out_w_ref, fc_w_ref, proj_w_ref, norm_ref, normed_ref, grad_out_ref,
        acc_ref, d_acc_ref, pre_ref, d_act_ref, bias_ref, vp_ref, spread_ref, d_kp_ref, d_vp_ref, row_ref, sems, row_sem,
    ) = refs
    step = pl.program_id(0)
    slots = q_ref.shape[0]
    copies = [
        pltpu.make_async_copy(out_w_hbm, out_w_ref, sems.at[0]),
        pltpu.make_async_copy(fc_w_hbm, fc_w_ref, sems.at[1]),
        pltpu.make_async_copy(proj_w_hbm, proj_w_ref, sems.at[2]),
    ]
    long_row = bucket_ref[0] == slots

    @pl.when(step == 0)
    def _():
        for copy in copies:
            copy.start()
        width = pieces[0].shape[1]
        for shift, piece in enumerate(pieces):
            owner = (place_ref[0] + (len(pieces) - shift)) % len(pieces)
            prefix_ref[:, pl.ds(pl.multiple_of(owner * width, 128), width)] = piece[...]
        vp_ref[...] = full_prefix(prefix_ref[:, D:])
        row = lax.broadcasted_iota(jnp.int32, (D, HEADS * PAD), 0) >> HEAD_DIM_BITS
        col = lax.broadcasted_iota(jnp.int32, (D, HEADS * PAD), 1) >> PAD_BITS
        spread_ref[...] = jnp.where(row == col, 1.0, 0.0).astype(BF)
        bias_ref[...] = row_of(fc_b_ref)
        d_kp_ref[...] = jnp.zeros_like(d_kp_ref)
        d_vp_ref[...] = jnp.zeros_like(d_vp_ref)

    attend_args = (q_ref, k_ref, v_ref, prefix_ref, att_ref, pp_ref, lse_ref, step)

    @pl.when((step < QUADS) & long_row)
    def _():
        attend(*attend_args, list(range(slots // BLK)), True)

    @pl.when((step < QUADS) & jnp.logical_not(long_row))
    def _():
        def body(block, carry):
            attend(*attend_args, [block], False)
            return carry

        lax.fori_loop(0, slots // BLK, body, 0)

    @pl.when(step == QUADS)
    def _():
        for copy in copies:
            copy.wait()

    @pl.when(step >= QUADS)
    def _():
        first = pl.multiple_of((step - QUADS) * BLK, BLK)
        rows = pl.ds(first, BLK)
        live = live_column(bucket_ref, lens_ref, first, BLK, slots)
        attended = att_ref[rows, :]
        mid = x_ref[...].astype(F32) + dot_nn(attended, out_w_ref[...]) + row_of(out_b_ref)
        norm, inv = normalise(mid)
        norm_ref[...] = norm
        normed_ref[...] = (norm * row_of(gain_ref) + row_of(shift_ref)).astype(BF)
        grad_out_ref[...] = jnp.where(live, cot_ref[...].astype(F32), 0.0).astype(BF)
        acc_ref[...] = mid + row_of(proj_b_ref)
        d_acc_ref[...] = jnp.zeros_like(d_acc_ref)

        def opened(chunk):
            part = pl.ds(pl.multiple_of(chunk * CHUNK, CHUNK), CHUNK)
            pre = dot_nn(normed_ref[...], fc_w_ref[:, part]) + bias_ref[:, part]
            return pre, dot_nt(grad_out_ref[...], proj_w_ref[part, :])

        def closed(chunk, pre, d_act):
            part = pl.ds(pl.multiple_of(chunk * CHUNK, CHUNK), CHUNK)
            act, slope = gelu_pair(pre)
            forth = dot_nn(act.astype(BF), proj_w_ref[part, :])
            back = dot_nt((d_act * slope).astype(BF), fc_w_ref[:, part])
            return acc_ref[...] + forth, d_acc_ref[...] + back

        def chunk_step(chunk, carry):
            pre, d_act = pre_ref[...], d_act_ref[...]
            next_pre, next_d_act = opened(chunk + 1)
            acc_ref[...], d_acc_ref[...] = closed(chunk, pre, d_act)
            pre_ref[...], d_act_ref[...] = next_pre, next_d_act
            return carry

        chunks = FF // CHUNK
        pre_ref[...], d_act_ref[...] = opened(0)
        lax.fori_loop(0, chunks - 1, chunk_step, 0, unroll=True)
        result, d_normed = closed(chunks - 1, pre_ref[...], d_act_ref[...])
        block_ref[...] = jnp.where(live, result, 0.0).astype(BF)
        d_mid = grad_out_ref[...].astype(F32) + norm_back(d_normed * row_of(gain_ref), norm_ref[...], inv)
        d_mid_ref[...] = d_mid
        d_att = dot_nt(d_mid.astype(BF), out_w_ref[...]).astype(BF)
        d_att_ref[...] = d_att
        product = (d_att.astype(F32) * attended.astype(F32)).astype(BF)
        delta = dot_nn(product, spread_ref[...])
        probs = pp_ref[rows, :]
        d_sp = (probs.astype(F32) * (dot_nt(d_att, vp_ref[...]) - delta)).astype(BF)
        d_sp_ref[...] = d_sp
        d_kp_ref[...] += dot_tn(d_sp, q_rows_ref[...])
        d_vp_ref[...] += dot_tn(probs, d_att)
        lse_t_ref[...] = lse_ref[rows, :].T
        delta_t_ref[...] = delta.T

    @pl.when(step == pl.num_programs(0) - 1)
    def _():
        shape = (HEADS * PAD, D)
        own = (
            lax.broadcasted_iota(jnp.int32, shape, 0) >> PAD_BITS
            == lax.broadcasted_iota(jnp.int32, shape, 1) >> HEAD_DIM_BITS
        )
        for index, ref in enumerate((d_kp_ref, d_vp_ref)):
            kept = jnp.where(own, ref[...], 0.0)
            total = kept[0:PAD, :]
            for head in range(1, HEADS):
                total = total + kept[head * PAD : (head + 1) * PAD, :]
            row_ref[:, index * D : (index + 1) * D] = total.astype(BF)
        sends = [
            pltpu.make_async_copy(row_ref, prefix_rows_hbm.at[place], row_sem)
            for place in range(prefix_rows_hbm.shape[0])
        ]
        for send in sends:
            send.start()
        for send in sends:
            send.wait()


def attend_back(
    q_ref, k_ref, v_ref, do_ref, pk_ref, dsp_ref, lse_ref, delta_ref, mix_ref, cols, pair, query_blocks, long_row
):
    causal = lax.broadcasted_iota(jnp.int32, (BLK, BLK), 0) <= lax.broadcasted_iota(jnp.int32, (BLK, BLK), 1)
    left = head_mask((BLK, 128), 0)
    row = lax.broadcasted_iota(jnp.int32, (128, 128), 0) >> PAD_BITS
    col = lax.broadcasted_iota(jnp.int32, (128, 128), 1) >> HEAD_DIM_BITS
    tiled = jnp.concatenate([pk_ref[...]] * 8, axis=0)
    prefix_keys = jnp.where(row == col + 2 * (pair % 4), tiled, jnp.zeros_like(tiled))

    def opened(block, side):
        rows, keys = block_rows(block), key_rows(block, long_row)
        mask = head_mask((BLK, 128), side)
        queries, d_out = q_ref[rows, :], do_ref[rows, :]
        raw = dot_nt(k_ref[keys, :], jnp.where(mask, queries, jnp.zeros_like(queries)))
        d_prob = dot_nt(v_ref[keys, :], jnp.where(mask, d_out, jnp.zeros_like(d_out)))
        own = jnp.where(causal, raw[-BLK:], masked_score)
        return (own if raw.shape[0] == BLK else jnp.concatenate([raw[:-BLK], own], axis=0)), d_prob

    units = [(block, side) for block in query_blocks for side in range(2)]
    ahead = 2
    queue = [opened(*unit) for unit in units[:ahead]]
    d_keys = [[None] * len(query_blocks) for _ in range(2)]
    d_vals = [[None] * len(query_blocks) for _ in range(2)]
    d_queries = [None, None]
    for index, (block, side) in enumerate(units):
        if index + ahead < len(units):
            queue.append(opened(*units[index + ahead]))
        score, d_prob = queue[index]
        queue[index] = None
        rows, keys = block_rows(block), key_rows(block, long_row)
        stat = slice(side * PAD, side * PAD + 1)
        prob = jnp.exp(score - lse_ref[stat, rows])
        d_score = (prob * (d_prob - delta_ref[stat, rows])).astype(BF)
        d_queries[side] = dot_tn(d_score, k_ref[keys, :])
        d_key = dot_nn(d_score, q_ref[rows, :])
        d_val = dot_nn(prob.astype(BF), do_ref[rows, :])
        for place in range(d_key.shape[0] // BLK):
            part = slice(place * BLK, (place + 1) * BLK)
            for sums, value in ((d_keys, d_key), (d_vals, d_val)):
                so_far = sums[side][place]
                sums[side][place] = value[part] if so_far is None else so_far + value[part]
        if side == 1:
            d_query = jnp.where(left, d_queries[0], d_queries[1]) + dot_nn(dsp_ref[rows, :], prefix_keys)
            mix_ref[0, rows, cols] = (d_query * HEAD_DIM**-0.5).astype(BF)
    for place, block in enumerate(query_blocks):
        rows = block_rows(block)
        mix_ref[1, rows, cols] = jnp.where(left, d_keys[0][place], d_keys[1][place]).astype(BF)
        mix_ref[2, rows, cols] = jnp.where(left, d_vals[0][place], d_vals[1][place]).astype(BF)


def attend_back_pair(bucket_ref, refs, mix_ref, cols, pair, here):
    blocks = refs[0].shape[0] // BLK
    long_row = bucket_ref[0] == refs[0].shape[0]
    args = (*refs, mix_ref, cols, pair)

    @pl.when(here & long_row)
    def _():
        attend_back(*args, list(range(blocks)), True)

    @pl.when(here & jnp.logical_not(long_row))
    def _():
        def body(block, carry):
            attend_back(*args, [block], False)
            return carry

        lax.fori_loop(0, blocks, body, 0)


def early_back_kernel(bucket_ref, *refs):
    *refs, mix_ref = refs
    step = pl.program_id(0)
    attend_back_pair(bucket_ref, refs, mix_ref, slice(0, 128), step, step >= 0)


def backward_kernel(bucket_ref, *refs):
    refs, (early_ref, x_ref, d_mid_ref, gain_ref, w_hbm, grad_ref, mix_ref, w_ref, sem) = refs[:8], refs[8:]
    step = pl.program_id(0)
    pairs = mix_ref.shape[2] // 128
    copy = pltpu.make_async_copy(w_hbm, w_ref, sem)

    @pl.when(step == 0)
    def _():
        copy.start()

    cols = pl.ds(pl.multiple_of(jnp.minimum(step, pairs - 1) * 128, 128), 128)
    attend_back_pair(bucket_ref, refs, mix_ref, cols, step + (HEADS // 2 - pairs), step < pairs)

    @pl.when(step == pairs)
    def _():
        copy.wait()

    @pl.when(step >= pairs)
    def _():
        rows = block_rows(step - pairs)
        d_mixed = jnp.concatenate(
            [part for third in range(3) for part in (early_ref[third], mix_ref[third, rows, :])], axis=1
        )
        d_normed = dot_nt(d_mixed, w_ref[...])
        norm, inv = normalise(x_ref[...].astype(F32))
        back = norm_back(d_normed * row_of(gain_ref), norm, inv)
        grad_ref[...] = (d_mid_ref[...] + back).astype(BF)


def summed_in_order(place, pieces, ordered_ref):
    for shift, piece in enumerate(pieces):
        ordered_ref[(place + (len(pieces) - shift)) % len(pieces)] = piece[...]
    total = ordered_ref[0].astype(F32)
    for owner in range(1, len(pieces)):
        total = total + ordered_ref[owner].astype(F32)
    return total


def tail_kernel(place_ref, tanh_ref, embed_ref, in_w_ref, *refs):
    count = (len(refs) - 9) // 2
    weights, pieces = refs[:count], refs[count : 2 * count]
    (
        embed_grad_ref, in_grad_ref, in_bias_ref, out_grad_ref, out_bias_ref,
        pad_ref, ordered_ref, sum_ref, parts_ref,
    ) = refs[2 * count :]
    tanh_pre = tanh_ref[...]
    sum_ref[...] = summed_in_order(place_ref[0], pieces, ordered_ref).astype(BF)
    width = out_grad_ref.shape[1]
    for shift, weight in enumerate(weights):
        owner = (place_ref[0] + (count - shift)) % count
        own_cols = sum_ref[:, pl.ds(pl.multiple_of(owner * width, 128), width)]
        parts_ref[owner] = dot_nt(own_cols, weight[...])
        if shift == 0:
            out_grad_ref[...] = dot_tn(tanh_pre.astype(BF), own_cols)
            out_bias_ref[...] = jnp.sum(own_cols.astype(F32), axis=0, keepdims=True)
    d_hidden = parts_ref[0]
    for owner in range(1, count):
        d_hidden = d_hidden + parts_ref[owner]
    d_pre = (d_hidden * (1.0 - tanh_pre * tanh_pre)).astype(BF)
    in_grad_ref[...] = dot_tn(padded_embed(embed_ref, pad_ref), d_pre)
    in_bias_ref[...] = jnp.sum(d_pre.astype(F32), axis=0, keepdims=True)
    embed_grad_ref[...] = dot_nt(d_pre, in_w_ref[...])[0:PREFIX]


SMEM = pl.BlockSpec(memory_space=pltpu.SMEM)
ANY = pl.BlockSpec(memory_space=pl.ANY)


def params(mib):
    return pltpu.CompilerParams(vmem_limit_bytes=mib * 2**20, dimension_semantics=("arbitrary",))


def cost(flops, moved):
    return pl.CostEstimate(flops=int(flops), bytes_accessed=int(moved), transcendentals=0)


def shape(dims, dtype):
    return jax.ShapeDtypeStruct(dims, dtype)


def whole(array):
    return pl.BlockSpec(array.shape, lambda g: (0,) * len(array.shape))


def to_all(value, axis):
    size = lax.axis_size(axis)
    return [value] + [
        lax.ppermute(value, axis, [(place, (place + shift) % size) for place in range(size)])
        for shift in range(1, size)
    ]


def local(
    tokens, ln1_gain, ln1_shift, qkv_weight, qkv_bias, out_weight, out_bias, ln2_gain, ln2_shift, fc_weight,
    fc_bias, proj_weight, proj_bias, prefix_embed, reparam_in, reparam_in_bias, reparam_out, reparam_out_bias,
    bucket, seg_lens, cotangent,
):
    x, cot = tokens[0], cotangent[0]
    slots = x.shape[0]
    blocks = slots // BLK
    own_width = reparam_out.shape[1]
    hidden_width = reparam_in.shape[1]
    rep_place = lax.axis_index("rep").astype(jnp.int32)[None]

    reparam_args = (prefix_embed, reparam_in, reparam_in_bias, reparam_out, reparam_out_bias)
    reparam_outs = (shape((PAD, hidden_width), F32), shape((PAD, own_width), BF))
    tanh_pre, own_kv = pl.pallas_call(
        reparam_kernel,
        grid=(1,),
        out_shape=reparam_outs,
        in_specs=[whole(arg) for arg in reparam_args],
        out_specs=tuple(whole(out) for out in reparam_outs),
        scratch_shapes=[pltpu.VMEM((PAD, D), F32)],
        compiler_params=params(60),
        name="reparam",
    )(*reparam_args)
    prefix_pieces = to_all(own_kv, "rep")

    mixed = pl.pallas_call(
        project_kernel,
        grid=(3,),
        out_shape=shape((slots, 3 * D), BF),
        in_specs=[
            whole(x), whole(ln1_gain), whole(ln1_shift),
            pl.BlockSpec((D,), lambda n: (n,)),
            pl.BlockSpec((D, D), lambda n: (0, n)),
        ],
        out_specs=pl.BlockSpec((slots, D), lambda n: (0, n)),
        scratch_shapes=[pltpu.VMEM((slots, D), BF)],
        compiler_params=params(60),
        cost_estimate=cost(6 * slots * D * D, 16 * 2**20),
        name="project",
    )(x, ln1_gain, ln1_shift, qkv_bias, qkv_weight)
    def quad_at(offset):
        return pl.BlockSpec((slots, QUAD), lambda g: (0, offset + jnp.minimum(g, QUADS - 1)))

    def block_of(width):
        return pl.BlockSpec((BLK, width), lambda g: (jnp.maximum(g - QUADS, 0), 0))

    lanes = HEADS * PAD
    block_t = pl.BlockSpec((lanes, BLK), lambda g: (0, jnp.maximum(g - QUADS, 0)))
    vectors = (out_bias, ln2_gain, ln2_shift, fc_bias, proj_bias)
    prefix_shape = shape((PAD, 2 * D), BF)
    block_out, d_mid, d_att, d_sp, lse_t, delta_t, prefix_rows, prefix_kv = pl.pallas_call(
        forward_kernel,
        grid=(QUADS + blocks,),
        out_shape=(
            shape((slots, D), BF),
            shape((slots, D), F32),
            shape((slots, D), BF),
            shape((slots, lanes), BF),
            shape((lanes, slots), F32),
            shape((lanes, slots), F32),
            shape((lax.axis_size("batch"), *prefix_shape.shape), BF),
            prefix_shape,
        ),
        in_specs=[
            SMEM, SMEM, SMEM, quad_at(0), quad_at(QUADS), quad_at(2 * QUADS),
            block_of(D), block_of(D), block_of(D),
            *[whole(vector) for vector in vectors], ANY, ANY, ANY, *[whole(piece) for piece in prefix_pieces],
        ],
        out_specs=(
            block_of(D), block_of(D), block_of(D), block_of(lanes), block_t, block_t,
            ANY, whole(prefix_shape),
        ),
        scratch_shapes=[
            pltpu.VMEM((slots, D), BF),
            pltpu.VMEM((slots, lanes), BF),
            pltpu.VMEM((slots, lanes), F32),
            pltpu.VMEM((D, D), BF),
            pltpu.VMEM((D, FF), BF),
            pltpu.VMEM((FF, D), BF),
            pltpu.VMEM((BLK, D), F32),
            pltpu.VMEM((BLK, D), BF),
            pltpu.VMEM((BLK, D), BF),
            pltpu.VMEM((BLK, D), F32),
            pltpu.VMEM((BLK, D), F32),
            pltpu.VMEM((BLK, CHUNK), F32),
            pltpu.VMEM((BLK, CHUNK), F32),
            pltpu.VMEM((1, FF), F32),
            pltpu.VMEM((lanes, D), BF),
            pltpu.VMEM((D, lanes), BF),
            pltpu.VMEM((lanes, D), F32),
            pltpu.VMEM((lanes, D), F32),
            pltpu.VMEM(prefix_shape.shape, BF),
            pltpu.SemaphoreType.DMA((3,)),
            pltpu.SemaphoreType.DMA,
        ],
        compiler_params=params(56),
        cost_estimate=cost(50e9, 40 * 2**20),
        name="forward",
    )(
        rep_place, bucket, seg_lens, mixed, mixed, mixed, x, cot, mixed, *vectors,
        out_weight, fc_weight, proj_weight, *prefix_pieces,
    )

    late_weight, _ = lax.optimization_barrier((reparam_out, prefix_rows))
    weight_pieces = to_all(late_weight, "rep")
    batch_rows = lax.all_to_all(prefix_rows, "batch", split_axis=0, concat_axis=0, tiled=True)

    pairs = HEADS // 2
    early = EARLY_PAIRS

    def back_specs(start, count):
        def pair_of(g):
            return start + jnp.minimum(g, count - 1)

        def pair_at(offset):
            return pl.BlockSpec((slots, 128), lambda g: (0, offset + pair_of(g)))

        stat_spec = pl.BlockSpec((2 * PAD, slots), lambda g: (pair_of(g), 0))
        return [
            SMEM,
            pair_at(0), pair_at(pairs), pair_at(2 * pairs), pair_at(0),
            pl.BlockSpec((PAD, 128), lambda g: (0, pair_of(g))),
            pl.BlockSpec((slots, 128), lambda g: (0, pair_of(g) // 4)),
            stat_spec, stat_spec,
        ]

    back_args = (bucket, mixed, mixed, mixed, d_att, prefix_kv, d_sp, lse_t, delta_t)
    d_mixed = pl.pallas_call(
        early_back_kernel,
        grid=(early,),
        out_shape=shape((3, slots, early * 128), BF),
        in_specs=back_specs(0, early),
        out_specs=pl.BlockSpec((3, slots, 128), lambda g: (0, 0, g)),
        compiler_params=params(60),
        cost_estimate=cost(14e9, 10 * 2**20),
        name="early_back",
    )(*back_args)

    group_sum = jnp.sum(batch_rows.astype(F32), axis=0).astype(BF)
    rep_pieces = to_all(group_sum, "rep")

    late = pairs - early
    late_rows = pl.BlockSpec((BLK, D), lambda g: (jnp.maximum(g - late, 0), 0))
    tokens_grad = pl.pallas_call(
        backward_kernel,
        grid=(late + blocks,),
        out_shape=shape((slots, D), BF),
        in_specs=[
            *back_specs(early, late),
            pl.BlockSpec((3, BLK, early * 128), lambda g: (0, jnp.maximum(g - late, 0), 0)),
            late_rows, late_rows, whole(ln1_gain), ANY,
        ],
        out_specs=late_rows,
        scratch_shapes=[
            pltpu.VMEM((3, slots, late * 128), BF),
            pltpu.VMEM((D, 3 * D), BF),
            pltpu.SemaphoreType.DMA,
        ],
        compiler_params=params(60),
        cost_estimate=cost(24e9, 30 * 2**20),
        name="backward",
    )(*back_args, d_mixed, x, d_mid, ln1_gain, qkv_weight)

    tail_args = (tanh_pre, prefix_embed, reparam_in, *weight_pieces, *rep_pieces)
    tail_outs = (
        shape((PREFIX, D), F32),
        shape((D, hidden_width), F32),
        shape((1, hidden_width), F32),
        shape((hidden_width, own_width), F32),
        shape((1, own_width), F32),
    )
    embed_grad, in_grad, in_bias_grad, out_grad, out_bias_grad = pl.pallas_call(
        tail_kernel,
        grid=(1,),
        out_shape=tail_outs,
        in_specs=[SMEM] + [whole(arg) for arg in tail_args],
        out_specs=tuple(whole(out) for out in tail_outs),
        scratch_shapes=[
            pltpu.VMEM((PAD, D), F32),
            pltpu.VMEM((len(rep_pieces), *prefix_shape.shape), BF),
            pltpu.VMEM(prefix_shape.shape, BF),
            pltpu.VMEM((len(rep_pieces), PAD, hidden_width), F32),
        ],
        compiler_params=params(16),
        name="tail",
    )(rep_place, *tail_args)
    return (
        block_out[None],
        tokens_grad[None],
        embed_grad,
        in_grad,
        in_bias_grad[0],
        out_grad,
        out_bias_grad[0],
    )


def solution(mesh):
    row = P(("batch", "rep"), None, None)
    placed = (row, *[P()] * 15, P(None, "rep"), P("rep"), P(("batch", "rep")), P(("batch", "rep"), None), row)
    return jax.shard_map(
        local,
        mesh=mesh,
        in_specs=placed,
        out_specs=(row, row, P(), P(), P(), P(None, "rep"), P("rep")),
        check_vma=False,
    )
```

```python
import jax
import jax.numpy as jnp
from jax import lax
from jax.experimental import pallas as pl
from jax.experimental.pallas import tpu as pltpu
from jax.sharding import PartitionSpec as P

D = 1024
HEADS = 16
HEAD_DIM = 64
FF = 4096
PREFIX = 10
PAD = 16
SHORT = 256
PAD_BITS, HEAD_DIM_BITS, SHORT_BITS = 4, 6, 8
BLK = 256
QUAD = 4 * HEAD_DIM
QUADS = HEADS // 4
EARLY_PAIRS = 4
CHUNK = 1024

BF = jnp.bfloat16
F32 = jnp.float32
norm_eps = 1e-05
gelu_coef = 0.7978845608028654
gelu_cube = 0.044715
masked_score = -1e30


def dot_nn(left, right):
    return jnp.dot(left, right, preferred_element_type=F32)


def dot_nt(left, right):
    return lax.dot_general(left, right, (((1,), (1,)), ((), ())), preferred_element_type=F32)


def dot_tn(left, right):
    return lax.dot_general(left, right, (((0,), (0,)), ((), ())), preferred_element_type=F32)


def normalise(values):
    row_mean = jnp.mean(values, axis=-1, keepdims=True)
    centred = values - row_mean
    variance = jnp.mean(centred * centred, axis=-1, keepdims=True)
    inv = lax.rsqrt(variance + norm_eps)
    return centred * inv, inv


def norm_back(grad, norm, inv):
    along = jnp.mean(grad * norm, axis=-1, keepdims=True)
    return (grad - jnp.mean(grad, axis=-1, keepdims=True) - norm * along) * inv


def gelu_pair(u):
    sq = u * u
    w = jnp.tanh(u * (gelu_coef + (gelu_coef * gelu_cube) * sq))
    a = 0.5 * w + 0.5
    slope = a * (1.0 + u * (1.0 - a) * (2.0 * gelu_coef + (6.0 * gelu_coef * gelu_cube) * sq))
    return u * a, slope


def head_mask(shape, head):
    lane = lax.broadcasted_iota(jnp.int32, shape, 1)
    return (lane < HEAD_DIM) if head % 2 == 0 else (lane >= HEAD_DIM)


def quad_prefix(prefix, quad):
    row = lax.broadcasted_iota(jnp.int32, (128, QUAD), 0) >> PAD_BITS
    col = lax.broadcasted_iota(jnp.int32, (128, QUAD), 1) >> HEAD_DIM_BITS
    tiled = jnp.concatenate([prefix] * 8, axis=0)
    return jnp.where(row == col + 4 * (quad % 2), tiled, jnp.zeros_like(tiled))


def full_prefix(prefix):
    shape = (HEADS * PAD, D)
    row = lax.broadcasted_iota(jnp.int32, shape, 0) >> PAD_BITS
    col = lax.broadcasted_iota(jnp.int32, shape, 1) >> HEAD_DIM_BITS
    tiled = jnp.concatenate([prefix] * HEADS, axis=0)
    return jnp.where(row == col, tiled, jnp.zeros_like(tiled))


def row_of(ref, first=0, size=None):
    size = ref.shape[0] if size is None else size
    return ref[first : first + size].astype(F32)[None, :]


def padded_embed(embed_ref, pad_ref):
    pad_ref[...] = jnp.zeros_like(pad_ref)
    pad_ref[0:PREFIX, :] = embed_ref[...].astype(F32)
    return pad_ref[...].astype(BF)


def reparam_kernel(embed_ref, in_w_ref, in_b_ref, out_w_ref, out_b_ref, tanh_ref, kv_ref, pad_ref):
    tanh_pre = jnp.tanh(dot_nn(padded_embed(embed_ref, pad_ref), in_w_ref[...]) + row_of(in_b_ref))
    tanh_ref[...] = tanh_pre
    kv_ref[...] = (dot_nn(tanh_pre.astype(BF), out_w_ref[...]) + row_of(out_b_ref)).astype(BF)


def project_kernel(x_ref, gain_ref, shift_ref, bias_ref, w_ref, out_ref, normed_ref):
    step = pl.program_id(0)
    slots = x_ref.shape[0]
    factor = jnp.where(step == 0, HEAD_DIM**-0.5, 1.0)

    def norm_part(first):
        norm, _ = normalise(x_ref[first : first + BLK, :].astype(F32))
        normed_ref[first : first + BLK, :] = (norm * row_of(gain_ref) + row_of(shift_ref)).astype(BF)

    def dot_part(first, count):
        rows = pl.ds(first, count)
        mixed = dot_nn(normed_ref[rows, :], w_ref[...]) + row_of(bias_ref)
        out_ref[rows, :] = (mixed.astype(BF).astype(F32) * factor).astype(BF)

    @pl.when(step == 0)
    def _():
        norm_part(0)
        for first in range(0, slots, BLK):
            if first + BLK < slots:
                norm_part(first + BLK)
            dot_part(first, BLK)

    @pl.when(step > 0)
    def _():
        def body(index, carry):
            dot_part(pl.multiple_of(index * 2 * BLK, 2 * BLK), 2 * BLK)
            return carry

        lax.fori_loop(0, slots // (2 * BLK), body, 0)


def live_column(bucket_ref, lens_ref, first, rows, slots):
    position = lax.broadcasted_iota(jnp.int32, (rows, 1), 0) + first
    segment = position >> SHORT_BITS
    total = jnp.int32(0)
    short_len = jnp.zeros((rows, 1), jnp.int32)
    for index in range(slots // SHORT):
        total = total + lens_ref[0, index]
        short_len = jnp.where(segment == index, lens_ref[0, index], short_len)
    return position < jnp.where(bucket_ref[0] == slots, total, segment * SHORT + short_len)


def block_rows(block):
    return pl.ds(block * BLK if isinstance(block, int) else pl.multiple_of(block * BLK, BLK), BLK)


def key_rows(block, long_row):
    return pl.ds(0, (block + 1) * BLK) if long_row else block_rows(block)


def attend(q_ref, k_ref, v_ref, prefix_ref, att_ref, pp_ref, lse_ref, quad, query_blocks, long_row):
    cols = pl.ds(pl.multiple_of(quad * QUAD, QUAD), QUAD)
    pair_cols = pl.ds(pl.multiple_of((quad // 2) * 128, 128), 128)
    prefix_keys = quad_prefix(prefix_ref[:, cols], quad)
    prefix_vals = quad_prefix(prefix_ref[:, pl.ds(pl.multiple_of(D + quad * QUAD, QUAD), QUAD)], quad)
    causal = lax.broadcasted_iota(jnp.int32, (BLK, BLK), 1) <= lax.broadcasted_iota(jnp.int32, (BLK, BLK), 0)
    lane = lax.broadcasted_iota(jnp.int32, (BLK, 128), 1)
    lane_head = (lane >> PAD_BITS) - 4 * (quad % 2)
    lane_real = (lane & (PAD - 1)) < PREFIX

    def scores(block, head):
        pair = slice(128 * (head // 2), 128 * (head // 2) + 128)
        queries = q_ref[block_rows(block), pair]
        queries = jnp.where(head_mask((BLK, 128), head), queries, jnp.zeros_like(queries))
        raw = dot_nt(queries, k_ref[key_rows(block, long_row), pair])
        own = jnp.where(causal, raw[:, -BLK:], masked_score)
        return own if raw.shape[1] == BLK else jnp.concatenate([raw[:, :-BLK], own], axis=1)

    units = [(block, head) for block in query_blocks for head in range(4)]
    ahead = 1
    queue = [scores(*unit) for unit in units[:ahead]]
    for index, (block, head) in enumerate(units):
        if index + ahead < len(units):
            queue.append(scores(*units[index + ahead]))
        rows = block_rows(block)
        if head == 0:
            prefix_raw = dot_nt(q_ref[rows, :], prefix_keys)
            probs_quad = jnp.zeros((BLK, 128), F32)
            lse_quad = jnp.zeros((BLK, 128), F32)
            outs = []
        pair = slice(128 * (head // 2), 128 * (head // 2) + 128)
        count = queue[index].shape[1]
        prefix_scores = jnp.where((lane_head == head) & lane_real, prefix_raw, masked_score)
        score = jnp.concatenate([queue[index], prefix_scores], axis=1)
        queue[index] = None
        peak = jnp.max(score, axis=1, keepdims=True)
        raised = jnp.exp(score - peak)
        summed = jnp.sum(raised, axis=1, keepdims=True)
        inv = 1.0 / summed
        outs.append(dot_nn(raised[:, :count].astype(BF), v_ref[key_rows(block, long_row), pair]) * inv)
        probs_quad = probs_quad + raised[:, count:] * inv
        lse_quad = jnp.where(lane_head == head, peak + jnp.log(summed), lse_quad)
        if head == 3:
            probs_low = probs_quad.astype(BF)
            left = head_mask((BLK, 128), 0)
            merged = jnp.concatenate(
                [jnp.where(left, outs[0], outs[1]), jnp.where(left, outs[2], outs[3])], axis=1
            ) + dot_nn(probs_low, prefix_vals)
            att_ref[rows, cols] = merged.astype(BF)

            @pl.when(quad % 2 == 0)
            def _():
                pp_ref[rows, pair_cols] = probs_low
                lse_ref[rows, pair_cols] = lse_quad

            @pl.when(quad % 2 == 1)
            def _():
                pp_ref[rows, pair_cols] = pp_ref[rows, pair_cols] + probs_low
                lse_ref[rows, pair_cols] = lse_ref[rows, pair_cols] + lse_quad


def forward_kernel(
    place_ref, bucket_ref, lens_ref, q_ref, k_ref, v_ref, x_ref, cot_ref, q_rows_ref,
    out_b_ref, gain_ref, shift_ref, fc_b_ref, proj_b_ref, out_w_hbm, fc_w_hbm, proj_w_hbm, *refs,
):
    pieces, refs = refs[: len(refs) - 29], refs[len(refs) - 29 :]
    (
        block_ref, d_mid_ref, d_att_ref, d_sp_ref, lse_t_ref, delta_t_ref, prefix_rows_hbm, prefix_ref,
        att_ref, pp_ref, lse_ref, out_w_ref, fc_w_ref, proj_w_ref, norm_ref, normed_ref, grad_out_ref,
        acc_ref, d_acc_ref, pre_ref, d_act_ref, bias_ref, vp_ref, spread_ref, d_kp_ref, d_vp_ref, row_ref, sems, row_sem,
    ) = refs
    step = pl.program_id(0)
    slots = q_ref.shape[0]
    copies = [
        pltpu.make_async_copy(out_w_hbm, out_w_ref, sems.at[0]),
        pltpu.make_async_copy(fc_w_hbm, fc_w_ref, sems.at[1]),
        pltpu.make_async_copy(proj_w_hbm, proj_w_ref, sems.at[2]),
    ]
    long_row = bucket_ref[0] == slots

    @pl.when(step == 0)
    def _():
        for copy in copies:
            copy.start()
        width = pieces[0].shape[1]
        for shift, piece in enumerate(pieces):
            owner = (place_ref[0] + (len(pieces) - shift)) % len(pieces)
            prefix_ref[:, pl.ds(pl.multiple_of(owner * width, 128), width)] = piece[...]
        vp_ref[...] = full_prefix(prefix_ref[:, D:])
        row = lax.broadcasted_iota(jnp.int32, (D, HEADS * PAD), 0) >> HEAD_DIM_BITS
        col = lax.broadcasted_iota(jnp.int32, (D, HEADS * PAD), 1) >> PAD_BITS
        spread_ref[...] = jnp.where(row == col, 1.0, 0.0).astype(BF)
        bias_ref[...] = row_of(fc_b_ref)
        d_kp_ref[...] = jnp.zeros_like(d_kp_ref)
        d_vp_ref[...] = jnp.zeros_like(d_vp_ref)

    attend_args = (q_ref, k_ref, v_ref, prefix_ref, att_ref, pp_ref, lse_ref, step)

    @pl.when((step < QUADS) & long_row)
    def _():
        attend(*attend_args, list(range(slots // BLK)), True)

    @pl.when((step < QUADS) & jnp.logical_not(long_row))
    def _():
        def body(block, carry):
            attend(*attend_args, [block], False)
            return carry

        lax.fori_loop(0, slots // BLK, body, 0)

    @pl.when(step == QUADS)
    def _():
        for copy in copies:
            copy.wait()

    @pl.when(step >= QUADS)
    def _():
        first = pl.multiple_of((step - QUADS) * BLK, BLK)
        rows = pl.ds(first, BLK)
        live = live_column(bucket_ref, lens_ref, first, BLK, slots)
        attended = att_ref[rows, :]
        mid = x_ref[...].astype(F32) + dot_nn(attended, out_w_ref[...]) + row_of(out_b_ref)
        norm, inv = normalise(mid)
        norm_ref[...] = norm
        normed_ref[...] = (norm * row_of(gain_ref) + row_of(shift_ref)).astype(BF)
        grad_out_ref[...] = jnp.where(live, cot_ref[...].astype(F32), 0.0).astype(BF)
        acc_ref[...] = mid + row_of(proj_b_ref)
        d_acc_ref[...] = jnp.zeros_like(d_acc_ref)

        def opened(chunk):
            part = pl.ds(pl.multiple_of(chunk * CHUNK, CHUNK), CHUNK)
            pre = dot_nn(normed_ref[...], fc_w_ref[:, part]) + bias_ref[:, part]
            return pre, dot_nt(grad_out_ref[...], proj_w_ref[part, :])

        def closed(chunk, pre, d_act):
            part = pl.ds(pl.multiple_of(chunk * CHUNK, CHUNK), CHUNK)
            act, slope = gelu_pair(pre)
            forth = dot_nn(act.astype(BF), proj_w_ref[part, :])
            back = dot_nt((d_act * slope).astype(BF), fc_w_ref[:, part])
            return acc_ref[...] + forth, d_acc_ref[...] + back

        def chunk_step(chunk, carry):
            pre, d_act = pre_ref[...], d_act_ref[...]
            next_pre, next_d_act = opened(chunk + 1)
            acc_ref[...], d_acc_ref[...] = closed(chunk, pre, d_act)
            pre_ref[...], d_act_ref[...] = next_pre, next_d_act
            return carry

        chunks = FF // CHUNK
        pre_ref[...], d_act_ref[...] = opened(0)
        lax.fori_loop(0, chunks - 1, chunk_step, 0, unroll=True)
        result, d_normed = closed(chunks - 1, pre_ref[...], d_act_ref[...])
        block_ref[...] = jnp.where(live, result, 0.0).astype(BF)
        d_mid = grad_out_ref[...].astype(F32) + norm_back(d_normed * row_of(gain_ref), norm_ref[...], inv)
        d_mid_ref[...] = d_mid
        d_att = dot_nt(d_mid.astype(BF), out_w_ref[...]).astype(BF)
        d_att_ref[...] = d_att
        product = (d_att.astype(F32) * attended.astype(F32)).astype(BF)
        delta = dot_nn(product, spread_ref[...])
        probs = pp_ref[rows, :]
        d_sp = (probs.astype(F32) * (dot_nt(d_att, vp_ref[...]) - delta)).astype(BF)
        d_sp_ref[...] = d_sp
        d_kp_ref[...] += dot_tn(d_sp, q_rows_ref[...])
        d_vp_ref[...] += dot_tn(probs, d_att)
        lse_t_ref[...] = lse_ref[rows, :].T
        delta_t_ref[...] = delta.T

    @pl.when(step == pl.num_programs(0) - 1)
    def _():
        shape = (HEADS * PAD, D)
        own = (
            lax.broadcasted_iota(jnp.int32, shape, 0) >> PAD_BITS
            == lax.broadcasted_iota(jnp.int32, shape, 1) >> HEAD_DIM_BITS
        )
        for index, ref in enumerate((d_kp_ref, d_vp_ref)):
            kept = jnp.where(own, ref[...], 0.0)
            total = kept[0:PAD, :]
            for head in range(1, HEADS):
                total = total + kept[head * PAD : (head + 1) * PAD, :]
            row_ref[:, index * D : (index + 1) * D] = total.astype(BF)
        sends = [
            pltpu.make_async_copy(row_ref, prefix_rows_hbm.at[place], row_sem)
            for place in range(prefix_rows_hbm.shape[0])
        ]
        for send in sends:
            send.start()
        for send in sends:
            send.wait()


def attend_back(
    q_ref, k_ref, v_ref, do_ref, pk_ref, dsp_ref, lse_ref, delta_ref, mix_ref, cols, pair, query_blocks, long_row
):
    causal = lax.broadcasted_iota(jnp.int32, (BLK, BLK), 0) <= lax.broadcasted_iota(jnp.int32, (BLK, BLK), 1)
    left = head_mask((BLK, 128), 0)
    row = lax.broadcasted_iota(jnp.int32, (128, 128), 0) >> PAD_BITS
    col = lax.broadcasted_iota(jnp.int32, (128, 128), 1) >> HEAD_DIM_BITS
    tiled = jnp.concatenate([pk_ref[...]] * 8, axis=0)
    prefix_keys = jnp.where(row == col + 2 * (pair % 4), tiled, jnp.zeros_like(tiled))

    def opened(block, side):
        rows, keys = block_rows(block), key_rows(block, long_row)
        mask = head_mask((BLK, 128), side)
        queries, d_out = q_ref[rows, :], do_ref[rows, :]
        raw = dot_nt(k_ref[keys, :], jnp.where(mask, queries, jnp.zeros_like(queries)))
        d_prob = dot_nt(v_ref[keys, :], jnp.where(mask, d_out, jnp.zeros_like(d_out)))
        own = jnp.where(causal, raw[-BLK:], masked_score)
        return (own if raw.shape[0] == BLK else jnp.concatenate([raw[:-BLK], own], axis=0)), d_prob

    units = [(block, side) for block in query_blocks for side in range(2)]
    ahead = 2
    queue = [opened(*unit) for unit in units[:ahead]]
    d_keys = [[None] * len(query_blocks) for _ in range(2)]
    d_vals = [[None] * len(query_blocks) for _ in range(2)]
    d_queries = [None, None]
    for index, (block, side) in enumerate(units):
        if index + ahead < len(units):
            queue.append(opened(*units[index + ahead]))
        score, d_prob = queue[index]
        queue[index] = None
        rows, keys = block_rows(block), key_rows(block, long_row)
        stat = slice(side * PAD, side * PAD + 1)
        prob = jnp.exp(score - lse_ref[stat, rows])
        d_score = (prob * (d_prob - delta_ref[stat, rows])).astype(BF)
        d_queries[side] = dot_tn(d_score, k_ref[keys, :])
        d_key = dot_nn(d_score, q_ref[rows, :])
        d_val = dot_nn(prob.astype(BF), do_ref[rows, :])
        for place in range(d_key.shape[0] // BLK):
            part = slice(place * BLK, (place + 1) * BLK)
            for sums, value in ((d_keys, d_key), (d_vals, d_val)):
                so_far = sums[side][place]
                sums[side][place] = value[part] if so_far is None else so_far + value[part]
        if side == 1:
            d_query = jnp.where(left, d_queries[0], d_queries[1]) + dot_nn(dsp_ref[rows, :], prefix_keys)
            mix_ref[0, rows, cols] = (d_query * HEAD_DIM**-0.5).astype(BF)
    for place, block in enumerate(query_blocks):
        rows = block_rows(block)
        mix_ref[1, rows, cols] = jnp.where(left, d_keys[0][place], d_keys[1][place]).astype(BF)
        mix_ref[2, rows, cols] = jnp.where(left, d_vals[0][place], d_vals[1][place]).astype(BF)


def attend_back_pair(bucket_ref, refs, mix_ref, cols, pair, here):
    blocks = refs[0].shape[0] // BLK
    long_row = bucket_ref[0] == refs[0].shape[0]
    args = (*refs, mix_ref, cols, pair)

    @pl.when(here & long_row)
    def _():
        attend_back(*args, list(range(blocks)), True)

    @pl.when(here & jnp.logical_not(long_row))
    def _():
        def body(block, carry):
            attend_back(*args, [block], False)
            return carry

        lax.fori_loop(0, blocks, body, 0)


def early_back_kernel(bucket_ref, *refs):
    *refs, mix_ref = refs
    step = pl.program_id(0)
    attend_back_pair(bucket_ref, refs, mix_ref, slice(0, 128), step, step >= 0)


def backward_kernel(bucket_ref, *refs):
    refs, (early_ref, x_ref, d_mid_ref, gain_ref, w_hbm, grad_ref, mix_ref, w_ref, sem) = refs[:8], refs[8:]
    step = pl.program_id(0)
    pairs = mix_ref.shape[2] // 128
    copy = pltpu.make_async_copy(w_hbm, w_ref, sem)

    @pl.when(step == 0)
    def _():
        copy.start()

    cols = pl.ds(pl.multiple_of(jnp.minimum(step, pairs - 1) * 128, 128), 128)
    attend_back_pair(bucket_ref, refs, mix_ref, cols, step + (HEADS // 2 - pairs), step < pairs)

    @pl.when(step == pairs)
    def _():
        copy.wait()

    @pl.when(step >= pairs)
    def _():
        rows = block_rows(step - pairs)
        d_mixed = jnp.concatenate(
            [part for third in range(3) for part in (early_ref[third], mix_ref[third, rows, :])], axis=1
        )
        d_normed = dot_nt(d_mixed, w_ref[...])
        norm, inv = normalise(x_ref[...].astype(F32))
        back = norm_back(d_normed * row_of(gain_ref), norm, inv)
        grad_ref[...] = (d_mid_ref[...] + back).astype(BF)


def summed_in_order(place, pieces, ordered_ref):
    for shift, piece in enumerate(pieces):
        ordered_ref[(place + (len(pieces) - shift)) % len(pieces)] = piece[...]
    total = ordered_ref[0].astype(F32)
    for owner in range(1, len(pieces)):
        total = total + ordered_ref[owner].astype(F32)
    return total


def tail_kernel(place_ref, tanh_ref, embed_ref, in_w_ref, *refs):
    count = (len(refs) - 9) // 2
    weights, pieces = refs[:count], refs[count : 2 * count]
    (
        embed_grad_ref, in_grad_ref, in_bias_ref, out_grad_ref, out_bias_ref,
        pad_ref, ordered_ref, sum_ref, parts_ref,
    ) = refs[2 * count :]
    tanh_pre = tanh_ref[...]
    sum_ref[...] = summed_in_order(place_ref[0], pieces, ordered_ref).astype(BF)
    width = out_grad_ref.shape[1]
    for shift, weight in enumerate(weights):
        owner = (place_ref[0] + (count - shift)) % count
        own_cols = sum_ref[:, pl.ds(pl.multiple_of(owner * width, 128), width)]
        parts_ref[owner] = dot_nt(own_cols, weight[...])
        if shift == 0:
            out_grad_ref[...] = dot_tn(tanh_pre.astype(BF), own_cols)
            out_bias_ref[...] = jnp.sum(own_cols.astype(F32), axis=0, keepdims=True)
    d_hidden = parts_ref[0]
    for owner in range(1, count):
        d_hidden = d_hidden + parts_ref[owner]
    d_pre = (d_hidden * (1.0 - tanh_pre * tanh_pre)).astype(BF)
    in_grad_ref[...] = dot_tn(padded_embed(embed_ref, pad_ref), d_pre)
    in_bias_ref[...] = jnp.sum(d_pre.astype(F32), axis=0, keepdims=True)
    embed_grad_ref[...] = dot_nt(d_pre, in_w_ref[...])[0:PREFIX]


SMEM = pl.BlockSpec(memory_space=pltpu.SMEM)
ANY = pl.BlockSpec(memory_space=pl.ANY)


def params(mib):
    return pltpu.CompilerParams(vmem_limit_bytes=mib * 2**20, dimension_semantics=("arbitrary",))


def cost(flops, moved):
    return pl.CostEstimate(flops=int(flops), bytes_accessed=int(moved), transcendentals=0)


def shape(dims, dtype):
    return jax.ShapeDtypeStruct(dims, dtype)


def whole(array):
    return pl.BlockSpec(array.shape, lambda g: (0,) * len(array.shape))


def to_all(value, axis):
    size = lax.axis_size(axis)
    return [value] + [
        lax.ppermute(value, axis, [(place, (place + shift) % size) for place in range(size)])
        for shift in range(1, size)
    ]


def local(
    tokens, ln1_gain, ln1_shift, qkv_weight, qkv_bias, out_weight, out_bias, ln2_gain, ln2_shift, fc_weight,
    fc_bias, proj_weight, proj_bias, prefix_embed, reparam_in, reparam_in_bias, reparam_out, reparam_out_bias,
    bucket, seg_lens, cotangent,
):
    x, cot = tokens[0], cotangent[0]
    slots = x.shape[0]
    blocks = slots // BLK
    own_width = reparam_out.shape[1]
    hidden_width = reparam_in.shape[1]
    rep_place = lax.axis_index("rep").astype(jnp.int32)[None]

    reparam_args = (prefix_embed, reparam_in, reparam_in_bias, reparam_out, reparam_out_bias)
    reparam_outs = (shape((PAD, hidden_width), F32), shape((PAD, own_width), BF))
    tanh_pre, own_kv = pl.pallas_call(
        reparam_kernel,
        grid=(1,),
        out_shape=reparam_outs,
        in_specs=[whole(arg) for arg in reparam_args],
        out_specs=tuple(whole(out) for out in reparam_outs),
        scratch_shapes=[pltpu.VMEM((PAD, D), F32)],
        compiler_params=params(60),
        name="reparam",
    )(*reparam_args)
    prefix_pieces = to_all(own_kv, "rep")

    mixed = pl.pallas_call(
        project_kernel,
        grid=(3,),
        out_shape=shape((slots, 3 * D), BF),
        in_specs=[
            whole(x), whole(ln1_gain), whole(ln1_shift),
            pl.BlockSpec((D,), lambda n: (n,)),
            pl.BlockSpec((D, D), lambda n: (0, n)),
        ],
        out_specs=pl.BlockSpec((slots, D), lambda n: (0, n)),
        scratch_shapes=[pltpu.VMEM((slots, D), BF)],
        compiler_params=params(60),
        cost_estimate=cost(6 * slots * D * D, 16 * 2**20),
        name="project",
    )(x, ln1_gain, ln1_shift, qkv_bias, qkv_weight)
    def quad_at(offset):
        return pl.BlockSpec((slots, QUAD), lambda g: (0, offset + jnp.minimum(g, QUADS - 1)))

    def block_of(width):
        return pl.BlockSpec((BLK, width), lambda g: (jnp.maximum(g - QUADS, 0), 0))

    lanes = HEADS * PAD
    block_t = pl.BlockSpec((lanes, BLK), lambda g: (0, jnp.maximum(g - QUADS, 0)))
    vectors = (out_bias, ln2_gain, ln2_shift, fc_bias, proj_bias)
    prefix_shape = shape((PAD, 2 * D), BF)
    block_out, d_mid, d_att, d_sp, lse_t, delta_t, prefix_rows, prefix_kv = pl.pallas_call(
        forward_kernel,
        grid=(QUADS + blocks,),
        out_shape=(
            shape((slots, D), BF),
            shape((slots, D), F32),
            shape((slots, D), BF),
            shape((slots, lanes), BF),
            shape((lanes, slots), F32),
            shape((lanes, slots), F32),
            shape((lax.axis_size("batch"), *prefix_shape.shape), BF),
            prefix_shape,
        ),
        in_specs=[
            SMEM, SMEM, SMEM, quad_at(0), quad_at(QUADS), quad_at(2 * QUADS),
            block_of(D), block_of(D), block_of(D),
            *[whole(vector) for vector in vectors], ANY, ANY, ANY, *[whole(piece) for piece in prefix_pieces],
        ],
        out_specs=(
            block_of(D), block_of(D), block_of(D), block_of(lanes), block_t, block_t,
            ANY, whole(prefix_shape),
        ),
        scratch_shapes=[
            pltpu.VMEM((slots, D), BF),
            pltpu.VMEM((slots, lanes), BF),
            pltpu.VMEM((slots, lanes), F32),
            pltpu.VMEM((D, D), BF),
            pltpu.VMEM((D, FF), BF),
            pltpu.VMEM((FF, D), BF),
            pltpu.VMEM((BLK, D), F32),
            pltpu.VMEM((BLK, D), BF),
            pltpu.VMEM((BLK, D), BF),
            pltpu.VMEM((BLK, D), F32),
            pltpu.VMEM((BLK, D), F32),
            pltpu.VMEM((BLK, CHUNK), F32),
            pltpu.VMEM((BLK, CHUNK), F32),
            pltpu.VMEM((1, FF), F32),
            pltpu.VMEM((lanes, D), BF),
            pltpu.VMEM((D, lanes), BF),
            pltpu.VMEM((lanes, D), F32),
            pltpu.VMEM((lanes, D), F32),
            pltpu.VMEM(prefix_shape.shape, BF),
            pltpu.SemaphoreType.DMA((3,)),
            pltpu.SemaphoreType.DMA,
        ],
        compiler_params=params(56),
        cost_estimate=cost(50e9, 40 * 2**20),
        name="forward",
    )(
        rep_place, bucket, seg_lens, mixed, mixed, mixed, x, cot, mixed, *vectors,
        out_weight, fc_weight, proj_weight, *prefix_pieces,
    )

    late_weight, _ = lax.optimization_barrier((reparam_out, prefix_rows))
    weight_pieces = to_all(late_weight, "rep")
    batch_rows = lax.all_to_all(prefix_rows, "batch", split_axis=0, concat_axis=0, tiled=True)

    pairs = HEADS // 2
    early = EARLY_PAIRS

    def back_specs(start, count):
        def pair_of(g):
            return start + jnp.minimum(g, count - 1)

        def pair_at(offset):
            return pl.BlockSpec((slots, 128), lambda g: (0, offset + pair_of(g)))

        stat_spec = pl.BlockSpec((2 * PAD, slots), lambda g: (pair_of(g), 0))
        return [
            SMEM,
            pair_at(0), pair_at(pairs), pair_at(2 * pairs), pair_at(0),
            pl.BlockSpec((PAD, 128), lambda g: (0, pair_of(g))),
            pl.BlockSpec((slots, 128), lambda g: (0, pair_of(g) // 4)),
            stat_spec, stat_spec,
        ]

    back_args = (bucket, mixed, mixed, mixed, d_att, prefix_kv, d_sp, lse_t, delta_t)
    d_mixed = pl.pallas_call(
        early_back_kernel,
        grid=(early,),
        out_shape=shape((3, slots, early * 128), BF),
        in_specs=back_specs(0, early),
        out_specs=pl.BlockSpec((3, slots, 128), lambda g: (0, 0, g)),
        compiler_params=params(60),
        cost_estimate=cost(14e9, 10 * 2**20),
        name="early_back",
    )(*back_args)

    group_sum = jnp.sum(batch_rows.astype(F32), axis=0).astype(BF)
    rep_pieces = to_all(group_sum, "rep")

    late = pairs - early
    late_rows = pl.BlockSpec((BLK, D), lambda g: (jnp.maximum(g - late, 0), 0))
    tokens_grad = pl.pallas_call(
        backward_kernel,
        grid=(late + blocks,),
        out_shape=shape((slots, D), BF),
        in_specs=[
            *back_specs(early, late),
            pl.BlockSpec((3, BLK, early * 128), lambda g: (0, jnp.maximum(g - late, 0), 0)),
            late_rows, late_rows, whole(ln1_gain), ANY,
        ],
        out_specs=late_rows,
        scratch_shapes=[
            pltpu.VMEM((3, slots, late * 128), BF),
            pltpu.VMEM((D, 3 * D), BF),
            pltpu.SemaphoreType.DMA,
        ],
        compiler_params=params(60),
        cost_estimate=cost(24e9, 30 * 2**20),
        name="backward",
    )(*back_args, d_mixed, x, d_mid, ln1_gain, qkv_weight)

    tail_args = (tanh_pre, prefix_embed, reparam_in, *weight_pieces, *rep_pieces)
    tail_outs = (
        shape((PREFIX, D), F32),
        shape((D, hidden_width), F32),
        shape((1, hidden_width), F32),
        shape((hidden_width, own_width), F32),
        shape((1, own_width), F32),
    )
    embed_grad, in_grad, in_bias_grad, out_grad, out_bias_grad = pl.pallas_call(
        tail_kernel,
        grid=(1,),
        out_shape=tail_outs,
        in_specs=[SMEM] + [whole(arg) for arg in tail_args],
        out_specs=tuple(whole(out) for out in tail_outs),
        scratch_shapes=[
            pltpu.VMEM((PAD, D), F32),
            pltpu.VMEM((len(rep_pieces), *prefix_shape.shape), BF),
            pltpu.VMEM(prefix_shape.shape, BF),
            pltpu.VMEM((len(rep_pieces), PAD, hidden_width), F32),
        ],
        compiler_params=params(16),
        name="tail",
    )(rep_place, *tail_args)
    return (
        block_out[None],
        tokens_grad[None],
        embed_grad,
        in_grad,
        in_bias_grad[0],
        out_grad,
        out_bias_grad[0],
    )


def solution(mesh):
    row = P(("batch", "rep"), None, None)
    placed = (row, *[P()] * 15, P(None, "rep"), P("rep"), P(("batch", "rep")), P(("batch", "rep"), None), row)
    return jax.shard_map(
        local,
        mesh=mesh,
        in_specs=placed,
        out_specs=(row, row, P(), P(), P(), P(None, "rep"), P("rep")),
        check_vma=False,
    )
```

```python
import jax
import jax.numpy as jnp
from jax import lax
from jax.experimental import pallas as pl
from jax.experimental.pallas import tpu as pltpu
from jax.sharding import PartitionSpec as P

D = 1024
HEADS = 16
HEAD_DIM = 64
FF = 4096
PREFIX = 10
PAD = 16
SHORT = 256
PAD_BITS, HEAD_DIM_BITS, SHORT_BITS = 4, 6, 8
BLK = 256
QUAD = 4 * HEAD_DIM
QUADS = HEADS // 4
EARLY_PAIRS = 4
CHUNK = 1024

BF = jnp.bfloat16
F32 = jnp.float32
norm_eps = 1e-05
gelu_coef = 0.7978845608028654
gelu_cube = 0.044715
masked_score = -1e30


def dot_nn(left, right):
    return jnp.dot(left, right, preferred_element_type=F32)


def dot_nt(left, right):
    return lax.dot_general(left, right, (((1,), (1,)), ((), ())), preferred_element_type=F32)


def dot_tn(left, right):
    return lax.dot_general(left, right, (((0,), (0,)), ((), ())), preferred_element_type=F32)


def normalise(values):
    row_mean = jnp.mean(values, axis=-1, keepdims=True)
    centred = values - row_mean
    variance = jnp.mean(centred * centred, axis=-1, keepdims=True)
    inv = lax.rsqrt(variance + norm_eps)
    return centred * inv, inv


def norm_back(grad, norm, inv):
    along = jnp.mean(grad * norm, axis=-1, keepdims=True)
    return (grad - jnp.mean(grad, axis=-1, keepdims=True) - norm * along) * inv


def gelu_pair(u):
    sq = u * u
    w = jnp.tanh(u * (gelu_coef + (gelu_coef * gelu_cube) * sq))
    a = 0.5 * w + 0.5
    slope = a * (1.0 + u * (1.0 - a) * (2.0 * gelu_coef + (6.0 * gelu_coef * gelu_cube) * sq))
    return u * a, slope


def head_mask(shape, head):
    lane = lax.broadcasted_iota(jnp.int32, shape, 1)
    return (lane < HEAD_DIM) if head % 2 == 0 else (lane >= HEAD_DIM)


def quad_prefix(prefix, quad):
    row = lax.broadcasted_iota(jnp.int32, (128, QUAD), 0) >> PAD_BITS
    col = lax.broadcasted_iota(jnp.int32, (128, QUAD), 1) >> HEAD_DIM_BITS
    tiled = jnp.concatenate([prefix] * 8, axis=0)
    return jnp.where(row == col + 4 * (quad % 2), tiled, jnp.zeros_like(tiled))


def full_prefix(prefix):
    shape = (HEADS * PAD, D)
    row = lax.broadcasted_iota(jnp.int32, shape, 0) >> PAD_BITS
    col = lax.broadcasted_iota(jnp.int32, shape, 1) >> HEAD_DIM_BITS
    tiled = jnp.concatenate([prefix] * HEADS, axis=0)
    return jnp.where(row == col, tiled, jnp.zeros_like(tiled))


def row_of(ref, first=0, size=None):
    size = ref.shape[0] if size is None else size
    return ref[first : first + size].astype(F32)[None, :]


def padded_embed(embed_ref, pad_ref):
    pad_ref[...] = jnp.zeros_like(pad_ref)
    pad_ref[0:PREFIX, :] = embed_ref[...].astype(F32)
    return pad_ref[...].astype(BF)


def reparam_kernel(embed_ref, in_w_ref, in_b_ref, out_w_ref, out_b_ref, tanh_ref, kv_ref, pad_ref):
    tanh_pre = jnp.tanh(dot_nn(padded_embed(embed_ref, pad_ref), in_w_ref[...]) + row_of(in_b_ref))
    tanh_ref[...] = tanh_pre
    kv_ref[...] = (dot_nn(tanh_pre.astype(BF), out_w_ref[...]) + row_of(out_b_ref)).astype(BF)


def project_kernel(x_ref, gain_ref, shift_ref, bias_ref, w_ref, out_ref, normed_ref):
    step = pl.program_id(0)
    slots = x_ref.shape[0]
    factor = jnp.where(step == 0, HEAD_DIM**-0.5, 1.0)

    def norm_part(first):
        norm, _ = normalise(x_ref[first : first + BLK, :].astype(F32))
        normed_ref[first : first + BLK, :] = (norm * row_of(gain_ref) + row_of(shift_ref)).astype(BF)

    def dot_part(first, count):
        rows = pl.ds(first, count)
        mixed = dot_nn(normed_ref[rows, :], w_ref[...]) + row_of(bias_ref)
        out_ref[rows, :] = (mixed.astype(BF).astype(F32) * factor).astype(BF)

    @pl.when(step == 0)
    def _():
        norm_part(0)
        for first in range(0, slots, BLK):
            if first + BLK < slots:
                norm_part(first + BLK)
            dot_part(first, BLK)

    @pl.when(step > 0)
    def _():
        def body(index, carry):
            dot_part(pl.multiple_of(index * 2 * BLK, 2 * BLK), 2 * BLK)
            return carry

        lax.fori_loop(0, slots // (2 * BLK), body, 0)


def live_column(bucket_ref, lens_ref, first, rows, slots):
    position = lax.broadcasted_iota(jnp.int32, (rows, 1), 0) + first
    segment = position >> SHORT_BITS
    total = jnp.int32(0)
    short_len = jnp.zeros((rows, 1), jnp.int32)
    for index in range(slots // SHORT):
        total = total + lens_ref[0, index]
        short_len = jnp.where(segment == index, lens_ref[0, index], short_len)
    return position < jnp.where(bucket_ref[0] == slots, total, segment * SHORT + short_len)


def block_rows(block):
    return pl.ds(block * BLK if isinstance(block, int) else pl.multiple_of(block * BLK, BLK), BLK)


def key_rows(block, long_row):
    return pl.ds(0, (block + 1) * BLK) if long_row else block_rows(block)


def attend(q_ref, k_ref, v_ref, prefix_ref, att_ref, pp_ref, lse_ref, quad, query_blocks, long_row):
    cols = pl.ds(pl.multiple_of(quad * QUAD, QUAD), QUAD)
    pair_cols = pl.ds(pl.multiple_of((quad // 2) * 128, 128), 128)
    prefix_keys = quad_prefix(prefix_ref[:, cols], quad)
    prefix_vals = quad_prefix(prefix_ref[:, pl.ds(pl.multiple_of(D + quad * QUAD, QUAD), QUAD)], quad)
    causal = lax.broadcasted_iota(jnp.int32, (BLK, BLK), 1) <= lax.broadcasted_iota(jnp.int32, (BLK, BLK), 0)
    lane = lax.broadcasted_iota(jnp.int32, (BLK, 128), 1)
    lane_head = (lane >> PAD_BITS) - 4 * (quad % 2)
    lane_real = (lane & (PAD - 1)) < PREFIX

    def scores(block, head):
        pair = slice(128 * (head // 2), 128 * (head // 2) + 128)
        queries = q_ref[block_rows(block), pair]
        queries = jnp.where(head_mask((BLK, 128), head), queries, jnp.zeros_like(queries))
        raw = dot_nt(queries, k_ref[key_rows(block, long_row), pair])
        own = jnp.where(causal, raw[:, -BLK:], masked_score)
        return own if raw.shape[1] == BLK else jnp.concatenate([raw[:, :-BLK], own], axis=1)

    units = [(block, head) for block in query_blocks for head in range(4)]
    ahead = 1
    queue = [scores(*unit) for unit in units[:ahead]]
    for index, (block, head) in enumerate(units):
        if index + ahead < len(units):
            queue.append(scores(*units[index + ahead]))
        rows = block_rows(block)
        if head == 0:
            prefix_raw = dot_nt(q_ref[rows, :], prefix_keys)
            probs_quad = jnp.zeros((BLK, 128), F32)
            lse_quad = jnp.zeros((BLK, 128), F32)
            outs = []
        pair = slice(128 * (head // 2), 128 * (head // 2) + 128)
        count = queue[index].shape[1]
        prefix_scores = jnp.where((lane_head == head) & lane_real, prefix_raw, masked_score)
        score = jnp.concatenate([queue[index], prefix_scores], axis=1)
        queue[index] = None
        peak = jnp.max(score, axis=1, keepdims=True)
        raised = jnp.exp(score - peak)
        summed = jnp.sum(raised, axis=1, keepdims=True)
        inv = 1.0 / summed
        outs.append(dot_nn(raised[:, :count].astype(BF), v_ref[key_rows(block, long_row), pair]) * inv)
        probs_quad = probs_quad + raised[:, count:] * inv
        lse_quad = jnp.where(lane_head == head, peak + jnp.log(summed), lse_quad)
        if head == 3:
            probs_low = probs_quad.astype(BF)
            left = head_mask((BLK, 128), 0)
            merged = jnp.concatenate(
                [jnp.where(left, outs[0], outs[1]), jnp.where(left, outs[2], outs[3])], axis=1
            ) + dot_nn(probs_low, prefix_vals)
            att_ref[rows, cols] = merged.astype(BF)

            @pl.when(quad % 2 == 0)
            def _():
                pp_ref[rows, pair_cols] = probs_low
                lse_ref[rows, pair_cols] = lse_quad

            @pl.when(quad % 2 == 1)
            def _():
                pp_ref[rows, pair_cols] = pp_ref[rows, pair_cols] + probs_low
                lse_ref[rows, pair_cols] = lse_ref[rows, pair_cols] + lse_quad


def forward_kernel(
    place_ref, bucket_ref, lens_ref, q_ref, k_ref, v_ref, x_ref, cot_ref, q_rows_ref,
    out_b_ref, gain_ref, shift_ref, fc_b_ref, proj_b_ref, out_w_hbm, fc_w_hbm, proj_w_hbm, *refs,
):
    pieces, refs = refs[: len(refs) - 29], refs[len(refs) - 29 :]
    (
        block_ref, d_mid_ref, d_att_ref, d_sp_ref, lse_t_ref, delta_t_ref, prefix_rows_hbm, prefix_ref,
        att_ref, pp_ref, lse_ref, out_w_ref, fc_w_ref, proj_w_ref, norm_ref, normed_ref, grad_out_ref,
        acc_ref, d_acc_ref, pre_ref, d_act_ref, bias_ref, vp_ref, spread_ref, d_kp_ref, d_vp_ref, row_ref, sems, row_sem,
    ) = refs
    step = pl.program_id(0)
    slots = q_ref.shape[0]
    copies = [
        pltpu.make_async_copy(out_w_hbm, out_w_ref, sems.at[0]),
        pltpu.make_async_copy(fc_w_hbm, fc_w_ref, sems.at[1]),
        pltpu.make_async_copy(proj_w_hbm, proj_w_ref, sems.at[2]),
    ]
    long_row = bucket_ref[0] == slots

    @pl.when(step == 0)
    def _():
        for copy in copies:
            copy.start()
        width = pieces[0].shape[1]
        for shift, piece in enumerate(pieces):
            owner = (place_ref[0] + (len(pieces) - shift)) % len(pieces)
            prefix_ref[:, pl.ds(pl.multiple_of(owner * width, 128), width)] = piece[...]
        vp_ref[...] = full_prefix(prefix_ref[:, D:])
        row = lax.broadcasted_iota(jnp.int32, (D, HEADS * PAD), 0) >> HEAD_DIM_BITS
        col = lax.broadcasted_iota(jnp.int32, (D, HEADS * PAD), 1) >> PAD_BITS
        spread_ref[...] = jnp.where(row == col, 1.0, 0.0).astype(BF)
        bias_ref[...] = row_of(fc_b_ref)
        d_kp_ref[...] = jnp.zeros_like(d_kp_ref)
        d_vp_ref[...] = jnp.zeros_like(d_vp_ref)

    attend_args = (q_ref, k_ref, v_ref, prefix_ref, att_ref, pp_ref, lse_ref, step)

    @pl.when((step < QUADS) & long_row)
    def _():
        attend(*attend_args, list(range(slots // BLK)), True)

    @pl.when((step < QUADS) & jnp.logical_not(long_row))
    def _():
        def body(block, carry):
            attend(*attend_args, [block], False)
            return carry

        lax.fori_loop(0, slots // BLK, body, 0)

    @pl.when(step == QUADS)
    def _():
        for copy in copies:
            copy.wait()

    @pl.when(step >= QUADS)
    def _():
        first = pl.multiple_of((step - QUADS) * BLK, BLK)
        rows = pl.ds(first, BLK)
        live = live_column(bucket_ref, lens_ref, first, BLK, slots)
        attended = att_ref[rows, :]
        mid = x_ref[...].astype(F32) + dot_nn(attended, out_w_ref[...]) + row_of(out_b_ref)
        norm, inv = normalise(mid)
        norm_ref[...] = norm
        normed_ref[...] = (norm * row_of(gain_ref) + row_of(shift_ref)).astype(BF)
        grad_out_ref[...] = jnp.where(live, cot_ref[...].astype(F32), 0.0).astype(BF)
        acc_ref[...] = mid + row_of(proj_b_ref)
        d_acc_ref[...] = jnp.zeros_like(d_acc_ref)

        def opened(chunk):
            part = pl.ds(pl.multiple_of(chunk * CHUNK, CHUNK), CHUNK)
            pre = dot_nn(normed_ref[...], fc_w_ref[:, part]) + bias_ref[:, part]
            return pre, dot_nt(grad_out_ref[...], proj_w_ref[part, :])

        def closed(chunk, pre, d_act):
            part = pl.ds(pl.multiple_of(chunk * CHUNK, CHUNK), CHUNK)
            act, slope = gelu_pair(pre)
            forth = dot_nn(act.astype(BF), proj_w_ref[part, :])
            back = dot_nt((d_act * slope).astype(BF), fc_w_ref[:, part])
            return acc_ref[...] + forth, d_acc_ref[...] + back

        def chunk_step(chunk, carry):
            pre, d_act = pre_ref[...], d_act_ref[...]
            next_pre, next_d_act = opened(chunk + 1)
            acc_ref[...], d_acc_ref[...] = closed(chunk, pre, d_act)
            pre_ref[...], d_act_ref[...] = next_pre, next_d_act
            return carry

        chunks = FF // CHUNK
        pre_ref[...], d_act_ref[...] = opened(0)
        lax.fori_loop(0, chunks - 1, chunk_step, 0, unroll=True)
        result, d_normed = closed(chunks - 1, pre_ref[...], d_act_ref[...])
        block_ref[...] = jnp.where(live, result, 0.0).astype(BF)
        d_mid = grad_out_ref[...].astype(F32) + norm_back(d_normed * row_of(gain_ref), norm_ref[...], inv)
        d_mid_ref[...] = d_mid
        d_att = dot_nt(d_mid.astype(BF), out_w_ref[...]).astype(BF)
        d_att_ref[...] = d_att
        product = (d_att.astype(F32) * attended.astype(F32)).astype(BF)
        delta = dot_nn(product, spread_ref[...])
        probs = pp_ref[rows, :]
        d_sp = (probs.astype(F32) * (dot_nt(d_att, vp_ref[...]) - delta)).astype(BF)
        d_sp_ref[...] = d_sp
        d_kp_ref[...] += dot_tn(d_sp, q_rows_ref[...])
        d_vp_ref[...] += dot_tn(probs, d_att)
        lse_t_ref[...] = lse_ref[rows, :].T
        delta_t_ref[...] = delta.T

    @pl.when(step == pl.num_programs(0) - 1)
    def _():
        shape = (HEADS * PAD, D)
        own = (
            lax.broadcasted_iota(jnp.int32, shape, 0) >> PAD_BITS
            == lax.broadcasted_iota(jnp.int32, shape, 1) >> HEAD_DIM_BITS
        )
        for index, ref in enumerate((d_kp_ref, d_vp_ref)):
            kept = jnp.where(own, ref[...], 0.0)
            total = kept[0:PAD, :]
            for head in range(1, HEADS):
                total = total + kept[head * PAD : (head + 1) * PAD, :]
            row_ref[:, index * D : (index + 1) * D] = total.astype(BF)
        sends = [
            pltpu.make_async_copy(row_ref, prefix_rows_hbm.at[place], row_sem)
            for place in range(prefix_rows_hbm.shape[0])
        ]
        for send in sends:
            send.start()
        for send in sends:
            send.wait()


def attend_back(
    q_ref, k_ref, v_ref, do_ref, pk_ref, dsp_ref, lse_ref, delta_ref, mix_ref, cols, pair, query_blocks, long_row
):
    causal = lax.broadcasted_iota(jnp.int32, (BLK, BLK), 0) <= lax.broadcasted_iota(jnp.int32, (BLK, BLK), 1)
    left = head_mask((BLK, 128), 0)
    row = lax.broadcasted_iota(jnp.int32, (128, 128), 0) >> PAD_BITS
    col = lax.broadcasted_iota(jnp.int32, (128, 128), 1) >> HEAD_DIM_BITS
    tiled = jnp.concatenate([pk_ref[...]] * 8, axis=0)
    prefix_keys = jnp.where(row == col + 2 * (pair % 4), tiled, jnp.zeros_like(tiled))

    def opened(block, side):
        rows, keys = block_rows(block), key_rows(block, long_row)
        mask = head_mask((BLK, 128), side)
        queries, d_out = q_ref[rows, :], do_ref[rows, :]
        raw = dot_nt(k_ref[keys, :], jnp.where(mask, queries, jnp.zeros_like(queries)))
        d_prob = dot_nt(v_ref[keys, :], jnp.where(mask, d_out, jnp.zeros_like(d_out)))
        own = jnp.where(causal, raw[-BLK:], masked_score)
        return (own if raw.shape[0] == BLK else jnp.concatenate([raw[:-BLK], own], axis=0)), d_prob

    units = [(block, side) for block in query_blocks for side in range(2)]
    ahead = 3
    queue = [opened(*unit) for unit in units[:ahead]]
    d_keys = [[None] * len(query_blocks) for _ in range(2)]
    d_vals = [[None] * len(query_blocks) for _ in range(2)]
    d_queries = [None, None]
    for index, (block, side) in enumerate(units):
        if index + ahead < len(units):
            queue.append(opened(*units[index + ahead]))
        score, d_prob = queue[index]
        queue[index] = None
        rows, keys = block_rows(block), key_rows(block, long_row)
        stat = slice(side * PAD, side * PAD + 1)
        prob = jnp.exp(score - lse_ref[stat, rows])
        d_score = (prob * (d_prob - delta_ref[stat, rows])).astype(BF)
        d_queries[side] = dot_tn(d_score, k_ref[keys, :])
        d_key = dot_nn(d_score, q_ref[rows, :])
        d_val = dot_nn(prob.astype(BF), do_ref[rows, :])
        for place in range(d_key.shape[0] // BLK):
            part = slice(place * BLK, (place + 1) * BLK)
            for sums, value in ((d_keys, d_key), (d_vals, d_val)):
                so_far = sums[side][place]
                sums[side][place] = value[part] if so_far is None else so_far + value[part]
        if side == 1:
            d_query = jnp.where(left, d_queries[0], d_queries[1]) + dot_nn(dsp_ref[rows, :], prefix_keys)
            mix_ref[0, rows, cols] = (d_query * HEAD_DIM**-0.5).astype(BF)
    for place, block in enumerate(query_blocks):
        rows = block_rows(block)
        mix_ref[1, rows, cols] = jnp.where(left, d_keys[0][place], d_keys[1][place]).astype(BF)
        mix_ref[2, rows, cols] = jnp.where(left, d_vals[0][place], d_vals[1][place]).astype(BF)


def attend_back_pair(bucket_ref, refs, mix_ref, cols, pair, here):
    blocks = refs[0].shape[0] // BLK
    long_row = bucket_ref[0] == refs[0].shape[0]
    args = (*refs, mix_ref, cols, pair)

    @pl.when(here & long_row)
    def _():
        attend_back(*args, list(range(blocks)), True)

    @pl.when(here & jnp.logical_not(long_row))
    def _():
        def body(block, carry):
            attend_back(*args, [block], False)
            return carry

        lax.fori_loop(0, blocks, body, 0)


def early_back_kernel(bucket_ref, *refs):
    *refs, mix_ref = refs
    step = pl.program_id(0)
    attend_back_pair(bucket_ref, refs, mix_ref, slice(0, 128), step, step >= 0)


def backward_kernel(bucket_ref, *refs):
    refs, (early_ref, x_ref, d_mid_ref, gain_ref, w_hbm, grad_ref, mix_ref, w_ref, sem) = refs[:8], refs[8:]
    step = pl.program_id(0)
    pairs = mix_ref.shape[2] // 128
    copy = pltpu.make_async_copy(w_hbm, w_ref, sem)

    @pl.when(step == 0)
    def _():
        copy.start()

    cols = pl.ds(pl.multiple_of(jnp.minimum(step, pairs - 1) * 128, 128), 128)
    attend_back_pair(bucket_ref, refs, mix_ref, cols, step + (HEADS // 2 - pairs), step < pairs)

    @pl.when(step == pairs)
    def _():
        copy.wait()

    @pl.when(step >= pairs)
    def _():
        rows = block_rows(step - pairs)
        d_mixed = jnp.concatenate(
            [part for third in range(3) for part in (early_ref[third], mix_ref[third, rows, :])], axis=1
        )
        d_normed = dot_nt(d_mixed, w_ref[...])
        norm, inv = normalise(x_ref[...].astype(F32))
        back = norm_back(d_normed * row_of(gain_ref), norm, inv)
        grad_ref[...] = (d_mid_ref[...] + back).astype(BF)


def summed_in_order(place, pieces, ordered_ref):
    for shift, piece in enumerate(pieces):
        ordered_ref[(place + (len(pieces) - shift)) % len(pieces)] = piece[...]
    total = ordered_ref[0].astype(F32)
    for owner in range(1, len(pieces)):
        total = total + ordered_ref[owner].astype(F32)
    return total


def tail_kernel(place_ref, tanh_ref, embed_ref, in_w_ref, *refs):
    count = (len(refs) - 9) // 2
    weights, pieces = refs[:count], refs[count : 2 * count]
    (
        embed_grad_ref, in_grad_ref, in_bias_ref, out_grad_ref, out_bias_ref,
        pad_ref, ordered_ref, sum_ref, parts_ref,
    ) = refs[2 * count :]
    tanh_pre = tanh_ref[...]
    sum_ref[...] = summed_in_order(place_ref[0], pieces, ordered_ref).astype(BF)
    width = out_grad_ref.shape[1]
    for shift, weight in enumerate(weights):
        owner = (place_ref[0] + (count - shift)) % count
        own_cols = sum_ref[:, pl.ds(pl.multiple_of(owner * width, 128), width)]
        parts_ref[owner] = dot_nt(own_cols, weight[...])
        if shift == 0:
            out_grad_ref[...] = dot_tn(tanh_pre.astype(BF), own_cols)
            out_bias_ref[...] = jnp.sum(own_cols.astype(F32), axis=0, keepdims=True)
    d_hidden = parts_ref[0]
    for owner in range(1, count):
        d_hidden = d_hidden + parts_ref[owner]
    d_pre = (d_hidden * (1.0 - tanh_pre * tanh_pre)).astype(BF)
    in_grad_ref[...] = dot_tn(padded_embed(embed_ref, pad_ref), d_pre)
    in_bias_ref[...] = jnp.sum(d_pre.astype(F32), axis=0, keepdims=True)
    embed_grad_ref[...] = dot_nt(d_pre, in_w_ref[...])[0:PREFIX]


SMEM = pl.BlockSpec(memory_space=pltpu.SMEM)
ANY = pl.BlockSpec(memory_space=pl.ANY)


def params(mib):
    return pltpu.CompilerParams(vmem_limit_bytes=mib * 2**20, dimension_semantics=("arbitrary",))


def cost(flops, moved):
    return pl.CostEstimate(flops=int(flops), bytes_accessed=int(moved), transcendentals=0)


def shape(dims, dtype):
    return jax.ShapeDtypeStruct(dims, dtype)


def whole(array):
    return pl.BlockSpec(array.shape, lambda g: (0,) * len(array.shape))


def to_all(value, axis):
    size = lax.axis_size(axis)
    return [value] + [
        lax.ppermute(value, axis, [(place, (place + shift) % size) for place in range(size)])
        for shift in range(1, size)
    ]


def local(
    tokens, ln1_gain, ln1_shift, qkv_weight, qkv_bias, out_weight, out_bias, ln2_gain, ln2_shift, fc_weight,
    fc_bias, proj_weight, proj_bias, prefix_embed, reparam_in, reparam_in_bias, reparam_out, reparam_out_bias,
    bucket, seg_lens, cotangent,
):
    x, cot = tokens[0], cotangent[0]
    slots = x.shape[0]
    blocks = slots // BLK
    own_width = reparam_out.shape[1]
    hidden_width = reparam_in.shape[1]
    rep_place = lax.axis_index("rep").astype(jnp.int32)[None]

    reparam_args = (prefix_embed, reparam_in, reparam_in_bias, reparam_out, reparam_out_bias)
    reparam_outs = (shape((PAD, hidden_width), F32), shape((PAD, own_width), BF))
    tanh_pre, own_kv = pl.pallas_call(
        reparam_kernel,
        grid=(1,),
        out_shape=reparam_outs,
        in_specs=[whole(arg) for arg in reparam_args],
        out_specs=tuple(whole(out) for out in reparam_outs),
        scratch_shapes=[pltpu.VMEM((PAD, D), F32)],
        compiler_params=params(60),
        name="reparam",
    )(*reparam_args)
    prefix_pieces = to_all(own_kv, "rep")

    mixed = pl.pallas_call(
        project_kernel,
        grid=(3,),
        out_shape=shape((slots, 3 * D), BF),
        in_specs=[
            whole(x), whole(ln1_gain), whole(ln1_shift),
            pl.BlockSpec((D,), lambda n: (n,)),
            pl.BlockSpec((D, D), lambda n: (0, n)),
        ],
        out_specs=pl.BlockSpec((slots, D), lambda n: (0, n)),
        scratch_shapes=[pltpu.VMEM((slots, D), BF)],
        compiler_params=params(60),
        cost_estimate=cost(6 * slots * D * D, 16 * 2**20),
        name="project",
    )(x, ln1_gain, ln1_shift, qkv_bias, qkv_weight)
    def quad_at(offset):
        return pl.BlockSpec((slots, QUAD), lambda g: (0, offset + jnp.minimum(g, QUADS - 1)))

    def block_of(width):
        return pl.BlockSpec((BLK, width), lambda g: (jnp.maximum(g - QUADS, 0), 0))

    lanes = HEADS * PAD
    block_t = pl.BlockSpec((lanes, BLK), lambda g: (0, jnp.maximum(g - QUADS, 0)))
    vectors = (out_bias, ln2_gain, ln2_shift, fc_bias, proj_bias)
    prefix_shape = shape((PAD, 2 * D), BF)
    block_out, d_mid, d_att, d_sp, lse_t, delta_t, prefix_rows, prefix_kv = pl.pallas_call(
        forward_kernel,
        grid=(QUADS + blocks,),
        out_shape=(
            shape((slots, D), BF),
            shape((slots, D), F32),
            shape((slots, D), BF),
            shape((slots, lanes), BF),
            shape((lanes, slots), F32),
            shape((lanes, slots), F32),
            shape((lax.axis_size("batch"), *prefix_shape.shape), BF),
            prefix_shape,
        ),
        in_specs=[
            SMEM, SMEM, SMEM, quad_at(0), quad_at(QUADS), quad_at(2 * QUADS),
            block_of(D), block_of(D), block_of(D),
            *[whole(vector) for vector in vectors], ANY, ANY, ANY, *[whole(piece) for piece in prefix_pieces],
        ],
        out_specs=(
            block_of(D), block_of(D), block_of(D), block_of(lanes), block_t, block_t,
            ANY, whole(prefix_shape),
        ),
        scratch_shapes=[
            pltpu.VMEM((slots, D), BF),
            pltpu.VMEM((slots, lanes), BF),
            pltpu.VMEM((slots, lanes), F32),
            pltpu.VMEM((D, D), BF),
            pltpu.VMEM((D, FF), BF),
            pltpu.VMEM((FF, D), BF),
            pltpu.VMEM((BLK, D), F32),
            pltpu.VMEM((BLK, D), BF),
            pltpu.VMEM((BLK, D), BF),
            pltpu.VMEM((BLK, D), F32),
            pltpu.VMEM((BLK, D), F32),
            pltpu.VMEM((BLK, CHUNK), F32),
            pltpu.VMEM((BLK, CHUNK), F32),
            pltpu.VMEM((1, FF), F32),
            pltpu.VMEM((lanes, D), BF),
            pltpu.VMEM((D, lanes), BF),
            pltpu.VMEM((lanes, D), F32),
            pltpu.VMEM((lanes, D), F32),
            pltpu.VMEM(prefix_shape.shape, BF),
            pltpu.SemaphoreType.DMA((3,)),
            pltpu.SemaphoreType.DMA,
        ],
        compiler_params=params(56),
        cost_estimate=cost(50e9, 40 * 2**20),
        name="forward",
    )(
        rep_place, bucket, seg_lens, mixed, mixed, mixed, x, cot, mixed, *vectors,
        out_weight, fc_weight, proj_weight, *prefix_pieces,
    )

    late_weight, _ = lax.optimization_barrier((reparam_out, prefix_rows))
    weight_pieces = to_all(late_weight, "rep")
    batch_rows = lax.all_to_all(prefix_rows, "batch", split_axis=0, concat_axis=0, tiled=True)

    pairs = HEADS // 2
    early = EARLY_PAIRS

    def back_specs(start, count):
        def pair_of(g):
            return start + jnp.minimum(g, count - 1)

        def pair_at(offset):
            return pl.BlockSpec((slots, 128), lambda g: (0, offset + pair_of(g)))

        stat_spec = pl.BlockSpec((2 * PAD, slots), lambda g: (pair_of(g), 0))
        return [
            SMEM,
            pair_at(0), pair_at(pairs), pair_at(2 * pairs), pair_at(0),
            pl.BlockSpec((PAD, 128), lambda g: (0, pair_of(g))),
            pl.BlockSpec((slots, 128), lambda g: (0, pair_of(g) // 4)),
            stat_spec, stat_spec,
        ]

    back_args = (bucket, mixed, mixed, mixed, d_att, prefix_kv, d_sp, lse_t, delta_t)
    d_mixed = pl.pallas_call(
        early_back_kernel,
        grid=(early,),
        out_shape=shape((3, slots, early * 128), BF),
        in_specs=back_specs(0, early),
        out_specs=pl.BlockSpec((3, slots, 128), lambda g: (0, 0, g)),
        compiler_params=params(60),
        cost_estimate=cost(14e9, 10 * 2**20),
        name="early_back",
    )(*back_args)

    group_sum = jnp.sum(batch_rows.astype(F32), axis=0).astype(BF)
    rep_pieces = to_all(group_sum, "rep")

    late = pairs - early
    late_rows = pl.BlockSpec((BLK, D), lambda g: (jnp.maximum(g - late, 0), 0))
    tokens_grad = pl.pallas_call(
        backward_kernel,
        grid=(late + blocks,),
        out_shape=shape((slots, D), BF),
        in_specs=[
            *back_specs(early, late),
            pl.BlockSpec((3, BLK, early * 128), lambda g: (0, jnp.maximum(g - late, 0), 0)),
            late_rows, late_rows, whole(ln1_gain), ANY,
        ],
        out_specs=late_rows,
        scratch_shapes=[
            pltpu.VMEM((3, slots, late * 128), BF),
            pltpu.VMEM((D, 3 * D), BF),
            pltpu.SemaphoreType.DMA,
        ],
        compiler_params=params(60),
        cost_estimate=cost(24e9, 30 * 2**20),
        name="backward",
    )(*back_args, d_mixed, x, d_mid, ln1_gain, qkv_weight)

    tail_args = (tanh_pre, prefix_embed, reparam_in, *weight_pieces, *rep_pieces)
    tail_outs = (
        shape((PREFIX, D), F32),
        shape((D, hidden_width), F32),
        shape((1, hidden_width), F32),
        shape((hidden_width, own_width), F32),
        shape((1, own_width), F32),
    )
    embed_grad, in_grad, in_bias_grad, out_grad, out_bias_grad = pl.pallas_call(
        tail_kernel,
        grid=(1,),
        out_shape=tail_outs,
        in_specs=[SMEM] + [whole(arg) for arg in tail_args],
        out_specs=tuple(whole(out) for out in tail_outs),
        scratch_shapes=[
            pltpu.VMEM((PAD, D), F32),
            pltpu.VMEM((len(rep_pieces), *prefix_shape.shape), BF),
            pltpu.VMEM(prefix_shape.shape, BF),
            pltpu.VMEM((len(rep_pieces), PAD, hidden_width), F32),
        ],
        compiler_params=params(16),
        name="tail",
    )(rep_place, *tail_args)
    return (
        block_out[None],
        tokens_grad[None],
        embed_grad,
        in_grad,
        in_bias_grad[0],
        out_grad,
        out_bias_grad[0],
    )


def solution(mesh):
    row = P(("batch", "rep"), None, None)
    placed = (row, *[P()] * 15, P(None, "rep"), P("rep"), P(("batch", "rep")), P(("batch", "rep"), None), row)
    return jax.shard_map(
        local,
        mesh=mesh,
        in_specs=placed,
        out_specs=(row, row, P(), P(), P(), P(None, "rep"), P("rep")),
        check_vma=False,
    )
```
